32 devices in a mesh: dp: 8 (over z, y), head: 4 (over x, core).
Axes of the slice: x: 2, y: 2, z: 4, core: 2. Of those that a mesh axis runs over, the one named last changes fastest.
Arguments:
- block_input: bfloat16 [16384, 768], P(('dp', 'head')), may hold values from -6 to 6
- gain_one: float32 [768], replicated, may hold values from 0.5 to 1.5
- gain_two: float32 [768], replicated, may hold values from 0.5 to 1.5
- qkv_weight: float32 [3, 768, 768], P(None, 'dp', 'head'), may hold values from -0.3125 to 0.3125
- out_weight: float32 [768, 768], P('head', 'dp'), may hold values from -0.875 to 0.875
- gate_weight: float32 [768, 8], replicated, may hold values from -0.15625 to 0.15625
- frozen_in: float32 [8, 768, 1536], P('dp', None, 'head'), may hold values from -0.21875 to 0.21875
- frozen_out: float32 [8, 1536, 768], P('dp', 'head'), may hold values from -0.109375 to 0.109375
- fresh_in: float32 [8, 768, 1536], P('dp', None, 'head'), may hold values from -0.21875 to 0.21875
- fresh_out: float32 [8, 1536, 768], P('dp', 'head'), may hold values from -0.109375 to 0.109375
- routes: int32 [16384, 2], P('dp'), may hold values from 0 to 7, all different within a row; in each aligned block of 2048 rows (0 to 2047, 2048 to 4095, ...) at most 768 rows name the same one
- doc_lengths: int32 [8, 4], P('dp'), may hold values from 1 to 2045, as said below
- cotangent: bfloat16 [16384, 768], P(('dp', 'head')), may hold values from -6 to 6
Outputs:
- block_output: bfloat16 [16384, 768], P(('dp', 'head'))
- grad_input: float32 [16384, 768], P(('dp', 'head'))
- grad_gain_one: float32 [768], replicated
- grad_gain_two: float32 [768], replicated
- grad_qkv: float32 [3, 768, 768], P(None, 'dp', 'head')
- grad_out_weight: float32 [768, 768], P('head', 'dp')
- grad_gate: float32 [768, 8], replicated
- grad_fresh_in: float32 [8, 768, 1536], P('dp', None, 'head')
- grad_fresh_out: float32 [8, 1536, 768], P('dp', 'head')
The draws below stay inside these ranges and needn't reach their ends.
Inputs may be any that keep to these rules, and one draw needn't show every extreme that they name: `routes`: in each aligned block of 2048 rows (the tokens of one group) every row names two different experts, no expert is named by more than 768 rows, a bound that some block reaches. `doc_lengths`: each row holds the lengths, in order, of the 4 documents of one group and sums to 2048; the second document begins within the group's first 512 tokens and ends within its last 512.
All inputs are finite; a program needn't handle non-finite values.
Results may differ from the reference program's by a relative error of at most 0.013.
The reference program's roundings to bfloat16 on the way count: a program that leaves them out, or rounds other values in their place, can miss the bound.
Values may be sent and summed in bfloat16 or wider, within the bound.
No kernel may reach another device: no remote copies, remote signals or barrier semaphores. Data moves between devices by JAX's collectives and lax.ppermute only.
A program may use at most 320 MiB of HBM per device.

```python
import math
import jax
import jax.numpy as jnp
import numpy as np
from jax import lax

D = 768
HEADS = 12
HD = 64
FF = 3072
TOK_DEV = 512
DOCS = 4
GROUPS = 8
ROW = 2048
TOKENS = 16384
FROZEN = 4
FRESH = 4
EXPERTS = 8
CAP = 768
PIECES = 8
SLICE_FF = 384
QBLOCK = 512


def draw_doc_lengths(key, part):
    key = jax.random.fold_in(key, 11)
    first_key, tail_key = jax.random.split(key, 2)
    leading = jax.random.randint(first_key, (GROUPS, 1), 1, TOK_DEV // 2 + 1, dtype=jnp.int32)
    trailing = jax.random.randint(tail_key, (GROUPS, DOCS - 2), 1, TOK_DEV // (2 * (DOCS - 2)) + 1, dtype=jnp.int32)
    longest = ROW - leading - jnp.sum(trailing, axis=1, keepdims=True)
    return jnp.concatenate([leading, longest, trailing], axis=1)


def with_spikes(result, own_key, source, target, parts, factor):
    def block_of(position):
        return (jnp.arange(result.shape[position]) // (result.shape[position] // parts)).reshape((-1,) + (1,) * (result.ndim - 1 - position))

    near = jax.random.permutation(own_key, parts)[block_of(target)]
    other_side = (block_of(target) + parts // 2) % parts
    return jnp.where((block_of(source) == near) | (block_of(source) == other_side), factor * result, result)


def block_levels(key, shape, shards, low, high):
    def one(dim, shards_of):
        heights = jax.random.uniform(jax.random.fold_in(jax.random.fold_in(key, 6), dim), (shards_of,), jnp.float32, low / len(shards), high / len(shards))
        return jnp.repeat(jnp.exp(heights), shape[dim] // shards_of).reshape((-1,) + (1,) * (len(shape) - dim - 1))

    loudness = one(*shards[0])
    for cut in shards[1:]:
        loudness = loudness * one(*cut)
    return loudness


def deal_out(key, own, number, rows, amount, top, most, lean):
    sequence = jax.random.permutation(key, amount)
    heavy_load, common = portions_of(amount, rows * top, most, lean, True), portions_of(amount, rows * top, most, lean, False)
    places = jnp.arange(amount)

    def named(tallies, rotation):
        used = int((tallies > 0).sum())
        fixed = max(1, used // 4)
        shifted = fixed + (places - fixed + rotation * (used - fixed)) % max(1, amount - fixed)
        return jnp.zeros((amount,), jnp.int32).at[sequence[jnp.where(places < fixed, places, shifted)]].set(jnp.asarray(tallies, jnp.int32))

    tallies = jnp.where(number % 4 == 0, named(heavy_load, number // 4), named(common, number - number // 4 - 1))
    mixed = jax.random.permutation(jax.random.fold_in(own, 3), amount)
    source_of, sink = mixed[0:amount // 2 * 2:2], mixed[1:amount // 2 * 2:2]
    slack = jnp.minimum(tallies[source_of] - 1, most - tallies[sink]) // 2
    slack = jnp.where((source_of == sequence[0]) | (sink == sequence[0]) | (tallies[sink] == 0), 0, jnp.maximum(slack, 0))
    shifted = jax.random.randint(jax.random.fold_in(own, 4), (amount // 2,), 0, 1 << 20) % (slack + 1)
    tallies = tallies.at[source_of].add(-shifted).at[sink].add(shifted)
    labels = jnp.searchsorted(jnp.cumsum(tallies), jnp.arange(rows * top), side="right").astype(jnp.int32)
    listing = labels.reshape(top, rows).T
    listing = listing[jax.random.permutation(jax.random.fold_in(own, 1), rows)]
    rotation = jax.random.randint(jax.random.fold_in(own, 2), (rows, 1), 0, top)
    return jnp.take_along_axis(listing, (jnp.arange(top)[None, :] + rotation) % top, axis=1)


def portions_of(number_of, total, most, lean, full):
    portions = [(1 << 20) // math.isqrt(rank ** lean) + 1 for rank in range(1, number_of + 1)]
    largest = most if full else min(most, max(-(-total // number_of), total * portions[0] // sum(portions)))
    least = 1 if total - largest >= number_of - 1 else 0
    given, surplus = [largest] + [least] * (number_of - 1), total - largest - least * (number_of - 1)
    while surplus > 0:
        movable = [i for i in range(1, number_of) if given[i] < largest] or [i for i in range(1, number_of) if given[i] < most]
        pool, budget = sum([portions[i] for i in movable]), surplus
        for i in movable:
            addition = min(most - given[i], max(1, budget * portions[i] // pool), surplus)
            given[i] = given[i] + addition
            surplus = surplus - addition
    return np.array(given)


def bell_draw(rng, shape, spread, limit, cuts=(), kind=jnp.bfloat16):
    entries = spread * jax.random.normal(rng, shape, jnp.float32)
    if cuts:
        entries = entries * block_levels(rng, shape, cuts, -0.22, 0.18)
    return jnp.clip(entries, -limit, limit).astype(kind)


def bell_draw_with(own_key, dims, deviation, bound, cuts, heavy, held_as=jnp.bfloat16):
    array = deviation * jax.random.normal(own_key, dims, jnp.float32)
    if cuts:
        array = array * block_levels(own_key, dims, cuts, -0.22, 0.18)
    return jnp.clip(with_spikes(array, jax.random.fold_in(own_key, 3), *heavy), -bound, bound).astype(held_as)


def setup_inputs(seed: int = 0) -> dict:
    key_of = jax.random.split(jax.random.key(seed), 14)
    block_input = bell_draw(key_of[0], (TOKENS, D), 1.0, 6.0, ((0, 32),))
    gain_one = jnp.clip(1.0 + 0.1 * jax.random.normal(key_of[1], (D,), jnp.float32), 0.5, 1.5)
    gain_two = jnp.clip(1.0 + 0.1 * jax.random.normal(key_of[2], (D,), jnp.float32), 0.5, 1.5)
    qkv_weight = bell_draw(key_of[3], (3, D, D), (D // 2) ** -0.5, 0.3125, ((1, 8), (2, 4)), jnp.float32)
    out_weight = bell_draw(key_of[4], (D, D), (D // 16) ** -0.5, 0.875, ((0, 4), (1, 8)), jnp.float32)
    gate_weight = bell_draw(key_of[5], (D, EXPERTS), (2 * D) ** -0.5, 0.15625, (), jnp.float32)
    frozen_in = bell_draw(key_of[6], (2 * FROZEN, D, FF // 2), D ** -0.5, 0.21875, ((0, 8), (2, 4)), jnp.float32)
    frozen_out = bell_draw(key_of[7], (2 * FROZEN, FF // 2, D), FF ** -0.5, 0.109375, ((0, 8), (1, 4)), jnp.float32)
    fresh_in = bell_draw(key_of[8], (2 * FRESH, D, FF // 2), D ** -0.5, 0.21875, ((0, 8), (2, 4)), jnp.float32)
    fresh_out = bell_draw(key_of[9], (2 * FRESH, FF // 2, D), FF ** -0.5, 0.109375, ((0, 8), (1, 4)), jnp.float32)
    routes_keys = jax.random.split(jax.random.fold_in(key_of[10], 1), TOKENS // ROW)
    routes_turns = jax.random.permutation(jax.random.fold_in(key_of[10], 3), TOKENS // ROW)
    routes = jax.vmap(lambda own, number: deal_out(jax.random.fold_in(key_of[10], 2), own, number, ROW, EXPERTS, 2, CAP, 1))(routes_keys, routes_turns).reshape((TOKENS, 2))
    doc_lengths = draw_doc_lengths(jax.random.fold_in(key_of[13], 71), 0)
    cotangent = bell_draw_with(key_of[12], (TOKENS, D), 1.0, 6.0, ((0, 32),), (0, 1, 32, 2.75))
    return {"block_input": block_input, "gain_one": gain_one, "gain_two": gain_two, "qkv_weight": qkv_weight, "out_weight": out_weight, "gate_weight": gate_weight, "frozen_in": frozen_in, "frozen_out": frozen_out, "fresh_in": fresh_in, "fresh_out": fresh_out, "routes": routes, "doc_lengths": doc_lengths, "cotangent": cotangent}


EPS = 1e-05
MASKED = -1000000000.0
ROOT_HALF = 0.7071067811865476

@jax.custom_vjp
def low(v):
    return lax.optimization_barrier(v.astype(jnp.bfloat16)).astype(jnp.float32)

@jax.custom_vjp
def low_back(v):
    return v

def low_keep(v):
    return (low(v), None)

def low_pass(kept, grad):
    return (grad,)

def back_keep(v):
    return (v, None)

def back_low(kept, grad):
    return (low(grad),)
low.defvjp(low_keep, low_pass)
low_back.defvjp(back_keep, back_low)

def gelu_value(inputs):
    return 0.5 * inputs * (1.0 + lax.erf(inputs * ROOT_HALF))

def layer_norm(values, gain):
    centred = values - lax.optimization_barrier(jnp.mean(values, axis=-1, keepdims=True))
    rstd = lax.rsqrt(lax.optimization_barrier(jnp.mean(centred * centred, axis=-1, keepdims=True)) + EPS)
    return centred * rstd * gain

def segment_ids(lengths):
    doc_ends = jnp.cumsum(lengths)
    places = jnp.arange(ROW, dtype=jnp.int32)
    return lax.optimization_barrier(jnp.sum((places[:, None] >= doc_ends[None, :]).astype(jnp.int32), axis=1))

def slot_places(group_routes):
    flat_ids = group_routes.reshape(-1)
    hit_table = (flat_ids[:, None] == jnp.arange(EXPERTS, dtype=jnp.int32)[None, :]).astype(jnp.int32)
    slot_index = lax.optimization_barrier(jnp.sum((jnp.cumsum(hit_table, axis=0) - 1) * hit_table, axis=1))
    kind_index = flat_ids // FROZEN
    places = (flat_ids % FROZEN * 2 + kind_index) * CAP + slot_index
    table = jnp.full((EXPERTS * CAP,), 2 * ROW, jnp.int32).at[places].set(jnp.arange(2 * ROW, dtype=jnp.int32))
    return (places, table)

def attend_group(group_rows, segments, qkv_low):
    score_scale = HD ** (-0.5)
    projected = [low_back(low(jnp.dot(group_rows, qkv_low[kind_index], precision=lax.Precision.HIGHEST))).reshape(ROW, HEADS, HD) for kind_index in range(3)]
    queries, key_rows, value_rows = projected
    places = jnp.arange(ROW, dtype=jnp.int32)

    def one_block(block_start):
        query_block = lax.dynamic_slice_in_dim(queries, block_start, QBLOCK, 0)
        seg_block = lax.dynamic_slice_in_dim(segments, block_start, QBLOCK, 0)
        pos_block = block_start + jnp.arange(QBLOCK, dtype=jnp.int32)
        scores = low_back(jnp.einsum('qhd,khd->hqk', query_block, key_rows, precision=lax.Precision.HIGHEST) * score_scale)
        allowed = (seg_block[:, None] == segments[None, :]) & (places[None, :] <= pos_block[:, None])
        scores = jnp.where(allowed[None], scores, MASKED)
        row_max = lax.optimization_barrier(jnp.max(scores, axis=-1, keepdims=True))
        raised = jnp.exp(scores - row_max)
        attn_probs = raised / lax.optimization_barrier(jnp.sum(raised, axis=-1, keepdims=True))
        return jnp.einsum('hqk,khd->qhd', low(attn_probs), value_rows, precision=lax.Precision.HIGHEST)
    starts = jnp.arange(ROW // QBLOCK, dtype=jnp.int32) * QBLOCK
    context = lax.map(jax.checkpoint(one_block), starts)
    return low_back(low(context.reshape(ROW, D)))

def run_expert(pieces):
    rows_in, first_w, second_w = pieces
    total_out = jnp.zeros((GROUPS * CAP, D), jnp.float32)
    for piece_index in range(PIECES):
        unit_range = slice(piece_index * SLICE_FF, (piece_index + 1) * SLICE_FF)
        hidden = low_back(jnp.dot(low_back(rows_in), first_w[:, unit_range], precision=lax.Precision.HIGHEST))
        activated = low(gelu_value(hidden))
        total_out = total_out + low_back(low(jnp.dot(activated, second_w[unit_range], precision=lax.Precision.HIGHEST)))
    return total_out

def first_layout(weights):
    return weights.reshape(FROZEN, 2, D, FF // 2).transpose(0, 2, 1, 3).reshape(FROZEN, D, FF)

def reference(block_input, gain_one, gain_two, qkv_weight, out_weight, gate_weight, frozen_in, frozen_out, fresh_in, fresh_out, routes, doc_lengths, cotangent):
    segments = jax.vmap(segment_ids)(doc_lengths)
    places, tables = jax.vmap(slot_places)(routes.reshape(GROUPS, ROW, 2))
    row_take = tables // 2
    frozen_first = first_layout(low(frozen_in))
    frozen_second = low(frozen_out).reshape(FROZEN, FF, D)

    def forward(inputs, gain_a, gain_b, qkv_w, out_w, gate_w, fresh_a, fresh_b):
        qkv_low = low(qkv_w)
        h_one = low(layer_norm(inputs, gain_a))
        context = lax.map(lambda group_pair: attend_group(group_pair[0], group_pair[1], qkv_low), (h_one.reshape(GROUPS, ROW, D), segments))
        attn = low_back(jnp.dot(context.reshape(TOKENS, D), low(out_w), precision=lax.Precision.HIGHEST))
        x_one = inputs + attn
        h_two = low(layer_norm(x_one, gain_b))
        logits = jnp.dot(h_two, low(gate_w), precision=lax.Precision.HIGHEST)
        chosen = jnp.take_along_axis(logits, routes, axis=1)
        gate_max = lax.optimization_barrier(jnp.max(chosen, axis=1, keepdims=True))
        gate_raised = jnp.exp(chosen - gate_max)
        gate_values = gate_raised / lax.optimization_barrier(jnp.sum(gate_raised, axis=1, keepdims=True))
        padded = jnp.concatenate([h_two.reshape(GROUPS, ROW, D), jnp.zeros((GROUPS, 1, D), jnp.float32)], axis=1)
        buffers = jax.vmap(lambda rows_group, take_group: rows_group[take_group])(padded, row_take)
        expert_rows = buffers.reshape(GROUPS, FROZEN, 2, CAP, D).transpose(2, 1, 0, 3, 4).reshape(EXPERTS, GROUPS * CAP, D)
        first_all = jnp.concatenate([frozen_first, first_layout(low(fresh_a))], axis=0)
        second_all = jnp.concatenate([frozen_second, low(fresh_b).reshape(FRESH, FF, D)], axis=0)
        outputs = lax.map(jax.checkpoint(run_expert), (expert_rows, first_all, second_all))
        outputs = outputs.reshape(2, FROZEN, GROUPS, CAP, D).transpose(2, 1, 0, 3, 4).reshape(GROUPS, EXPERTS * CAP, D)
        per_route = jax.vmap(lambda out_group, place_group: out_group[place_group])(outputs, places).reshape(TOKENS, 2, D)
        mixture = lax.optimization_barrier(jnp.sum(gate_values[:, :, None] * per_route, axis=1))
        return x_one + mixture
    output, pullback = jax.vjp(forward, block_input.astype(jnp.float32), gain_one, gain_two, qkv_weight, out_weight, gate_weight, fresh_in, fresh_out)
    grads = pullback(cotangent.astype(jnp.float32))
    return (output.astype(jnp.bfloat16), grads[0], grads[1], grads[2], grads[3], grads[4], grads[5], grads[6], grads[7])
```

```python
import functools

import jax
import jax.numpy as jnp
from jax import lax
from jax.experimental import pallas as pl
from jax.experimental.pallas import tpu as pltpu
from jax.sharding import PartitionSpec as P

HD = 64
EPS = 1e-05
MASKED = -1000000000.0
ROOT_HALF = 0.7071067811865476
INV_ROOT_TAU = 0.3989422804014327
BLOCK = 256
LOW = jnp.bfloat16
WIDE = jnp.float32
NT = (((1,), (1,)), ((), ()))
TN = (((0,), (0,)), ((), ()))


def mm(a, b):
    return jnp.dot(a, b, preferred_element_type=WIDE)


def mm_nt(a, b):
    return lax.dot_general(a, b, NT, preferred_element_type=WIDE)


def mm_tn(a, b):
    return lax.dot_general(a, b, TN, preferred_element_type=WIDE)


def flip(array, axis, bits):
    size = lax.axis_size(axis)
    return lax.ppermute(array, axis, [(i, i ^ bits) for i in range(size)])


def norm_parts(values):
    centred = values - jnp.mean(values, axis=-1, keepdims=True)
    rstd = lax.rsqrt(jnp.mean(centred * centred, axis=-1, keepdims=True) + EPS)
    return centred * rstd, rstd


def norm_back(grad_out, normed, rstd, gain):
    scaled = grad_out * gain
    mean_plain = jnp.mean(scaled, axis=-1, keepdims=True)
    mean_normed = jnp.mean(scaled * normed, axis=-1, keepdims=True)
    return rstd * (scaled - mean_plain - normed * mean_normed)


def head_pieces(piece):
    far = flip(piece, "head", 2)
    near = flip(piece, "head", 1)
    return [piece, near, far, flip(far, "head", 1)]


def in_order(pieces, index):
    rows = pieces[0].shape[0]
    out = jnp.zeros((rows * len(pieces),) + pieces[0].shape[1:], pieces[0].dtype)
    for k, piece in enumerate(pieces):
        out = lax.dynamic_update_slice_in_dim(out, piece, (index ^ k) * rows, 0)
    return out


def over_dp(piece, axis):
    size, index = lax.axis_size("dp"), lax.axis_index("dp")
    bits, span, width = size // 2, 1, piece.shape[axis]
    held = {0: piece}
    while bits:
        joined = flip(jnp.stack(list(held.values())), "dp", bits)
        held.update({k ^ bits: joined[n] for n, k in enumerate(list(held))})
        bits //= 2
    shape = list(piece.shape)
    shape[axis] *= size
    out = jnp.zeros(shape, piece.dtype)
    for k, one in held.items():
        out = lax.dynamic_update_slice_in_dim(out, one, (index ^ k) * width, axis)
    return out


def sum_everywhere(value):
    for axis in ("head", "dp"):
        bits = 1
        while bits < lax.axis_size(axis):
            value = value + flip(value, axis, bits)
            bits *= 2
    return value


def sum_over_dp_scattered(value, axis):
    size, index = lax.axis_size("dp"), lax.axis_index("dp")
    width = value.shape[axis] // size
    held = {
        k: lax.dynamic_slice_in_dim(value, (index ^ k) * width, width, axis) for k in range(size)
    }
    bits = 1
    while bits < size:
        keep = [k for k in held if not k & bits]
        come = flip(jnp.stack([held[k ^ bits].astype(LOW) for k in keep]), "dp", bits)
        held = {k: held[k] + come[n].astype(WIDE) for n, k in enumerate(keep)}
        bits *= 2
    return held[0]


def sum_over_head(partial):
    near = lax.axis_index("head") % 2
    half = partial.shape[0] // 2
    mine = lax.dynamic_slice_in_dim(partial, near * half, half, 0)
    other = lax.dynamic_slice_in_dim(partial, (1 - near) * half, half, 0)
    mine = (mine + flip(other.astype(LOW), "head", 1).astype(WIDE)).astype(LOW)
    mine = mine.astype(WIDE) + flip(mine, "head", 2).astype(WIDE)
    mine = mine.astype(LOW)
    back = flip(mine, "head", 1)
    return jnp.concatenate(
        [jnp.where(near == 0, mine, back), jnp.where(near == 0, back, mine)], axis=0
    ).astype(WIDE)


def own_sum_over_head(partial):
    index, size = lax.axis_index("head"), lax.axis_size("head")
    rows = partial.shape[0] // size
    cut = [lax.dynamic_slice_in_dim(partial, (index ^ k) * rows, rows, 0) for k in range(size)]
    come = flip(jnp.stack([cut[1], cut[3]]).astype(LOW), "head", 1).astype(WIDE)
    far = flip((cut[2] + come[1]).astype(LOW), "head", 2).astype(WIDE)
    return cut[0] + come[0] + far


def attend_kernel(first_ref, start_ref, qt_ref, k_ref, vt_ref, ctx_ref, ctxt_ref, lse_ref):
    step = pl.program_id(0)
    heads = qt_ref.shape[0]
    start = start_ref[...]
    key_iota = lax.broadcasted_iota(jnp.int32, (BLOCK, BLOCK), 0)
    query_iota = lax.broadcasted_iota(jnp.int32, (BLOCK, BLOCK), 1)

    def block(j, carry, last):
        base = pl.multiple_of(j * BLOCK, BLOCK)
        allowed = key_iota + base >= start
        if last:
            allowed = allowed & (key_iota <= query_iota)
        out = []
        for h in range(heads):
            top, total, acc = carry[h]
            scores = mm(k_ref[h, pl.ds(base, BLOCK), :], qt_ref[h])
            scores = jnp.where(allowed, scores, MASKED)
            peak = jnp.maximum(top, jnp.max(scores, axis=0, keepdims=True))
            raised = jnp.exp(scores - peak)
            fade = jnp.exp(top - peak)
            total = total * fade + jnp.sum(raised, axis=0, keepdims=True)
            acc = acc * fade + mm(vt_ref[h, :, pl.ds(base, BLOCK)], raised.astype(LOW))
            out.append((peak, total, acc))
        return tuple(out)

    carry = tuple(
        (
            jnp.full((1, BLOCK), MASKED, WIDE),
            jnp.zeros((1, BLOCK), WIDE),
            jnp.zeros((HD, BLOCK), WIDE),
        )
        for _ in range(heads)
    )
    carry = lax.fori_loop(first_ref[step], step, lambda j, c: block(j, c, False), carry)
    carry = block(step, carry, True)
    parts = []
    for h in range(heads):
        top, total, acc = carry[h]
        acc = acc / total
        ctxt_ref[h] = acc
        lse_ref[h] = top + jnp.log(total)
        parts.append(acc.T)
    ctx_ref[...] = jnp.concatenate(parts, axis=1).astype(LOW)


def attend(first, start, qt, keys, vt):
    heads, _, rows = qt.shape
    grid_spec = pltpu.PrefetchScalarGridSpec(
        num_scalar_prefetch=1,
        grid=(rows // BLOCK,),
        in_specs=[
            pl.BlockSpec((1, BLOCK), lambda i, f: (0, i)),
            pl.BlockSpec((heads, HD, BLOCK), lambda i, f: (0, 0, i)),
            pl.BlockSpec((heads, rows, HD), lambda i, f: (0, 0, 0)),
            pl.BlockSpec((heads, HD, rows), lambda i, f: (0, 0, 0)),
        ],
        out_specs=[
            pl.BlockSpec((BLOCK, heads * HD), lambda i, f: (i, 0)),
            pl.BlockSpec((heads, HD, BLOCK), lambda i, f: (0, 0, i)),
            pl.BlockSpec((heads, 1, BLOCK), lambda i, f: (0, 0, i)),
        ],
    )
    return pl.pallas_call(
        attend_kernel,
        grid_spec=grid_spec,
        out_shape=[
            jax.ShapeDtypeStruct((rows, heads * HD), LOW),
            jax.ShapeDtypeStruct((heads, HD, rows), WIDE),
            jax.ShapeDtypeStruct((heads, 1, rows), WIDE),
        ],
        compiler_params=pltpu.CompilerParams(vmem_limit_bytes=40 * 2**20),
        cost_estimate=pl.CostEstimate(
            flops=8 * rows * rows * HD * heads, bytes_accessed=8 * 2**20, transcendentals=0
        ),
    )(first, start, qt, keys, vt)


def attend_back_kernel(
    first_ref, start_ref, qt_ref, q_ref, k_ref, kt_ref, v_ref, gt_ref, g_ref, ctxt_ref, lse_ref,
    dq_ref, dk_ref, dv_ref, dk_acc, dv_acc,
):
    step = pl.program_id(0)
    heads = qt_ref.shape[0]
    start = start_ref[...]
    key_iota = lax.broadcasted_iota(jnp.int32, (BLOCK, BLOCK), 0)
    query_iota = lax.broadcasted_iota(jnp.int32, (BLOCK, BLOCK), 1)

    @pl.when(step == 0)
    def _():
        dk_acc[...] = jnp.zeros_like(dk_acc)
        dv_acc[...] = jnp.zeros_like(dv_acc)

    delta = [
        jnp.sum(gt_ref[h].astype(WIDE) * ctxt_ref[h], axis=0, keepdims=True) for h in range(heads)
    ]

    def block(j, carry, last):
        base = pl.multiple_of(j * BLOCK, BLOCK)
        rows = pl.ds(base, BLOCK)
        allowed = key_iota + base >= start
        if last:
            allowed = allowed & (key_iota <= query_iota)
        out = []
        for h in range(heads):
            scores = mm(k_ref[h, rows, :], qt_ref[h])
            probs = jnp.where(allowed, jnp.exp(scores - lse_ref[h]), 0.0)
            slopes = mm(v_ref[h, rows, :], gt_ref[h])
            score_grads = (probs * (slopes - delta[h])).astype(LOW)
            dv_acc[h, rows, :] += mm(probs.astype(LOW), g_ref[h])
            dk_acc[h, rows, :] += mm(score_grads, q_ref[h])
            out.append(carry[h] + mm(kt_ref[h, :, rows], score_grads))
        return tuple(out)

    carry = tuple(jnp.zeros((HD, BLOCK), WIDE) for _ in range(heads))
    carry = lax.fori_loop(first_ref[step], step, lambda j, c: block(j, c, False), carry)
    carry = block(step, carry, True)
    scale = HD**-0.5
    dq_ref[...] = jnp.concatenate([(c * scale).T for c in carry], axis=1).astype(LOW)

    @pl.when(step == pl.num_programs(0) - 1)
    def _():
        for n in range(dk_acc.shape[1] // BLOCK):
            rows = slice(n * BLOCK, (n + 1) * BLOCK)
            dk_ref[rows, :] = jnp.concatenate(
                [dk_acc[h, rows, :] for h in range(heads)], axis=1
            ).astype(LOW)
            dv_ref[rows, :] = jnp.concatenate(
                [dv_acc[h, rows, :] for h in range(heads)], axis=1
            ).astype(LOW)


def attend_back(first, start, qt, q, keys, kt, values, gt, g, ctxt, lse):
    heads, _, rows = qt.shape
    by_column = pl.BlockSpec((heads, HD, BLOCK), lambda i, f: (0, 0, i))
    by_row = pl.BlockSpec((heads, BLOCK, HD), lambda i, f: (0, i, 0))
    all_rows = pl.BlockSpec((heads, rows, HD), lambda i, f: (0, 0, 0))
    all_columns = pl.BlockSpec((heads, HD, rows), lambda i, f: (0, 0, 0))
    whole = pl.BlockSpec((rows, heads * HD), lambda i, f: (0, 0))
    grid_spec = pltpu.PrefetchScalarGridSpec(
        num_scalar_prefetch=1,
        grid=(rows // BLOCK,),
        in_specs=[
            pl.BlockSpec((1, BLOCK), lambda i, f: (0, i)),
            by_column,
            by_row,
            all_rows,
            all_columns,
            all_rows,
            by_column,
            by_row,
            by_column,
            pl.BlockSpec((heads, 1, BLOCK), lambda i, f: (0, 0, i)),
        ],
        out_specs=[pl.BlockSpec((BLOCK, heads * HD), lambda i, f: (i, 0)), whole, whole],
        scratch_shapes=[pltpu.VMEM((heads, rows, HD), WIDE)] * 2,
    )
    return pl.pallas_call(
        attend_back_kernel,
        grid_spec=grid_spec,
        out_shape=[jax.ShapeDtypeStruct((rows, heads * HD), LOW)] * 3,
        compiler_params=pltpu.CompilerParams(vmem_limit_bytes=50 * 2**20),
        cost_estimate=pl.CostEstimate(
            flops=20 * rows * rows * HD * heads, bytes_accessed=8 * 2**20, transcendentals=0
        ),
    )(first, start, qt, q, keys, kt, values, gt, g, ctxt, lse)


def expert_kernel(
    own_ref, x_ref, c_ref, pair_ref, wg_ref, w1_ref, w2_ref,
    a_ref, du_ref, dx_ref, dy_ref, mark_ref, gate_ref, acc, dots, others,
):
    step = pl.program_id(0)
    rows, kinds = x_ref.shape[0], wg_ref.shape[1]
    lanes = lax.broadcasted_iota(jnp.int32, (rows, kinds), 1)
    own = own_ref[0]

    @pl.when(step == 0)
    def _():
        logits = mm(x_ref[...], wg_ref[...])
        here, there = lanes == own, lanes == pair_ref[...] - own
        mine = jnp.sum(jnp.where(here, logits, 0.0), axis=1, keepdims=True)
        theirs = jnp.sum(jnp.where(there, logits, 0.0), axis=1, keepdims=True)
        peak = jnp.maximum(mine, theirs)
        mine, theirs = jnp.exp(mine - peak), jnp.exp(theirs - peak)
        gate_ref[...] = mine / (mine + theirs)
        others[...] = theirs / (mine + theirs)
        dy_ref[...] = (gate_ref[...] * c_ref[...].astype(WIDE)).astype(LOW)
        acc[...] = jnp.zeros_like(acc)
        dots[...] = jnp.zeros_like(dots)

    size = 128
    for n in range(rows // size):
        part = slice(n * size, (n + 1) * size)
        u = mm(x_ref[part, :], w1_ref[0])
        da = mm_nt(c_ref[part, :], w2_ref[0])
        share = 0.5 * (1.0 + lax.erf(u * ROOT_HALF))
        a = (u * share).astype(LOW)
        slope = share + u * jnp.exp(-0.5 * u * u) * INV_ROOT_TAU
        dots[part, :] += jnp.sum(a.astype(WIDE) * da, axis=1, keepdims=True)
        du = (gate_ref[part, :] * da * slope).astype(LOW)
        a_ref[part, :] = a
        du_ref[part, :] = du
        acc[part, :] += mm_nt(du, w1_ref[0])

    @pl.when(step == pl.num_programs(0) - 1)
    def _():
        pull = gate_ref[...] * others[...] * dots[...]
        here, there = lanes == own, lanes == pair_ref[...] - own
        marks = jnp.where(here, pull, 0.0) - jnp.where(there, pull, 0.0)
        mark_ref[...] = marks
        high = marks.astype(LOW)
        rest = (marks - high.astype(WIDE)).astype(LOW)
        dx_ref[...] = (acc[...] + mm_nt(high, wg_ref[...]) + mm_nt(rest, wg_ref[...])).astype(LOW)


def run_experts(own, x, c, pairs, gate_low, first, second):
    rows, features = x.shape
    count, _, units = first.shape
    kinds = gate_low.shape[1]
    whole = lambda *shape: pl.BlockSpec(shape, lambda p, o: (0,) * len(shape))
    by_piece = pl.BlockSpec((rows, units), lambda p, o: (0, p))
    grid_spec = pltpu.PrefetchScalarGridSpec(
        num_scalar_prefetch=1,
        grid=(count,),
        in_specs=[
            whole(rows, features),
            whole(rows, features),
            whole(rows, 1),
            whole(features, kinds),
            pl.BlockSpec((1, features, units), lambda p, o: (p, 0, 0)),
            pl.BlockSpec((1, units, features), lambda p, o: (p, 0, 0)),
        ],
        out_specs=[
            by_piece,
            by_piece,
            whole(rows, features),
            whole(rows, features),
            whole(rows, kinds),
            whole(rows, 1),
        ],
        scratch_shapes=[
            pltpu.VMEM((rows, features), WIDE),
            pltpu.VMEM((rows, 1), WIDE),
            pltpu.VMEM((rows, 1), WIDE),
        ],
    )
    return pl.pallas_call(
        expert_kernel,
        grid_spec=grid_spec,
        out_shape=[
            jax.ShapeDtypeStruct((rows, count * units), LOW),
            jax.ShapeDtypeStruct((rows, count * units), LOW),
            jax.ShapeDtypeStruct((rows, features), LOW),
            jax.ShapeDtypeStruct((rows, features), LOW),
            jax.ShapeDtypeStruct((rows, kinds), WIDE),
            jax.ShapeDtypeStruct((rows, 1), WIDE),
        ],
        compiler_params=pltpu.CompilerParams(vmem_limit_bytes=50 * 2**20),
        cost_estimate=pl.CostEstimate(
            flops=10 * rows * features * count * units,
            bytes_accessed=24 * 2**20,
            transcendentals=0,
        ),
    )(own, x, c, pairs, gate_low, first, second)


def split_dot(a, marks):
    high = marks.astype(LOW)
    rest = (marks - high.astype(WIDE)).astype(LOW)
    return mm_tn(a, high) + mm_tn(a, rest)


def body(
    block_input,
    gain_one,
    gain_two,
    qkv_weight,
    out_weight,
    gate_weight,
    frozen_in,
    frozen_out,
    fresh_in,
    fresh_out,
    routes,
    doc_lengths,
    cotangent,
):
    own_rows, features = block_input.shape
    head_count, dp_count = lax.axis_size("head"), lax.axis_size("dp")
    head_index, dp_index = lax.axis_index("head"), lax.axis_index("dp")
    total = own_rows * head_count
    kinds = gate_weight.shape[1]
    share = 3 * total // kinds // head_count
    width = qkv_weight.shape[2]
    heads = width // HD
    first_own = head_index * own_rows

    def own_part(array):
        return lax.dynamic_slice_in_dim(array, first_own, own_rows, 0)

    rows_in = in_order(head_pieces(block_input), head_index).astype(WIDE)
    qkv = over_dp(qkv_weight.astype(LOW), 1)

    tokens = jnp.arange(total, dtype=jnp.int32)
    hits = (routes[:, :, None] == jnp.arange(kinds, dtype=jnp.int32)).astype(LOW)
    earlier = (tokens[:, None] > tokens[None, :]).astype(LOW)
    counts = mm(earlier, hits.reshape(total, 2 * kinds)).reshape(total, 2, kinds)
    counts = counts + jnp.sum(hits[:, 0].astype(WIDE), axis=0)[None, None] * jnp.array([0.0, 1.0])[None, :, None]
    slots = jnp.sum(counts * hits.astype(WIDE), axis=2).astype(jnp.int32)
    hosts = routes % (kinds // 2) * 2 + routes // (kinds // 2)
    places = (hosts ^ dp_index) * share + slots // head_count
    places = jnp.where(slots % head_count == head_index, places, -1)
    spots = jnp.arange(dp_count * share, dtype=jnp.int32)[:, None]
    picks = ((places[:, 0][None] == spots) | (places[:, 1][None] == spots)).astype(LOW)
    pair_sums = jnp.sum(routes, axis=1).astype(LOW)
    pairs_out = mm(picks, pair_sums[:, None]).reshape(dp_count, share)

    def exchange(rows):
        parts = rows.reshape(dp_count, share, rows.shape[-1])
        return [parts[0]] + [flip(parts[k], "dp", k) for k in range(1, dp_count)]

    order = dp_index ^ jnp.arange(dp_count, dtype=jnp.int32)
    pairs_out = jnp.sum(
        jnp.where((order[:, None] == jnp.arange(dp_count)[None])[:, :, None], pairs_out[:, None], 0.0), axis=0
    )
    pairs_in = lax.all_to_all(pairs_out, "dp", 0, 0, tiled=True)
    pairs_in = jnp.sum(
        jnp.where((order[:, None] == jnp.arange(dp_count)[None])[:, :, None], pairs_in[None], 0.0), axis=1
    )
    pairs_in = pairs_in.reshape(dp_count * share, 1).astype(jnp.int32)

    upstream_rows = in_order(head_pieces(cotangent), head_index)
    c_parts = exchange(mm(picks, upstream_rows).astype(LOW))

    odd = dp_index % 2
    keep_in = jnp.where(odd == 0, frozen_in[0], fresh_in[0]).astype(LOW)
    keep_out = jnp.where(odd == 0, frozen_out[0], fresh_out[0]).astype(LOW)
    give_in = jnp.where(odd == 0, fresh_in[0], frozen_in[0]).astype(LOW)
    give_out = jnp.where(odd == 0, fresh_out[0], frozen_out[0]).astype(LOW)
    half_in = jnp.stack([keep_in, flip(give_in, "dp", 1)])
    half_out = jnp.stack([keep_out, flip(give_out, "dp", 1)])
    first = jnp.concatenate(head_pieces(half_in))
    second = jnp.concatenate(head_pieces(half_out))
    own_kind = dp_index // 2 + odd * (kinds // 2)

    normed_one, rstd_one = norm_parts(rows_in)
    h_one = (normed_one * gain_one).astype(LOW)
    by_head = qkv.reshape(3, features, heads, HD)
    scale = HD**-0.5

    def columns(weight):
        return jnp.einsum("dhe,rd->her", weight, h_one, preferred_element_type=WIDE).astype(LOW)

    def lines(weight):
        return jnp.einsum("rd,dhe->hre", h_one, weight, preferred_element_type=WIDE).astype(LOW)

    qt, queries = columns(by_head[0]) * scale, lines(by_head[0]) * scale
    kt, keys = columns(by_head[1]), lines(by_head[1])
    vt, values = columns(by_head[2]), lines(by_head[2])
    qt, queries = qt.astype(LOW), queries.astype(LOW)
    ends = jnp.cumsum(doc_lengths[0])
    start = jnp.max(jnp.where(tokens[:, None] >= ends[None], ends[None], 0), axis=1)
    first_block = start[::BLOCK] // BLOCK
    start = start[None]
    context, context_t, log_totals = attend(first_block, start, qt, keys, vt)

    out_full = over_dp(out_weight.astype(LOW), 1)
    out_pieces = jnp.concatenate(head_pieces(out_full))
    contexts = jnp.concatenate(head_pieces(context), axis=1)
    x_one = rows_in + mm(contexts, out_pieces)
    normed_two, rstd_two = norm_parts(x_one)
    h_two = (normed_two * gain_two).astype(LOW)

    gate_low = gate_weight.astype(LOW)
    x_parts = exchange(mm(picks, h_two).astype(LOW))
    per = dp_count // 4
    own_list = own_kind.astype(jnp.int32)[None]
    done = []
    for n in range(4):
        ks = range(n * per, (n + 1) * per)
        x = jnp.concatenate([x_parts[k] for k in ks])
        c = jnp.concatenate([c_parts[k] for k in ks])
        done.append(
            (x,) + tuple(run_experts(
                own_list, x, c, pairs_in[n * per * share : (n + 1) * per * share], gate_low, first, second
            ))
        )
    dx_parts = []
    for n in range(4):
        for m in range(per):
            k = n * per + m
            part = done[n][3][m * share : (m + 1) * share]
            dx_parts.append(part if k == 0 else flip(part, "dp", k))
    dx_rows = jnp.concatenate(dx_parts)
    dh_two = sum_over_head(mm_tn(picks, dx_rows))

    hidden_low = jnp.concatenate([d[1] for d in done])
    hidden_grads = jnp.concatenate([d[2] for d in done])
    x_all = jnp.concatenate([d[0] for d in done])
    dy_all = jnp.concatenate([d[4] for d in done])
    marks = jnp.concatenate([d[5] for d in done])
    gates = jnp.concatenate([d[6] for d in done])
    units = first.shape[2]
    gated = (mm(hidden_low, second.reshape(-1, features)) * gates).astype(LOW)
    gated = jnp.concatenate(exchange(gated))
    mixture = own_sum_over_head(mm_tn(picks, gated))
    result = (own_part(x_one) + mixture).astype(LOW)
    grad_second = mm_tn(hidden_low, dy_all).reshape(head_count, 2, units, features)
    grad_first = jnp.stack(
        [
            mm_tn(x_all, hidden_grads[:, n * units : (n + 1) * units])
            for n in range(2 * head_count)
        ]
    ).reshape(head_count, 2, features, units)

    def home(grad):
        come = flip(jnp.stack([grad[1], grad[3]]).astype(LOW), "head", 1).astype(WIDE)
        far = flip((grad[2] + come[1]).astype(LOW), "head", 2).astype(WIDE)
        both = grad[0] + come[0] + far
        other = flip(both[1].astype(LOW), "dp", 1).astype(WIDE)
        return jnp.where(odd == 1, both[0], other)[None]

    grad_fresh_in, grad_fresh_out = home(grad_first), home(grad_second)
    grad_gate = split_dot(x_all, marks)

    upstream = upstream_rows.astype(WIDE)
    dx_one = upstream + norm_back(dh_two, normed_two, rstd_two, gain_two)
    grad_gain_two = jnp.sum(own_part(dh_two) * own_part(normed_two), axis=0)
    dattn = dx_one.astype(LOW)
    out_heads = out_full.reshape(heads, HD, features)
    gt = jnp.einsum("hed,rd->her", out_heads, dattn, preferred_element_type=WIDE).astype(LOW)
    g = jnp.einsum("rd,hed->hre", dattn, out_heads, preferred_element_type=WIDE).astype(LOW)
    dq, dk, dv = attend_back(
        first_block, start, qt, queries, keys, kt, values, gt, g, context_t, log_totals
    )
    grad_out_weight = sum_over_dp_scattered(mm_tn(context, dattn), 1)
    dqkv = jnp.concatenate([dq, dk, dv], axis=1)
    back_weight = qkv.transpose(1, 0, 2).reshape(features, 3 * width)
    dh_one = own_sum_over_head(mm_nt(dqkv, back_weight))
    grad_qkv = mm_tn(h_one, dqkv).reshape(features, 3, width).transpose(1, 0, 2)
    grad_qkv = sum_over_dp_scattered(grad_qkv, 1)
    own_normed, own_rstd = own_part(normed_one), own_part(rstd_one)
    grad_input = own_part(dx_one) + norm_back(dh_one, own_normed, own_rstd, gain_one)
    grad_gain_one = jnp.sum(dh_one * own_normed, axis=0)
    small = sum_everywhere(jnp.concatenate([grad_gain_two[None], grad_gate.T]))
    grad_gain_one = sum_everywhere(grad_gain_one)
    return (
        result,
        grad_input,
        grad_gain_one,
        small[0],
        grad_qkv,
        grad_out_weight,
        small[1:].T,
        grad_fresh_in,
        grad_fresh_out,
    )


def solution(mesh):
    return jax.shard_map(
        body,
        mesh=mesh,
        in_specs=(
            P(("dp", "head"), None),
            P(),
            P(),
            P(None, "dp", "head"),
            P("head", "dp"),
            P(),
            P("dp", None, "head"),
            P("dp", "head", None),
            P("dp", None, "head"),
            P("dp", "head", None),
            P("dp", None),
            P("dp", None),
            P(("dp", "head"), None),
        ),
        out_specs=(
            P(("dp", "head"), None),
            P(("dp", "head"), None),
            P(),
            P(),
            P(None, "dp", "head"),
            P("head", "dp"),
            P(),
            P("dp", None, "head"),
            P("dp", "head", None),
        ),
        check_vma=False,
    )
```

```python
import functools

import jax
import jax.numpy as jnp
from jax import lax
from jax.experimental import pallas as pl
from jax.experimental.pallas import tpu as pltpu
from jax.sharding import PartitionSpec as P

HD = 64
EPS = 1e-05
MASKED = -1000000000.0
ROOT_HALF = 0.7071067811865476
INV_ROOT_TAU = 0.3989422804014327
BLOCK = 512
LOW = jnp.bfloat16
WIDE = jnp.float32
LITTLE = pl.CostEstimate(flops=10**6, bytes_accessed=10**5, transcendentals=0)
NT = (((1,), (1,)), ((), ()))
TN = (((0,), (0,)), ((), ()))
ERF_P = 0.4
ERF_C = (
    0.11596113048765463,
    0.08091125192311208,
    0.23413842084756234,
    -0.1854556415158047,
    0.35457470270248115,
    -0.10012987827403336,
)


def mm(a, b):
    return jnp.dot(a, b, preferred_element_type=WIDE)


def mm_nt(a, b):
    return lax.dot_general(a, b, NT, preferred_element_type=WIDE)


def mm_tn(a, b):
    return lax.dot_general(a, b, TN, preferred_element_type=WIDE)


def spot_of(k):
    return (k % 2) * 2 + k // 2


def select_piece(spot, refs, out):
    for n, ref in enumerate(refs):

        @pl.when((spot == n) if n < 2 else (spot >= 2))
        def _(ref=ref):
            out[...] = ref[...]


def piece_specs(rows, features, spot):
    still = pl.BlockSpec((rows, features), lambda *i: (0, 0))
    return [still, still, pl.BlockSpec((rows, features), lambda *i: (jnp.maximum(spot(*i) - 2, 0), 0))]


def norm_parts(values):
    centred = values - jnp.mean(values, axis=-1, keepdims=True)
    rstd = lax.rsqrt(jnp.mean(centred * centred, axis=-1, keepdims=True) + EPS)
    return centred * rstd, rstd


def attend_kernel(
    meta_ref, start_ref, x_own_ref, x_far_ref, x_near_ref, gain_ref, w_ref,
    h_ref, qt_ref, q_ref, k_ref, kt_ref, v_ref, ctx_ref, ctxt_ref, lse_ref, k_all, vt_all, x_ref,
):
    step = pl.program_id(0)
    heads = qt_ref.shape[0]
    width = heads * HD
    start = start_ref[...]
    key_iota = lax.broadcasted_iota(jnp.int32, (BLOCK, BLOCK), 0)
    query_iota = lax.broadcasted_iota(jnp.int32, (BLOCK, BLOCK), 1)

    select_piece(spot_of(step ^ meta_ref[0]), (x_own_ref, x_far_ref, x_near_ref), x_ref)
    normed, _ = norm_parts(x_ref[...].astype(WIDE))
    h_one = (normed * gain_ref[...]).astype(LOW)
    h_ref[...] = h_one
    here = pl.ds(pl.multiple_of(step * BLOCK, BLOCK), BLOCK)
    q = mm(h_one, w_ref[:, :width]).astype(LOW) * (HD**-0.5)
    k = mm(h_one, w_ref[:, width : 2 * width]).astype(LOW)
    v = mm(h_one, w_ref[:, 2 * width : 3 * width]).astype(LOW)
    q = q.astype(LOW)
    q_t, k_t, v_t = q.T, k.T, v.T
    for h in range(heads):
        rows = slice(h * HD, (h + 1) * HD)
        qt_ref[h] = q_t[rows]
        q_ref[h] = q[:, rows]
        kt_ref[h] = k_t[rows]
        k_ref[h] = k[:, rows]
        k_all[h, here, :] = k[:, rows]
        v_ref[h] = v[:, rows]
        vt_all[h, :, here] = v_t[rows]

    def block(j, carry, last):
        base = pl.multiple_of(j * BLOCK, BLOCK)
        allowed = key_iota + base >= start
        if last:
            allowed = allowed & (key_iota <= query_iota)
        out = []
        for h in range(heads):
            top, total, acc = carry[h]
            scores = mm(k_all[h, pl.ds(base, BLOCK), :], qt_ref[h])
            scores = jnp.where(allowed, scores, MASKED)
            peak = jnp.maximum(top, jnp.max(scores, axis=0, keepdims=True))
            raised = jnp.exp(scores - peak)
            fade = jnp.exp(top - peak)
            total = total * fade + jnp.sum(raised, axis=0, keepdims=True)
            acc = acc * fade + mm(vt_all[h, :, pl.ds(base, BLOCK)], raised.astype(LOW))
            out.append((peak, total, acc))
        return tuple(out)

    carry = tuple(
        (
            jnp.full((1, BLOCK), MASKED, WIDE),
            jnp.zeros((1, BLOCK), WIDE),
            jnp.zeros((HD, BLOCK), WIDE),
        )
        for _ in range(heads)
    )
    carry = lax.fori_loop(meta_ref[1 + step], step, lambda j, c: block(j, c, False), carry)
    carry = block(step, carry, True)
    for h in range(heads):
        top, total, acc = carry[h]
        acc = acc / total
        ctxt_ref[h] = acc
        lse_ref[h] = top + jnp.log(total)
        ctx_ref[h * HD : (h + 1) * HD, :] = acc.astype(LOW)


def attend(meta, start, pieces, gain, weights, width):
    features = gain.shape[1]
    rows = 4 * BLOCK
    heads = width // HD
    spot = lambda i, m: spot_of(i ^ m[0])
    place = lambda i, m: (spot(i, m), 0)

    by_column = pl.BlockSpec((heads, HD, BLOCK), lambda i, m: (0, 0, i))
    by_row = pl.BlockSpec((heads, BLOCK, HD), lambda i, m: (0, i, 0))
    grid_spec = pltpu.PrefetchScalarGridSpec(
        num_scalar_prefetch=1,
        grid=(rows // BLOCK,),
        in_specs=[
            pl.BlockSpec((1, BLOCK), lambda i, m: (0, i)),
            *piece_specs(BLOCK, features, spot),
            pl.BlockSpec((1, features), lambda i, m: (0, 0)),
            pl.BlockSpec(weights.shape, lambda i, m: (0, 0)),
        ],
        out_specs=[
            pl.BlockSpec((BLOCK, features), place),
            by_column,
            by_row,
            by_row,
            by_column,
            by_row,
            pl.BlockSpec((width, BLOCK), lambda i, m: (0, spot(i, m))),
            by_column,
            pl.BlockSpec((heads, 1, BLOCK), lambda i, m: (0, 0, i)),
        ],
        scratch_shapes=[
            pltpu.VMEM((heads, rows, HD), LOW),
            pltpu.VMEM((heads, HD, rows), LOW),
            pltpu.VMEM((BLOCK, features), LOW),
        ],
    )
    tall = jax.ShapeDtypeStruct((heads, rows, HD), LOW)
    flat = jax.ShapeDtypeStruct((heads, HD, rows), LOW)
    return pl.pallas_call(
        attend_kernel,
        grid_spec=grid_spec,
        out_shape=[
            jax.ShapeDtypeStruct((rows, features), LOW),
            flat,
            tall,
            tall,
            flat,
            tall,
            jax.ShapeDtypeStruct((width, rows), LOW),
            jax.ShapeDtypeStruct((heads, HD, rows), WIDE),
            jax.ShapeDtypeStruct((heads, 1, rows), WIDE),
        ],
        compiler_params=pltpu.CompilerParams(vmem_limit_bytes=50 * 2**20),
        cost_estimate=LITTLE,
    )(meta, start, *pieces, gain, weights)


def attend_back_kernel(
    meta_ref, start_ref, x_ref, dh_mine_ref, dh_near_ref, c_own_ref, c_far_ref, c_near_ref,
    gain_ref, wo_ref, qt_ref, q_ref, k_ref, kt_ref, v_ref, ctxt_ref, lse_ref,
    d_ref, dx_ref, dgain_ref, dqkv_ref, dq_all, dk_acc, dv_acc, dh_ref, c_ref,
):
    step = pl.program_id(0)
    heads = qt_ref.shape[0]
    start = start_ref[...]
    key_iota = lax.broadcasted_iota(jnp.int32, (BLOCK, BLOCK), 0)
    query_iota = lax.broadcasted_iota(jnp.int32, (BLOCK, BLOCK), 1)

    @pl.when(step == 0)
    def _():
        dk_acc[...] = jnp.zeros_like(dk_acc)
        dv_acc[...] = jnp.zeros_like(dv_acc)

    spot = spot_of(step ^ meta_ref[0])
    select_piece(spot, (c_own_ref, c_far_ref, c_near_ref), c_ref)

    @pl.when(spot < 2)
    def _():
        dh_ref[...] = dh_mine_ref[...]

    @pl.when(spot >= 2)
    def _():
        dh_ref[...] = dh_near_ref[...]

    normed, rstd = norm_parts(x_ref[...])
    dh = dh_ref[...].astype(WIDE)
    scaled = dh * gain_ref[...]
    mean_plain = jnp.mean(scaled, axis=-1, keepdims=True)
    mean_normed = jnp.mean(scaled * normed, axis=-1, keepdims=True)
    dx = c_ref[...].astype(WIDE) + rstd * (scaled - mean_plain - normed * mean_normed)
    dattn = dx.astype(LOW)
    d_ref[...] = dattn

    @pl.when(step == meta_ref[0])
    def _():
        dx_ref[...] = dx
        dgain_ref[...] = jnp.sum(dh * normed, axis=0, keepdims=True)

    g_all = mm(dattn, wo_ref[:, 3 * heads * HD :]).astype(LOW)
    gt_all = g_all.T
    g = [g_all[:, h * HD : (h + 1) * HD] for h in range(heads)]
    gt = [gt_all[h * HD : (h + 1) * HD] for h in range(heads)]
    delta = [
        jnp.sum(gt[h].astype(WIDE) * ctxt_ref[h], axis=0, keepdims=True) for h in range(heads)
    ]

    def block(j, carry, last):
        base = pl.multiple_of(j * BLOCK, BLOCK)
        rows = pl.ds(base, BLOCK)
        allowed = key_iota + base >= start
        if last:
            allowed = allowed & (key_iota <= query_iota)
        out = []
        for h in range(heads):
            scores = mm(k_ref[h, rows, :], qt_ref[h])
            probs = jnp.where(allowed, jnp.exp(scores - lse_ref[h]), 0.0)
            slopes = mm(v_ref[h, rows, :], gt[h])
            score_grads = (probs * (slopes - delta[h])).astype(LOW)
            dv_acc[h, rows, :] += mm(probs.astype(LOW), g[h])
            dk_acc[h, rows, :] += mm(score_grads, q_ref[h])
            out.append(carry[h] + mm(kt_ref[h, :, rows], score_grads))
        return tuple(out)

    carry = tuple(jnp.zeros((HD, BLOCK), WIDE) for _ in range(heads))
    carry = lax.fori_loop(meta_ref[1 + step], step, lambda j, c: block(j, c, False), carry)
    carry = block(step, carry, True)
    here = pl.ds(pl.multiple_of(step * BLOCK, BLOCK), BLOCK)
    scale = HD**-0.5
    for h in range(heads):
        dq_all[h, here, :] = (carry[h] * scale).T

    @pl.when(step == pl.num_programs(0) - 1)
    def _():
        for n in range(4):
            rows = slice(n * BLOCK, (n + 1) * BLOCK)
            to = pl.ds(pl.multiple_of(spot_of(n ^ meta_ref[0]) * BLOCK, BLOCK), BLOCK)
            dqkv_ref[to, :] = jnp.concatenate(
                [part[h, rows, :] for part in (dq_all, dk_acc, dv_acc) for h in range(heads)],
                axis=1,
            ).astype(LOW)


def attend_back(meta, start, x_one, dh_pieces, c_pieces, gain, weights, qt, q, keys, kt, values, ctxt, lse):
    heads, _, rows = qt.shape
    features = x_one.shape[1]
    spot = lambda i, m: spot_of(i ^ m[0])
    place = lambda i, m: (spot(i, m), 0)

    by_column = pl.BlockSpec((heads, HD, BLOCK), lambda i, m: (0, 0, i))
    by_row = pl.BlockSpec((heads, BLOCK, HD), lambda i, m: (0, i, 0))
    by_place = pl.BlockSpec((BLOCK, features), place)
    whole = lambda *shape: pl.BlockSpec(shape, lambda i, m: (0,) * len(shape))
    grid_spec = pltpu.PrefetchScalarGridSpec(
        num_scalar_prefetch=1,
        grid=(rows // BLOCK,),
        in_specs=[
            pl.BlockSpec((1, BLOCK), lambda i, m: (0, i)),
            by_place,
            pl.BlockSpec((BLOCK, features), lambda i, m: (jnp.minimum(spot(i, m), 1), 0)),
            pl.BlockSpec((BLOCK, features), lambda i, m: (jnp.maximum(spot(i, m) - 2, 0), 0)),
            *piece_specs(BLOCK, features, spot),
            whole(1, features),
            whole(*weights.shape),
            by_column,
            by_row,
            whole(heads, rows, HD),
            whole(heads, HD, rows),
            whole(heads, rows, HD),
            by_column,
            pl.BlockSpec((heads, 1, BLOCK), lambda i, m: (0, 0, i)),
        ],
        out_specs=[
            by_place,
            whole(rows // 4, features),
            whole(1, features),
            whole(rows, 3 * heads * HD),
        ],
        scratch_shapes=[pltpu.VMEM((heads, rows, HD), WIDE)] * 3
        + [pltpu.VMEM((BLOCK, features), LOW)] * 2,
    )
    return pl.pallas_call(
        attend_back_kernel,
        grid_spec=grid_spec,
        out_shape=[
            jax.ShapeDtypeStruct((rows, features), LOW),
            jax.ShapeDtypeStruct((rows // 4, features), WIDE),
            jax.ShapeDtypeStruct((1, features), WIDE),
            jax.ShapeDtypeStruct((rows, 3 * heads * HD), LOW),
        ],
        compiler_params=pltpu.CompilerParams(vmem_limit_bytes=60 * 2**20),
        cost_estimate=LITTLE,
    )(meta, start, x_one, *dh_pieces, *c_pieces, gain, weights, qt, q, keys, kt, values, ctxt, lse)


def hot_rows(placed_ref, line, first, rows):
    spots = lax.broadcasted_iota(jnp.int32, (rows, placed_ref.shape[1]), 0) + first
    hot = (placed_ref[line : line + 1, :] == spots) | (placed_ref[line + 1 : line + 2, :] == spots)
    return jnp.where(hot, 1.0, 0.0).astype(LOW)


def send_kernel(
    index_ref, placed_ref, c_own_ref, c_far_ref, c_near_ref, c_ref, in_order_ref, picks_ref, rows_all
):
    step = pl.program_id(0)
    share = in_order_ref.shape[0]
    size = c_own_ref.shape[0]

    @pl.when(step == 0)
    def _():
        rows_all[:size, :] = c_own_ref[...]
        rows_all[size : 2 * size, :] = c_far_ref[...]
        rows_all[2 * size :, :] = c_near_ref[...]

    hot = hot_rows(placed_ref, 2, step * share, share)
    in_order_ref[...] = hot
    picks_ref[...] = hot
    c_ref[0, :share, :] = mm(hot, rows_all[...]).astype(LOW)
    sums = mm_nt(placed_ref[...].astype(WIDE).astype(LOW), hot)[4:5]
    line = jnp.concatenate(
        [sums, jnp.zeros((1, c_ref.shape[2] - share), WIDE)], axis=1
    ) if c_ref.shape[2] > share else sums
    c_ref[0, share:, :] = jnp.broadcast_to(line, (16, c_ref.shape[2])).astype(LOW)


def send_rows(index, placed, pieces, count, share):
    size, features = pieces[0].shape
    total = 4 * size
    whole = lambda *shape: pl.BlockSpec(shape, lambda p, o: (0,) * len(shape))
    grid_spec = pltpu.PrefetchScalarGridSpec(
        num_scalar_prefetch=1,
        grid=(count,),
        in_specs=[
            whole(*placed.shape),
            whole(size, features),
            whole(size, features),
            whole(2 * size, features),
        ],
        out_specs=[
            pl.BlockSpec((1, share + 16, features), lambda p, o: (p, 0, 0)),
            pl.BlockSpec((share, total), lambda p, o: (p, 0)),
            pl.BlockSpec((share, total), lambda p, o: (p ^ o[0], 0)),
        ],
        scratch_shapes=[pltpu.VMEM((total, features), LOW)],
    )
    return pl.pallas_call(
        send_kernel,
        grid_spec=grid_spec,
        out_shape=[
            jax.ShapeDtypeStruct((count, share + 16, features), LOW),
            jax.ShapeDtypeStruct((count * share, total), LOW),
            jax.ShapeDtypeStruct((count * share, total), LOW),
        ],
        compiler_params=pltpu.CompilerParams(vmem_limit_bytes=40 * 2**20),
        cost_estimate=LITTLE,
    )(index, placed, *pieces)


def halves_kernel(odd_ref, frozen_in_ref, frozen_out_ref, fresh_in_ref, fresh_out_ref, kept_ref, given_ref):
    units = frozen_out_ref.shape[1]

    def store(out, first, second):
        out[:units, :] = first[0].T.astype(LOW)
        out[units:, :] = second[0].astype(LOW)

    @pl.when(odd_ref[0] == 0)
    def _():
        store(kept_ref, frozen_in_ref, frozen_out_ref)
        store(given_ref, fresh_in_ref, fresh_out_ref)

    @pl.when(odd_ref[0] == 1)
    def _():
        store(kept_ref, fresh_in_ref, fresh_out_ref)
        store(given_ref, frozen_in_ref, frozen_out_ref)


def expert_halves(odd, frozen_in, frozen_out, fresh_in, fresh_out):
    _, features, units = frozen_in.shape
    grid_spec = pltpu.PrefetchScalarGridSpec(
        num_scalar_prefetch=1,
        grid=(1,),
        in_specs=[
            pl.BlockSpec(w.shape, lambda p, o: (0, 0, 0))
            for w in (frozen_in, frozen_out, fresh_in, fresh_out)
        ],
        out_specs=[pl.BlockSpec((2 * units, features), lambda p, o: (0, 0))] * 2,
    )
    return pl.pallas_call(
        halves_kernel,
        grid_spec=grid_spec,
        out_shape=[jax.ShapeDtypeStruct((2 * units, features), LOW)] * 2,
        compiler_params=pltpu.CompilerParams(vmem_limit_bytes=40 * 2**20),
        cost_estimate=LITTLE,
    )(odd, frozen_in, frozen_out, fresh_in, fresh_out)


def mix_kernel(count, gain_ref, placed_ref, *refs):
    context_refs, weight_refs, piece_refs = refs[:4], refs[4:8], refs[8:11]
    x_one_ref, taken_refs, x_ref, h_all = refs[11], refs[12 : 12 + count], refs[-2], refs[-1]
    step = pl.program_id(0)
    size = x_ref.shape[0]
    select_piece(step, piece_refs, x_ref)
    attn = mm(context_refs[0][...].T, weight_refs[0][...])
    for n in range(1, 4):
        attn = attn + mm(context_refs[n][...].T, weight_refs[n][...])
    x_one = x_ref[...].astype(WIDE) + attn
    x_one_ref[...] = x_one
    normed, _ = norm_parts(x_one)
    h_all[pl.ds(pl.multiple_of(step * size, size), size), :] = (normed * gain_ref[...]).astype(LOW)

    @pl.when(step == pl.num_programs(0) - 1)
    def _():
        share = taken_refs[0].shape[0]
        for k in range(count):
            hot = hot_rows(placed_ref, 0, k * share, share)
            taken_refs[k][...] = mm(hot, h_all[...]).astype(LOW)


def mix(placed, pieces, gain, contexts, weights, count, share):
    width, rows = contexts[0].shape
    features = gain.shape[1]
    size = rows // 4

    def context_spec(n):
        return pl.BlockSpec((width, size), lambda i: (0, i ^ n))

    def weight_spec(n):
        return pl.BlockSpec((width, features), lambda i: (n // 3, 0))

    return pl.pallas_call(
        functools.partial(mix_kernel, count),
        grid=(4,),
        in_specs=[
            pl.BlockSpec((1, features), lambda i: (0, 0)),
            pl.BlockSpec(placed.shape, lambda i: (0, 0)),
        ]
        + [context_spec(n) for n in range(4)]
        + [weight_spec(n) for n in range(4)]
        + piece_specs(size, features, lambda i: i),
        scratch_shapes=[pltpu.VMEM((size, features), LOW), pltpu.VMEM((rows, features), LOW)],
        out_specs=[pl.BlockSpec((size, features), lambda i: (i, 0))]
        + [pl.BlockSpec((share, features), lambda i: (0, 0))] * count,
        out_shape=[jax.ShapeDtypeStruct((rows, features), WIDE)]
        + [jax.ShapeDtypeStruct((share, features), LOW)] * count,
        compiler_params=pltpu.CompilerParams(vmem_limit_bytes=40 * 2**20),
        cost_estimate=LITTLE,
    )(gain, placed, *contexts, *weights, weights[2], *pieces)


def expert_kernel(count, meta_ref, *refs):
    x_refs, refs = refs[:count], refs[count:]
    c_refs, refs = refs[:count], refs[count:]
    wg_ref, weight_refs = refs[0], refs[1:9]
    refs = refs[-(15 + count) :]
    a_ref, du_ref, xs_ref, dy_ref, mark_ref, y_ref = refs[:6]
    dx_refs, refs = refs[6 : 6 + count], refs[6 + count :]
    cs, w1_all, w2_all, sems, acc, acc_y, dots, others, gate = refs
    step, steps = pl.program_id(0), pl.num_programs(0)
    rows, kinds = xs_ref.shape[0], wg_ref.shape[1]
    share = rows // count
    units = w1_all.shape[1] // 2
    lanes = lax.broadcasted_iota(jnp.int32, (rows, kinds), 1)
    own = meta_ref[0]

    def fetches(n):
        slot = n % 2
        for m in range(2):
            span = slice(m * units, (m + 1) * units)
            for p, target in enumerate((w1_all, w2_all)):
                yield pltpu.make_async_copy(
                    weight_refs[2 * n + m].at[p * units : (p + 1) * units],
                    target.at[slot, span],
                    sems.at[slot, 2 * m + p],
                )

    def kinds_of():
        sums = [
            c_refs[n][0, share : share + 16, : -(-share // 128) * 128].astype(WIDE).T[:share, :1]
            for n in range(count)
        ]
        sums = jnp.concatenate(sums, axis=0).astype(jnp.int32)
        return lanes == own, lanes == sums - own

    @pl.when(step == 0)
    def _():
        for copy in fetches(0):
            copy.start()
        for n in range(count):
            xs_ref[n * share : (n + 1) * share, :] = x_refs[n][...]
            cs[n * share : (n + 1) * share, :] = c_refs[n][0, :share, :]
        logits = mm(xs_ref[...], wg_ref[...].astype(LOW))
        here, there = kinds_of()
        mine = jnp.sum(jnp.where(here, logits, 0.0), axis=1, keepdims=True)
        theirs = jnp.sum(jnp.where(there, logits, 0.0), axis=1, keepdims=True)
        peak = jnp.maximum(mine, theirs)
        mine, theirs = jnp.exp(mine - peak), jnp.exp(theirs - peak)
        gate[...] = mine / (mine + theirs)
        others[...] = theirs / (mine + theirs)
        dy_ref[...] = (gate[...] * cs[...].astype(WIDE)).astype(LOW)
        acc[...] = jnp.zeros_like(acc)
        acc_y[...] = jnp.zeros_like(acc_y)
        dots[...] = jnp.zeros_like(dots)

    for n in range(4):

        @pl.when(step == n)
        def _(n=n):
            if n < 3:
                for copy in fetches(n + 1):
                    copy.start()
            for copy in fetches(n):
                copy.wait()

    w1, w2 = w1_all[step % 2], w2_all[step % 2]
    u = mm_nt(xs_ref[...], w1)
    da = mm_nt(cs[...], w2)
    bell = jnp.exp(u * u * -0.5)
    t = 1.0 / (1.0 + jnp.abs(u) * (ERF_P * ROOT_HALF))
    tail = ERF_C[-1] * t
    for coefficient in ERF_C[-2::-1]:
        tail = (tail + coefficient) * t
    tail = tail * bell
    part = jnp.where(u >= 0.0, 1.0 - tail, tail)
    a = (u * part).astype(LOW)
    slope = part + u * bell * INV_ROOT_TAU
    dots[...] += jnp.sum(a.astype(WIDE) * da, axis=1, keepdims=True)
    du = (gate[...] * da * slope).astype(LOW)
    a_ref[...] = a
    du_ref[...] = du
    acc_y[...] += mm(a, w2)
    acc[...] += mm(du, w1)

    @pl.when(step == steps - 1)
    def _():
        pull = gate[...] * others[...] * dots[...]
        here, there = kinds_of()
        marks = jnp.where(here, pull, 0.0) - jnp.where(there, pull, 0.0)
        mark_ref[...] = marks
        high = marks.astype(LOW)
        rest = (marks - high.astype(WIDE)).astype(LOW)
        gate_low = wg_ref[...].astype(LOW)
        dx = acc[...] + mm_nt(high, gate_low) + mm_nt(rest, gate_low)
        for n in range(count):
            dx_refs[n][...] = dx[n * share : (n + 1) * share].astype(LOW)
        y = (gate[...] * acc_y[...]).astype(LOW)
        for n in range(count):
            base = pl.multiple_of((meta_ref[1] % count ^ n) * share, 16)
            y_ref[pl.ds(base, share), :] = y[n * share : (n + 1) * share]


def run_experts(meta, xs, c, gate_weight, weights, chunk, chunks, held):
    count = len(xs)
    share, features = xs[0].shape
    rows = count * share
    units = weights[0].shape[0]
    kinds = gate_weight.shape[1]
    whole = lambda *shape: pl.BlockSpec(shape, lambda p, o: (0,) * len(shape))
    by_piece = pl.BlockSpec((rows, units), lambda p, o: (chunk, p))
    by_chunk = lambda width: pl.BlockSpec((rows, width), lambda p, o: (chunk, 0))
    anywhere = pl.BlockSpec(memory_space=pl.ANY)

    def c_spec(n):
        return pl.BlockSpec((1,) + c.shape[1:], lambda p, o: (o[1] ^ (chunk * count + n), 0, 0))

    operands = [meta, *xs, *([c] * count), gate_weight, *weights]
    in_specs = (
        [whole(share, features)] * count
        + [c_spec(n) for n in range(count)]
        + [whole(features, kinds)]
        + [anywhere] * 8
    )
    aliases = {}
    if held is not None:
        aliases = {len(operands) + n: n for n in range(6)}
        operands += held
        in_specs += [anywhere] * 6
    every = chunks * rows
    grid_spec = pltpu.PrefetchScalarGridSpec(
        num_scalar_prefetch=1,
        grid=(4,),
        in_specs=in_specs,
        out_specs=[
            by_piece,
            by_piece,
            by_chunk(features),
            by_chunk(features),
            by_chunk(kinds),
            pl.BlockSpec((rows, features), lambda p, o: (o[1] // count ^ chunk, 0)),
            *([whole(share, features)] * count),
        ],
        scratch_shapes=[
            pltpu.VMEM((rows, features), LOW),
            pltpu.VMEM((2, units, features), LOW),
            pltpu.VMEM((2, units, features), LOW),
            pltpu.SemaphoreType.DMA((2, 4)),
            pltpu.VMEM((rows, features), WIDE),
            pltpu.VMEM((rows, features), WIDE),
            pltpu.VMEM((rows, 1), WIDE),
            pltpu.VMEM((rows, 1), WIDE),
            pltpu.VMEM((rows, 1), WIDE),
        ],
    )
    out = pl.pallas_call(
        functools.partial(expert_kernel, count),
        grid_spec=grid_spec,
        out_shape=[
            jax.ShapeDtypeStruct((every, 4 * units), LOW),
            jax.ShapeDtypeStruct((every, 4 * units), LOW),
            jax.ShapeDtypeStruct((every, features), LOW),
            jax.ShapeDtypeStruct((every, features), LOW),
            jax.ShapeDtypeStruct((every, kinds), WIDE),
            jax.ShapeDtypeStruct((every, features), LOW),
            *([jax.ShapeDtypeStruct((share, features), LOW)] * count),
        ],
        input_output_aliases=aliases,
        compiler_params=pltpu.CompilerParams(vmem_limit_bytes=58 * 2**20),
        cost_estimate=LITTLE,
    )(*operands)
    return out[:6], out[6:]


def expert_grads_kernel(a_ref, du_ref, x_ref, dy_ref, give_ref, keep_ref):
    step = pl.program_id(0)
    units = a_ref.shape[1] // 2

    def store(out, kind):
        first = mm_tn(du_ref[...], x_ref[...])
        second = mm_tn(a_ref[...], dy_ref[...])
        for m in range(2):
            span = slice(m * units, (m + 1) * units)
            out[0, m, :units, :] = first[span].astype(kind)
            out[0, m, units:, :] = second[span].astype(kind)

    @pl.when(step < 2)
    def _():
        store(give_ref, LOW)

    @pl.when(step >= 2)
    def _():
        store(keep_ref, WIDE)


def expert_grads(hidden, hidden_grads, x, dy):
    rows, features = x.shape
    units = hidden.shape[1] // 4
    piece = pl.BlockSpec((rows, units), lambda p: (0, p ^ 2))
    all_rows = pl.BlockSpec((rows, features), lambda p: (0, 0))
    shape = (2, 2, units, features)
    return pl.pallas_call(
        expert_grads_kernel,
        grid=(4,),
        in_specs=[piece, piece, all_rows, all_rows],
        out_specs=[
            pl.BlockSpec((1,) + shape[1:], lambda p: (jnp.minimum(p, 1), 0, 0, 0)),
            pl.BlockSpec((1,) + shape[1:], lambda p: (jnp.maximum(p - 2, 0), 0, 0, 0)),
        ],
        out_shape=[jax.ShapeDtypeStruct(shape, LOW), jax.ShapeDtypeStruct(shape, WIDE)],
        compiler_params=pltpu.CompilerParams(vmem_limit_bytes=58 * 2**20),
        cost_estimate=LITTLE,
    )(hidden, hidden_grads, x, dy)


def weight_kernel(
    index_ref, h_ref, dqkv_ref, d_ref, ctx_ref, w_ref, keep_ref, give_ref, dots_ref, acc
):
    step = pl.program_id(0)
    width = dqkv_ref.shape[1]

    @pl.when(step == 0)
    def _():
        acc[...] = jnp.zeros_like(acc)

    acc[:, :width] += mm_tn(h_ref[...], dqkv_ref[...])
    acc[:, width:] += mm_tn(d_ref[...], ctx_ref[...].T)

    @pl.when(step == pl.num_programs(0) - 1)
    def _():
        count, size = 2 * keep_ref.shape[0], keep_ref.shape[1]
        dots_ref[...] = jnp.sum(
            acc[:, :width] * w_ref[:, :width].astype(WIDE), axis=1, keepdims=True
        )
        for n in range(count):
            k = sum(((n >> b) & 1) * (count >> 1 >> b) for b in range(count.bit_length() - 1))
            part = acc[pl.ds(pl.multiple_of((index_ref[0] ^ k) * size, 8), size), :]
            if n < count // 2:
                keep_ref[n] = part
            else:
                give_ref[n - count // 2] = part.astype(LOW)


def weight_grads(index, h_one, dqkv, dattn, context, weights, count):
    rows, features = h_one.shape
    width, narrow = dqkv.shape[1], context.shape[0]
    size = features // count
    by_row = lambda columns: pl.BlockSpec((BLOCK, columns), lambda i, o: (i, 0))
    share = pl.BlockSpec((count // 2, size, width + narrow), lambda i, o: (0, 0, 0))
    grid_spec = pltpu.PrefetchScalarGridSpec(
        num_scalar_prefetch=1,
        grid=(rows // BLOCK,),
        in_specs=[
            by_row(features),
            by_row(width),
            by_row(features),
            pl.BlockSpec((narrow, BLOCK), lambda i, o: (0, i)),
            pl.BlockSpec(weights.shape, lambda i, o: (0, 0)),
        ],
        out_specs=[share, share, pl.BlockSpec((features, 1), lambda i, o: (0, 0))],
        scratch_shapes=[pltpu.VMEM((features, width + narrow), WIDE)],
    )
    return pl.pallas_call(
        weight_kernel,
        grid_spec=grid_spec,
        out_shape=[
            jax.ShapeDtypeStruct((count // 2, size, width + narrow), WIDE),
            jax.ShapeDtypeStruct((count // 2, size, width + narrow), LOW),
            jax.ShapeDtypeStruct((features, 1), WIDE),
        ],
        compiler_params=pltpu.CompilerParams(vmem_limit_bytes=40 * 2**20),
        cost_estimate=LITTLE,
    )(index, h_one, dqkv, dattn, context, weights)


def finish_kernel(keep_ref, near_ref, far_ref, x_ref, gain_ref, dx_ref, out_ref):
    dh = keep_ref[...] + near_ref[...].astype(WIDE) + far_ref[...].astype(WIDE)
    normed, rstd = norm_parts(x_ref[...].astype(WIDE))
    scaled = dh * gain_ref[...]
    mean_plain = jnp.mean(scaled, axis=-1, keepdims=True)
    mean_normed = jnp.mean(scaled * normed, axis=-1, keepdims=True)
    out_ref[...] = dx_ref[...] + rstd * (scaled - mean_plain - normed * mean_normed)


def finish(keep, near, far, x, gain, dx):
    rows, features = x.shape
    size = 256
    by_row = pl.BlockSpec((size, features), lambda i: (i, 0))
    return pl.pallas_call(
        finish_kernel,
        grid=(rows // size,),
        in_specs=[by_row] * 4 + [pl.BlockSpec((1, features), lambda i: (0, 0)), by_row],
        out_specs=by_row,
        out_shape=jax.ShapeDtypeStruct((rows, features), WIDE),
        cost_estimate=LITTLE,
    )(keep, near, far, x, gain, dx)


def flip(array, axis, bits):
    size = lax.axis_size(axis)
    return lax.ppermute(array, axis, [(i, i ^ bits) for i in range(size)])


def flip_head_where(array, bits, odd):
    heads, rest = lax.axis_size("head"), lax.axis_size("dp")
    pairs = [
        (d * heads + h, d * heads + (h ^ bits)) for d in range(odd, rest, 2) for h in range(heads)
    ]
    return lax.ppermute(array, ("dp", "head"), pairs)


def after(value, *others):
    return lax.optimization_barrier((value, *others))[0]


def joined(pieces):
    return jnp.concatenate(pieces, axis=0)


def sum_everywhere(value):
    for axis in ("head", "dp"):
        bits = 1
        while bits < lax.axis_size(axis):
            value = value + flip(value, axis, bits)
            bits *= 2
    return value


def sum_over_dp_scattered(keep, give):
    bits = 1
    while True:
        keep = keep + flip(give, "dp", bits).astype(WIDE)
        count = keep.shape[0]
        if count == 1:
            return keep[0]
        keep, give = keep[: count // 2], keep[count // 2 :].astype(LOW)
        bits *= 2


def split_dot(a, marks):
    high = marks.astype(LOW)
    rest = (marks - high.astype(WIDE)).astype(LOW)
    return mm_tn(a, high) + mm_tn(a, rest)


def body(
    block_input,
    gain_one,
    gain_two,
    qkv_weight,
    out_weight,
    gate_weight,
    frozen_in,
    frozen_out,
    fresh_in,
    fresh_out,
    routes,
    doc_lengths,
    cotangent,
):
    own_rows, features = block_input.shape
    head_count, dp_count = lax.axis_size("head"), lax.axis_size("dp")
    head_index, dp_index = lax.axis_index("head"), lax.axis_index("dp")
    total = own_rows * head_count
    half = total // 2
    kinds = gate_weight.shape[1]
    share = 3 * total // kinds // head_count
    width = qkv_weight.shape[2]
    odd = dp_index % 2
    gain_one, gain_two = gain_one[None], gain_two[None]

    c_far = flip(cotangent, "head", 2)
    c_near = flip(joined([cotangent, c_far]), "head", 1)
    c_pieces = [cotangent, c_far, c_near]
    x_far = flip(after(block_input, c_far), "head", 2)

    piece = jnp.concatenate(
        [qkv_weight[0], qkv_weight[1], qkv_weight[2], out_weight.T], axis=1
    ).astype(LOW)
    weights = lax.all_to_all(
        jnp.broadcast_to(piece[None], (dp_count,) + piece.shape), "dp", 0, 0, tiled=True
    ).reshape(features, 4 * width)

    tokens = jnp.arange(total, dtype=jnp.int32)
    hits = (routes[:, :, None] == jnp.arange(kinds, dtype=jnp.int32)).astype(LOW)
    earlier = (tokens[:, None] > tokens[None, :]).astype(LOW)
    counts = mm(earlier, hits.reshape(total, 2 * kinds)).reshape(total, 2, kinds)
    firsts = jnp.sum(hits[:, 0].astype(WIDE), axis=0)
    counts = counts + jnp.stack([jnp.zeros_like(firsts), firsts])[None]
    slots = jnp.sum(counts * hits.astype(WIDE), axis=2).astype(jnp.int32)
    hosts = routes % (kinds // 2) * 2 + routes // (kinds // 2)
    held_here = slots % head_count == head_index
    near_places = jnp.where(held_here, (hosts ^ dp_index) * share + slots // head_count, -1)
    places = jnp.where(held_here, hosts * share + slots // head_count, -1)
    placed = jnp.concatenate([near_places, places, jnp.sum(routes, axis=1, keepdims=True)], axis=1)
    placed = placed.reshape(head_count, own_rows, 5)
    placed = joined(
        [
            lax.dynamic_index_in_dim(placed, head_index ^ k, 0, keepdims=False)
            for k in (0, 2, 1, 3)
        ]
    ).T
    placed = jnp.pad(placed, ((0, 3), (0, 0)))
    here_dp = dp_index.astype(jnp.int32)[None]

    kept, given = expert_halves(
        odd.astype(jnp.int32)[None], frozen_in, frozen_out, fresh_in, fresh_out
    )

    c_out, in_order, picks = send_rows(here_dp, placed, after(c_pieces, kept), dp_count, share)
    x_far = after(x_far, c_out)
    x_near = flip(joined([block_input, x_far]), "head", 1)
    x_pieces = [block_input, x_far, x_near]
    c_in = lax.all_to_all(c_out, "dp", 0, 0, tiled=True)

    come = flip(after(given, weights), "dp", 1)
    kept_far = flip(after(kept, x_far), "head", 2)

    near_kept = flip(kept, "head", 1)
    out = weights[:, 3 * width :].T
    out_far = flip(out, "head", 2)
    out_near = flip(joined([out, out_far]), "head", 1)

    ends = jnp.cumsum(doc_lengths[0])
    start = jnp.max(jnp.where(tokens[:, None] >= ends[None], ends[None], 0), axis=1)
    meta = jnp.concatenate([head_index[None], start[::BLOCK] // BLOCK]).astype(jnp.int32)
    start = start[None]
    h_one, qt, queries, keys, kt, values, context, context_t, log_totals = attend(
        meta, start, x_pieces, gain_one, weights, width
    )
    near_context = flip(context, "head", 1)
    far_context = flip(after(context, kept_far, out_far, near_kept), "head", 2)
    last_context = flip(far_context, "head", 1)
    come_far = flip(after(come, far_context), "head", 2)
    near_come = flip(come, "head", 1)
    last_kept = flip(kept_far, "head", 1)
    per = dp_count // 4
    x_one, *x_out = mix(
        placed, x_pieces, after(gain_two, c_in, near_come, last_kept),
        [context, far_context, near_context, last_context], [out, out_far, out_near],
        dp_count, share,
    )
    last_come = flip(after(come_far, x_one), "head", 1)
    halves = [kept, come, kept_far, come_far, near_kept, near_come, last_kept, last_come]

    x_parts = [x_out[0]] + [flip(x_out[k], "dp", k) for k in range(1, 3 * per)]
    held, dx_parts = None, []
    own_kind = dp_index // 2 + odd * (kinds // 2)
    expert_meta = jnp.stack([own_kind, dp_index]).astype(jnp.int32)
    for n in range(4):
        ks = range(n * per, (n + 1) * per)
        xs = [x_parts[k] for k in ks]
        if n >= 2:
            xs[0] = after(xs[0], *dx_parts[(n - 2) * per : (n - 1) * per])
        held, dx = run_experts(
            expert_meta, xs, c_in, gate_weight, halves, n, 4, held
        )
        dx_parts += [part if k == 0 else flip(part, "dp", k) for k, part in zip(ks, dx)]
        if n == 0:
            ready = x_parts[2 * per :]
            x_parts += [
                flip(after(x_out[k], dx[0], *ready), "dp", k) for k in range(3 * per, dp_count)
            ]

    hidden, hidden_grads, x_all, dy_all, marks, gated = held
    cut = 2 * per * share
    early = joined(dx_parts[: 2 * per])
    there = mm_tn(picks[:cut, half:], early)
    here = mm_tn(picks[:cut, :half], early)
    give, keep = expert_grads(hidden, hidden_grads, after(x_all, there, here), dy_all)
    late = joined([after(dx_parts[2 * per], give), *dx_parts[2 * per + 1 :]])
    there = (there + mm_tn(picks[cut:, half:], late)).astype(LOW)
    sent = flip(there, "head", 1)
    here = (here + mm_tn(picks[cut:, :half], late) + sent.astype(WIDE)).astype(LOW)
    across = flip(here, "head", 2)

    give = [flip(after(give[:, n], here), "head", 1) for n in (1, 0)]
    leave = [(keep[n, 1] + give[0][n].astype(WIDE)).astype(LOW) for n in (1, 0)]
    gated = after(gated, *leave)
    leave = [flip(part, "dp", 1) for part in leave]
    across = across.astype(WIDE)
    dh_mine = (here.astype(WIDE) + joined([across[own_rows:], across[:own_rows]])).astype(LOW)
    dh_near = flip(dh_mine, "head", 1)
    stay = (keep[1, 0] + give[1][1].astype(WIDE)).astype(LOW)
    crossed = flip_head_where(after(stay, dh_mine), 2, 1) + flip_head_where(after(leave[0], dh_mine), 2, 0)
    home = jnp.where(odd == 1, keep[0, 0] + give[1][0].astype(WIDE), leave[1].astype(WIDE))

    dattn, dx_one, grad_gain_two, dqkv = attend_back(
        meta, start, x_one, [dh_mine, dh_near], c_pieces, gain_two, weights,
        qt, queries, keys, kt, values, context_t, log_totals,
    )
    back = weights[:, : 3 * width]
    keep, give, dots = weight_grads(
        dp_index.astype(jnp.int32)[None], h_one, dqkv, dattn, context, weights, dp_count
    )
    sent = flip(mm_nt(after(dqkv, give)[half:], back).astype(LOW), "head", 1)
    mine = mm_nt(dqkv[:half], back)
    far = flip((mine[own_rows:] + sent[own_rows:].astype(WIDE)).astype(LOW), "head", 2)
    grad_input = finish(mine[:own_rows], sent[:own_rows], far, block_input, gain_one, dx_one)
    grads = sum_over_dp_scattered(keep, give)
    grad_qkv = jnp.stack([grads[:, n * width : (n + 1) * width] for n in range(3)])
    grad_out_weight = grads[:, 3 * width :].T

    gated = lax.all_to_all(
        gated.reshape(dp_count, share, features), "dp", 0, 0, tiled=True
    ).reshape(dp_count * share, features)
    gated = after(gated, mine)
    sent = flip(mm_tn(in_order[:, half:], gated).astype(LOW), "head", 1).astype(WIDE)
    mine = mm_tn(in_order[:, :half], gated) + sent
    mixture = mine[:own_rows] + flip(mine[own_rows:].astype(LOW), "head", 2).astype(WIDE)
    result = (x_one[:own_rows] + mixture).astype(LOW)
    home = home + after(crossed, mine).astype(WIDE)
    units = home.shape[0] // 2
    grad_fresh_in, grad_fresh_out = home[:units].T[None], home[units:][None]
    grad_gate = split_dot(after(x_all, give), marks)
    small = sum_everywhere(joined([dots[:, 0][None] / gain_one, grad_gain_two, grad_gate.T]))
    return (
        result,
        grad_input,
        small[0],
        small[1],
        grad_qkv,
        grad_out_weight,
        small[2:].T,
        grad_fresh_in,
        grad_fresh_out,
    )


def solution(mesh):
    return jax.shard_map(
        body,
        mesh=mesh,
        in_specs=(
            P(("dp", "head"), None),
            P(),
            P(),
            P(None, "dp", "head"),
            P("head", "dp"),
            P(),
            P("dp", None, "head"),
            P("dp", "head", None),
            P("dp", None, "head"),
            P("dp", "head", None),
            P("dp", None),
            P("dp", None),
            P(("dp", "head"), None),
        ),
        out_specs=(
            P(("dp", "head"), None),
            P(("dp", "head"), None),
            P(),
            P(),
            P(None, "dp", "head"),
            P("head", "dp"),
            P(),
            P("dp", None, "head"),
            P("dp", "head", None),
        ),
        check_vma=False,
    )
```

```python
import functools

import jax
import jax.numpy as jnp
from jax import lax
from jax.experimental import pallas as pl
from jax.experimental.pallas import tpu as pltpu
from jax.sharding import PartitionSpec as P

HD = 64
EPS = 1e-05
MASKED = -1000000000.0
ROOT_HALF = 0.7071067811865476
INV_ROOT_TAU = 0.3989422804014327
BLOCK = 512
LOW = jnp.bfloat16
WIDE = jnp.float32
LITTLE = pl.CostEstimate(flops=10**6, bytes_accessed=10**5, transcendentals=0)
NT = (((1,), (1,)), ((), ()))
TN = (((0,), (0,)), ((), ()))
ERF_P = 0.4
ERF_C = (
    0.11596113048765463,
    0.08091125192311208,
    0.23413842084756234,
    -0.1854556415158047,
    0.35457470270248115,
    -0.10012987827403336,
)


def mm(a, b):
    return jnp.dot(a, b, preferred_element_type=WIDE)


def mm_nt(a, b):
    return lax.dot_general(a, b, NT, preferred_element_type=WIDE)


def mm_tn(a, b):
    return lax.dot_general(a, b, TN, preferred_element_type=WIDE)


def spot_of(k):
    return (k % 2) * 2 + k // 2


def select_piece(spot, refs, out):
    for n, ref in enumerate(refs):

        @pl.when(spot == n)
        def _(ref=ref):
            out[...] = ref[...]


def piece_specs(rows, features):
    return [pl.BlockSpec((rows, features), lambda *i: (0, 0))] * 4


def norm_parts(values):
    centred = values - jnp.mean(values, axis=-1, keepdims=True)
    rstd = lax.rsqrt(jnp.mean(centred * centred, axis=-1, keepdims=True) + EPS)
    return centred * rstd, rstd


def attend_kernel(
    meta_ref, start_ref, x_0_ref, x_1_ref, x_2_ref, x_3_ref, gain_ref, w_ref,
    h_ref, qt_ref, q_ref, k_ref, kt_ref, v_ref, ctx_ref, ctxt_ref, lse_ref, k_all, vt_all, x_ref,
):
    step = pl.program_id(0)
    heads = qt_ref.shape[0]
    width = heads * HD
    start = start_ref[...]
    key_iota = lax.broadcasted_iota(jnp.int32, (BLOCK, BLOCK), 0)
    query_iota = lax.broadcasted_iota(jnp.int32, (BLOCK, BLOCK), 1)

    select_piece(spot_of(step ^ meta_ref[0]), (x_0_ref, x_1_ref, x_2_ref, x_3_ref), x_ref)
    normed, _ = norm_parts(x_ref[...].astype(WIDE))
    h_one = (normed * gain_ref[...]).astype(LOW)
    h_ref[...] = h_one
    here = pl.ds(pl.multiple_of(step * BLOCK, BLOCK), BLOCK)
    q = mm(h_one, w_ref[:, :width]).astype(LOW) * (HD**-0.5)
    k = mm(h_one, w_ref[:, width : 2 * width]).astype(LOW)
    v = mm(h_one, w_ref[:, 2 * width : 3 * width]).astype(LOW)
    q = q.astype(LOW)
    q_t, k_t, v_t = q.T, k.T, v.T
    for h in range(heads):
        rows = slice(h * HD, (h + 1) * HD)
        qt_ref[h] = q_t[rows]
        q_ref[h] = q[:, rows]
        kt_ref[h] = k_t[rows]
        k_ref[h] = k[:, rows]
        k_all[h, here, :] = k[:, rows]
        v_ref[h] = v[:, rows]
        vt_all[h, :, here] = v_t[rows]

    def block(j, carry, last):
        base = pl.multiple_of(j * BLOCK, BLOCK)
        allowed = key_iota + base >= start
        if last:
            allowed = allowed & (key_iota <= query_iota)
        out = []
        for h in range(heads):
            top, total, acc = carry[h]
            scores = mm(k_all[h, pl.ds(base, BLOCK), :], qt_ref[h])
            scores = jnp.where(allowed, scores, MASKED)
            peak = jnp.maximum(top, jnp.max(scores, axis=0, keepdims=True))
            raised = jnp.exp(scores - peak)
            fade = jnp.exp(top - peak)
            total = total * fade + jnp.sum(raised, axis=0, keepdims=True)
            acc = acc * fade + mm(vt_all[h, :, pl.ds(base, BLOCK)], raised.astype(LOW))
            out.append((peak, total, acc))
        return tuple(out)

    carry = tuple(
        (
            jnp.full((1, BLOCK), MASKED, WIDE),
            jnp.zeros((1, BLOCK), WIDE),
            jnp.zeros((HD, BLOCK), WIDE),
        )
        for _ in range(heads)
    )
    carry = lax.fori_loop(meta_ref[1 + step], step, lambda j, c: block(j, c, False), carry)
    carry = block(step, carry, True)
    for h in range(heads):
        top, total, acc = carry[h]
        acc = acc / total
        ctxt_ref[h] = acc
        lse_ref[h] = top + jnp.log(total)
        ctx_ref[h * HD : (h + 1) * HD, :] = acc.astype(LOW)


def attend(meta, start, pieces, gain, weights, width):
    features = gain.shape[1]
    rows = 4 * BLOCK
    heads = width // HD
    spot = lambda i, m: spot_of(i ^ m[0])
    place = lambda i, m: (spot(i, m), 0)

    by_column = pl.BlockSpec((heads, HD, BLOCK), lambda i, m: (0, 0, i))
    by_row = pl.BlockSpec((heads, BLOCK, HD), lambda i, m: (0, i, 0))
    grid_spec = pltpu.PrefetchScalarGridSpec(
        num_scalar_prefetch=1,
        grid=(rows // BLOCK,),
        in_specs=[
            pl.BlockSpec((1, BLOCK), lambda i, m: (0, i)),
            *piece_specs(BLOCK, features),
            pl.BlockSpec((1, features), lambda i, m: (0, 0)),
            pl.BlockSpec(weights.shape, lambda i, m: (0, 0)),
        ],
        out_specs=[
            pl.BlockSpec((BLOCK, features), place),
            by_column,
            by_row,
            by_row,
            by_column,
            by_row,
            pl.BlockSpec((width, BLOCK), lambda i, m: (0, spot(i, m))),
            by_column,
            pl.BlockSpec((heads, 1, BLOCK), lambda i, m: (0, 0, i)),
        ],
        scratch_shapes=[
            pltpu.VMEM((heads, rows, HD), LOW),
            pltpu.VMEM((heads, HD, rows), LOW),
            pltpu.VMEM((BLOCK, features), LOW),
        ],
    )
    tall = jax.ShapeDtypeStruct((heads, rows, HD), LOW)
    flat = jax.ShapeDtypeStruct((heads, HD, rows), LOW)
    return pl.pallas_call(
        attend_kernel,
        grid_spec=grid_spec,
        out_shape=[
            jax.ShapeDtypeStruct((rows, features), LOW),
            flat,
            tall,
            tall,
            flat,
            tall,
            jax.ShapeDtypeStruct((width, rows), LOW),
            jax.ShapeDtypeStruct((heads, HD, rows), WIDE),
            jax.ShapeDtypeStruct((heads, 1, rows), WIDE),
        ],
        compiler_params=pltpu.CompilerParams(vmem_limit_bytes=50 * 2**20),
        cost_estimate=LITTLE,
    )(meta, start, *pieces, gain, weights)


def attend_back_kernel(
    meta_ref, start_ref, x_ref, dh_mine_ref, dh_near_ref, c_0_ref, c_1_ref, c_2_ref, c_3_ref,
    gain_ref, w_ref, qt_ref, q_ref, k_ref, kt_ref, v_ref, ctxt_ref, lse_ref, h_ref, ctx_ref,
    dx_ref, dgain_ref, send_ref, mine_ref, keep_ref, give_ref, dots_ref,
    dk_acc, dv_acc, dh_ref, c_ref, dqkv, d_all, acc,
):
    step = pl.program_id(0)
    heads = qt_ref.shape[0]
    width = heads * HD

    @pl.when(step == 0)
    def _():
        dk_acc[...] = jnp.zeros_like(dk_acc)
        dv_acc[...] = jnp.zeros_like(dv_acc)
        acc[...] = jnp.zeros_like(acc)

    def place(piece):
        return pl.ds(pl.multiple_of(spot_of(piece ^ meta_ref[0]) * BLOCK, BLOCK), BLOCK)

    @pl.when(step < 4)
    def _():
        start = start_ref[...]
        key_iota = lax.broadcasted_iota(jnp.int32, (BLOCK, BLOCK), 0)
        query_iota = lax.broadcasted_iota(jnp.int32, (BLOCK, BLOCK), 1)
        spot = spot_of(step ^ meta_ref[0])
        select_piece(spot, (c_0_ref, c_1_ref, c_2_ref, c_3_ref), c_ref)

        @pl.when(spot < 2)
        def _():
            dh_ref[...] = dh_mine_ref[...]

        @pl.when(spot >= 2)
        def _():
            dh_ref[...] = dh_near_ref[...]

        normed, rstd = norm_parts(x_ref[...])
        dh = dh_ref[...].astype(WIDE)
        scaled = dh * gain_ref[...]
        mean_plain = jnp.mean(scaled, axis=-1, keepdims=True)
        mean_normed = jnp.mean(scaled * normed, axis=-1, keepdims=True)
        dx = c_ref[...].astype(WIDE) + rstd * (scaled - mean_plain - normed * mean_normed)
        dattn = dx.astype(LOW)
        d_all[place(step), :] = dattn

        @pl.when(step == meta_ref[0])
        def _():
            dx_ref[...] = dx
            dgain_ref[...] = jnp.sum(dh * normed, axis=0, keepdims=True)

        g_all = mm(dattn, w_ref[:, 3 * width :]).astype(LOW)
        gt_all = g_all.T
        g = [g_all[:, h * HD : (h + 1) * HD] for h in range(heads)]
        gt = [gt_all[h * HD : (h + 1) * HD] for h in range(heads)]
        delta = [
            jnp.sum(gt[h].astype(WIDE) * ctxt_ref[h], axis=0, keepdims=True)
            for h in range(heads)
        ]

        def block(j, carry, last):
            base = pl.multiple_of(j * BLOCK, BLOCK)
            rows = pl.ds(base, BLOCK)
            allowed = key_iota + base >= start
            if last:
                allowed = allowed & (key_iota <= query_iota)
            out = []
            for h in range(heads):
                scores = mm(k_ref[h, rows, :], qt_ref[h])
                probs = jnp.where(allowed, jnp.exp(scores - lse_ref[h]), 0.0)
                slopes = mm(v_ref[h, rows, :], gt[h])
                score_grads = (probs * (slopes - delta[h])).astype(LOW)
                dv_acc[h, rows, :] += mm(probs.astype(LOW), g[h])
                dk_acc[h, rows, :] += mm(score_grads, q_ref[h])
                out.append(carry[h] + mm(kt_ref[h, :, rows], score_grads))
            return tuple(out)

        carry = tuple(jnp.zeros((HD, BLOCK), WIDE) for _ in range(heads))
        carry = lax.fori_loop(meta_ref[1 + step], step, lambda j, c: block(j, c, False), carry)
        carry = block(step, carry, True)
        scale = HD**-0.5
        dqkv[place(step), :width] = jnp.concatenate(
            [(c * scale).T for c in carry], axis=1
        ).astype(LOW)

    @pl.when(step == 3)
    def _():
        for n in range(4):
            rows = slice(n * BLOCK, (n + 1) * BLOCK)
            dqkv[place(n), width:] = jnp.concatenate(
                [part[h, rows, :] for part in (dk_acc, dv_acc) for h in range(heads)], axis=1
            ).astype(LOW)

    def rest(out, kind):
        rows = pl.ds(pl.multiple_of(((step - 4) ^ 2) * BLOCK, BLOCK), BLOCK)
        grads = dqkv[rows, :]
        out[...] = mm_nt(grads, w_ref[:, : 3 * width]).astype(kind)
        acc[:, : 3 * width] += mm_tn(h_ref[...], grads)
        acc[:, 3 * width :] += mm_tn(d_all[rows, :], ctx_ref[...].T)

    @pl.when((step == 4) | (step == 5))
    def _():
        rest(send_ref, LOW)

    @pl.when(step >= 6)
    def _():
        rest(mine_ref, WIDE)

    @pl.when(step == 7)
    def _():
        dots_ref[...] = jnp.sum(
            acc[:, : 3 * width] * w_ref[:, : 3 * width].astype(WIDE), axis=1, keepdims=True
        )
        count, size = 2 * keep_ref.shape[0], keep_ref.shape[1]
        for n in range(count):
            k = sum(((n >> b) & 1) * (count >> 1 >> b) for b in range(count.bit_length() - 1))
            part = acc[pl.ds(pl.multiple_of((meta_ref[5] ^ k) * size, 8), size), :]
            if n < count // 2:
                keep_ref[n] = part
            else:
                give_ref[n - count // 2] = part.astype(LOW)


def attend_back(
    meta, start, x_one, dh_pieces, c_pieces, gain, weights,
    qt, q, keys, kt, values, ctxt, lse, h_one, context, count,
):
    heads, _, rows = qt.shape
    features = x_one.shape[1]
    every = weights.shape[1]
    low = lambda i: jnp.minimum(i, 3)
    high = lambda i: jnp.maximum(i - 4, 0) ^ 2
    spot = lambda i, m: spot_of(low(i) ^ m[0])
    once = pl.Buffered(1)
    by_column = pl.BlockSpec((heads, HD, BLOCK), lambda i, m: (0, 0, low(i)))
    by_row = pl.BlockSpec((heads, BLOCK, HD), lambda i, m: (0, low(i), 0))

    def whole(*shape):
        return pl.BlockSpec(shape, lambda i, m: (0,) * len(shape), pipeline_mode=once)

    def out(*shape):
        return pl.BlockSpec(shape, lambda i, m: (0,) * len(shape))

    share = (count // 2, features // count, every)
    grid_spec = pltpu.PrefetchScalarGridSpec(
        num_scalar_prefetch=1,
        grid=(8,),
        in_specs=[
            pl.BlockSpec((1, BLOCK), lambda i, m: (0, low(i))),
            pl.BlockSpec((BLOCK, features), lambda i, m: (spot(i, m), 0)),
            pl.BlockSpec((BLOCK, features), lambda i, m: (jnp.minimum(spot(i, m), 1), 0)),
            pl.BlockSpec((BLOCK, features), lambda i, m: (jnp.maximum(spot(i, m) - 2, 0), 0)),
            *([whole(BLOCK, features)] * 4),
            whole(1, features),
            whole(*weights.shape),
            by_column,
            by_row,
            whole(heads, rows, HD),
            whole(heads, HD, rows),
            whole(heads, rows, HD),
            by_column,
            pl.BlockSpec((heads, 1, BLOCK), lambda i, m: (0, 0, low(i))),
            pl.BlockSpec((BLOCK, features), lambda i, m: (high(i), 0)),
            pl.BlockSpec((heads * HD, BLOCK), lambda i, m: (0, high(i))),
        ],
        out_specs=[
            out(BLOCK, features),
            out(1, features),
            pl.BlockSpec((BLOCK, features), lambda i, m: (jnp.clip(i - 4, 0, 1), 0)),
            pl.BlockSpec((BLOCK, features), lambda i, m: (jnp.clip(i - 6, 0, 1), 0)),
            out(*share),
            out(*share),
            out(features, 1),
        ],
        scratch_shapes=[pltpu.VMEM((heads, rows, HD), WIDE)] * 2
        + [pltpu.VMEM((BLOCK, features), LOW)] * 2
        + [
            pltpu.VMEM((rows, 3 * heads * HD), LOW),
            pltpu.VMEM((rows, features), LOW),
            pltpu.VMEM((features, every), WIDE),
        ],
    )
    return pl.pallas_call(
        attend_back_kernel,
        grid_spec=grid_spec,
        out_shape=[
            jax.ShapeDtypeStruct((BLOCK, features), WIDE),
            jax.ShapeDtypeStruct((1, features), WIDE),
            jax.ShapeDtypeStruct((2 * BLOCK, features), LOW),
            jax.ShapeDtypeStruct((2 * BLOCK, features), WIDE),
            jax.ShapeDtypeStruct(share, WIDE),
            jax.ShapeDtypeStruct(share, LOW),
            jax.ShapeDtypeStruct((features, 1), WIDE),
        ],
        compiler_params=pltpu.CompilerParams(vmem_limit_bytes=61 * 2**20),
        cost_estimate=LITTLE,
    )(
        meta, start, x_one, *dh_pieces, *c_pieces, gain, weights,
        qt, q, keys, kt, values, ctxt, lse, h_one, context,
    )


def hot_rows(placed_ref, line, first, rows):
    spots = lax.broadcasted_iota(jnp.int32, (rows, placed_ref.shape[1]), 0) + first
    hot = (placed_ref[line : line + 1, :] == spots) | (placed_ref[line + 1 : line + 2, :] == spots)
    return jnp.where(hot, 1.0, 0.0).astype(LOW)


def send_kernel(
    index_ref, placed_ref, c_0_ref, c_1_ref, c_2_ref, c_3_ref, c_ref, in_order_ref, picks_ref, rows_all
):
    step = pl.program_id(0)
    share = in_order_ref.shape[0]
    size = c_0_ref.shape[0]

    @pl.when(step == 0)
    def _():
        for n, ref in enumerate((c_0_ref, c_1_ref, c_2_ref, c_3_ref)):
            rows_all[n * size : (n + 1) * size, :] = ref[...]

    hot = hot_rows(placed_ref, 2, step * share, share)
    in_order_ref[...] = hot
    picks_ref[...] = hot
    c_ref[0, :share, :] = mm(hot, rows_all[...]).astype(LOW)
    sums = mm_nt(placed_ref[...].astype(WIDE).astype(LOW), hot)[4:5]
    line = jnp.concatenate(
        [sums, jnp.zeros((1, c_ref.shape[2] - share), WIDE)], axis=1
    ) if c_ref.shape[2] > share else sums
    c_ref[0, share:, :] = jnp.broadcast_to(line, (16, c_ref.shape[2])).astype(LOW)


def send_rows(index, placed, pieces, count, share):
    size, features = pieces[0].shape
    total = 4 * size
    whole = lambda *shape: pl.BlockSpec(shape, lambda p, o: (0,) * len(shape))
    grid_spec = pltpu.PrefetchScalarGridSpec(
        num_scalar_prefetch=1,
        grid=(count,),
        in_specs=[
            whole(*placed.shape),
            *([whole(size, features)] * 4),
        ],
        out_specs=[
            pl.BlockSpec((1, share + 16, features), lambda p, o: (p, 0, 0)),
            pl.BlockSpec((share, total), lambda p, o: (p, 0)),
            pl.BlockSpec((share, total), lambda p, o: (p ^ o[0], 0)),
        ],
        scratch_shapes=[pltpu.VMEM((total, features), LOW)],
    )
    return pl.pallas_call(
        send_kernel,
        grid_spec=grid_spec,
        out_shape=[
            jax.ShapeDtypeStruct((count, share + 16, features), LOW),
            jax.ShapeDtypeStruct((count * share, total), LOW),
            jax.ShapeDtypeStruct((count * share, total), LOW),
        ],
        compiler_params=pltpu.CompilerParams(vmem_limit_bytes=40 * 2**20),
        cost_estimate=pl.CostEstimate(flops=4 * 10**10, bytes_accessed=10**7, transcendentals=0),
    )(index, placed, *pieces)


def halves_kernel(odd_ref, frozen_in_ref, frozen_out_ref, fresh_in_ref, fresh_out_ref, kept_ref, given_ref):
    units = frozen_out_ref.shape[1]

    def store(out, first, second):
        out[:units, :] = first[0].T.astype(LOW)
        out[units:, :] = second[0].astype(LOW)

    @pl.when(odd_ref[0] == 0)
    def _():
        store(kept_ref, frozen_in_ref, frozen_out_ref)
        store(given_ref, fresh_in_ref, fresh_out_ref)

    @pl.when(odd_ref[0] == 1)
    def _():
        store(kept_ref, fresh_in_ref, fresh_out_ref)
        store(given_ref, frozen_in_ref, frozen_out_ref)


def expert_halves(odd, frozen_in, frozen_out, fresh_in, fresh_out):
    _, features, units = frozen_in.shape
    grid_spec = pltpu.PrefetchScalarGridSpec(
        num_scalar_prefetch=1,
        grid=(1,),
        in_specs=[
            pl.BlockSpec(w.shape, lambda p, o: (0, 0, 0))
            for w in (frozen_in, frozen_out, fresh_in, fresh_out)
        ],
        out_specs=[pl.BlockSpec((2 * units, features), lambda p, o: (0, 0))] * 2,
    )
    return pl.pallas_call(
        halves_kernel,
        grid_spec=grid_spec,
        out_shape=[jax.ShapeDtypeStruct((2 * units, features), LOW)] * 2,
        compiler_params=pltpu.CompilerParams(vmem_limit_bytes=40 * 2**20),
        cost_estimate=LITTLE,
    )(odd, frozen_in, frozen_out, fresh_in, fresh_out)


def mix_kernel(count, gain_ref, placed_ref, *refs):
    context_refs, weight_refs, piece_refs = refs[:4], refs[4:8], refs[8:12]
    x_one_ref, taken_refs, x_ref, h_all = refs[12], refs[13 : 13 + count], refs[-2], refs[-1]
    step = pl.program_id(0)
    size = x_ref.shape[0]
    select_piece(step, piece_refs, x_ref)
    attn = mm_nt(context_refs[0][...].T, weight_refs[0][...])
    for n in range(1, 4):
        attn = attn + mm_nt(context_refs[n][...].T, weight_refs[n][...])
    x_one = x_ref[...].astype(WIDE) + attn
    x_one_ref[...] = x_one
    normed, _ = norm_parts(x_one)
    h_all[pl.ds(pl.multiple_of(step * size, size), size), :] = (normed * gain_ref[...]).astype(LOW)

    @pl.when(step == pl.num_programs(0) - 1)
    def _():
        share = taken_refs[0].shape[0]
        for k in range(count):
            hot = hot_rows(placed_ref, 0, k * share, share)
            taken_refs[k][...] = mm(hot, h_all[...]).astype(LOW)


def mix(placed, pieces, gain, contexts, weights, count, share):
    width, rows = contexts[0].shape
    features = gain.shape[1]
    size = rows // 4

    def context_spec(n):
        return pl.BlockSpec((width, size), lambda i: (0, i ^ n))

    return pl.pallas_call(
        functools.partial(mix_kernel, count),
        grid=(4,),
        in_specs=[
            pl.BlockSpec((1, features), lambda i: (0, 0)),
            pl.BlockSpec(placed.shape, lambda i: (0, 0)),
        ]
        + [context_spec(n) for n in range(4)]
        + [pl.BlockSpec((features, width), lambda i: (0, 0))] * 4
        + piece_specs(size, features),
        scratch_shapes=[pltpu.VMEM((size, features), LOW), pltpu.VMEM((rows, features), LOW)],
        out_specs=[pl.BlockSpec((size, features), lambda i: (i, 0))]
        + [pl.BlockSpec((share, features), lambda i: (0, 0))] * count,
        out_shape=[jax.ShapeDtypeStruct((rows, features), WIDE)]
        + [jax.ShapeDtypeStruct((share, features), LOW)] * count,
        compiler_params=pltpu.CompilerParams(vmem_limit_bytes=60 * 2**20),
        cost_estimate=LITTLE,
    )(gain, placed, *contexts, *weights, *pieces)


def expert_kernel(count, meta_ref, *refs):
    x_refs, refs = refs[:count], refs[count:]
    c_refs, refs = refs[:count], refs[count:]
    wg_ref, weight_refs = refs[0], refs[1:9]
    refs = refs[-(15 + count) :]
    a_ref, du_ref, xs_ref, dy_ref, mark_ref, y_ref = refs[:6]
    dx_refs, refs = refs[6 : 6 + count], refs[6 + count :]
    cs, w1_all, w2_all, sems, acc, acc_y, dots, others, gate = refs
    step, steps = pl.program_id(0), pl.num_programs(0)
    rows, kinds = xs_ref.shape[0], wg_ref.shape[0]
    share = rows // count
    units = w1_all.shape[1] // 2
    lanes = lax.broadcasted_iota(jnp.int32, (rows, kinds), 1)
    own = meta_ref[6]

    def fetches(n):
        slot = n % 2
        for m in range(2):
            span = slice(m * units, (m + 1) * units)
            for p, target in enumerate((w1_all, w2_all)):
                yield pltpu.make_async_copy(
                    weight_refs[2 * n + m].at[p * units : (p + 1) * units],
                    target.at[slot, span],
                    sems.at[slot, 2 * m + p],
                )

    def kinds_of():
        sums = [
            c_refs[n][0, share : share + 16, : -(-share // 128) * 128].astype(WIDE).T[:share, :1]
            for n in range(count)
        ]
        sums = jnp.concatenate(sums, axis=0).astype(jnp.int32)
        return lanes == own, lanes == sums - own

    @pl.when(step == 0)
    def _():
        for copy in fetches(0):
            copy.start()
        for n in range(count):
            xs_ref[n * share : (n + 1) * share, :] = x_refs[n][...]
            cs[n * share : (n + 1) * share, :] = c_refs[n][0, :share, :]
        logits = mm_nt(xs_ref[...], wg_ref[...].astype(LOW))
        here, there = kinds_of()
        mine = jnp.sum(jnp.where(here, logits, 0.0), axis=1, keepdims=True)
        theirs = jnp.sum(jnp.where(there, logits, 0.0), axis=1, keepdims=True)
        peak = jnp.maximum(mine, theirs)
        mine, theirs = jnp.exp(mine - peak), jnp.exp(theirs - peak)
        gate[...] = mine / (mine + theirs)
        others[...] = theirs / (mine + theirs)
        dy_ref[...] = (gate[...] * cs[...].astype(WIDE)).astype(LOW)
        acc[...] = jnp.zeros_like(acc)
        acc_y[...] = jnp.zeros_like(acc_y)
        dots[...] = jnp.zeros_like(dots)

    for n in range(4):

        @pl.when(step == n)
        def _(n=n):
            if n < 3:
                for copy in fetches(n + 1):
                    copy.start()
            for copy in fetches(n):
                copy.wait()

    w1, w2 = w1_all[step % 2], w2_all[step % 2]
    u = mm_nt(xs_ref[...], w1)
    da = mm_nt(cs[...], w2)
    bell = jnp.exp(u * u * -0.5)
    t = 1.0 / (1.0 + jnp.abs(u) * (ERF_P * ROOT_HALF))
    tail = ERF_C[-1] * t
    for coefficient in ERF_C[-2::-1]:
        tail = (tail + coefficient) * t
    tail = tail * bell
    part = jnp.where(u >= 0.0, 1.0 - tail, tail)
    a = (u * part).astype(LOW)
    slope = part + u * bell * INV_ROOT_TAU
    dots[...] += jnp.sum(a.astype(WIDE) * da, axis=1, keepdims=True)
    du = (gate[...] * da * slope).astype(LOW)
    a_ref[...] = a
    du_ref[...] = du
    acc_y[...] += mm(a, w2)
    acc[...] += mm(du, w1)

    @pl.when(step == steps - 1)
    def _():
        pull = gate[...] * others[...] * dots[...]
        here, there = kinds_of()
        marks = jnp.where(here, pull, 0.0) - jnp.where(there, pull, 0.0)
        mark_ref[...] = marks
        high = marks.astype(LOW)
        rest = (marks - high.astype(WIDE)).astype(LOW)
        gate_low = wg_ref[...].astype(LOW)
        dx = acc[...] + mm(high, gate_low) + mm(rest, gate_low)
        for n in range(count):
            dx_refs[n][...] = dx[n * share : (n + 1) * share].astype(LOW)
        y = (gate[...] * acc_y[...]).astype(LOW)
        for n in range(count):
            base = pl.multiple_of((meta_ref[5] % count ^ n) * share, 16)
            y_ref[pl.ds(base, share), :] = y[n * share : (n + 1) * share]


def run_experts(meta, xs, c, gate_weight, weights, chunk, chunks, held):
    count = len(xs)
    share, features = xs[0].shape
    rows = count * share
    units = weights[0].shape[0]
    kinds = gate_weight.shape[0]
    whole = lambda *shape: pl.BlockSpec(shape, lambda p, o: (0,) * len(shape))
    by_piece = pl.BlockSpec((rows, units), lambda p, o: (chunk, p))
    by_chunk = lambda width: pl.BlockSpec((rows, width), lambda p, o: (chunk, 0))
    anywhere = pl.BlockSpec(memory_space=pl.ANY)

    def c_spec(n):
        return pl.BlockSpec((1,) + c.shape[1:], lambda p, o: (o[5] ^ (chunk * count + n), 0, 0))

    operands = [meta, *xs, *([c] * count), gate_weight, *weights]
    in_specs = (
        [whole(share, features)] * count
        + [c_spec(n) for n in range(count)]
        + [whole(kinds, features)]
        + [anywhere] * 8
    )
    aliases = {}
    if held is not None:
        aliases = {len(operands) + n: n for n in range(6)}
        operands += held
        in_specs += [anywhere] * 6
    every = chunks * rows
    grid_spec = pltpu.PrefetchScalarGridSpec(
        num_scalar_prefetch=1,
        grid=(4,),
        in_specs=in_specs,
        out_specs=[
            by_piece,
            by_piece,
            by_chunk(features),
            by_chunk(features),
            by_chunk(kinds),
            pl.BlockSpec((rows, features), lambda p, o: (o[5] // count ^ chunk, 0)),
            *([whole(share, features)] * count),
        ],
        scratch_shapes=[
            pltpu.VMEM((rows, features), LOW),
            pltpu.VMEM((2, units, features), LOW),
            pltpu.VMEM((2, units, features), LOW),
            pltpu.SemaphoreType.DMA((2, 4)),
            pltpu.VMEM((rows, features), WIDE),
            pltpu.VMEM((rows, features), WIDE),
            pltpu.VMEM((rows, 1), WIDE),
            pltpu.VMEM((rows, 1), WIDE),
            pltpu.VMEM((rows, 1), WIDE),
        ],
    )
    out = pl.pallas_call(
        functools.partial(expert_kernel, count),
        grid_spec=grid_spec,
        out_shape=[
            jax.ShapeDtypeStruct((every, 4 * units), LOW),
            jax.ShapeDtypeStruct((every, 4 * units), LOW),
            jax.ShapeDtypeStruct((every, features), LOW),
            jax.ShapeDtypeStruct((every, features), LOW),
            jax.ShapeDtypeStruct((every, kinds), WIDE),
            jax.ShapeDtypeStruct((every, features), LOW),
            *([jax.ShapeDtypeStruct((share, features), LOW)] * count),
        ],
        input_output_aliases=aliases,
        compiler_params=pltpu.CompilerParams(vmem_limit_bytes=58 * 2**20),
        cost_estimate=LITTLE,
    )(*operands)
    return out[:6], out[6:]


def expert_grads_kernel(a_ref, du_ref, x_ref, dy_ref, marks_ref, *refs):
    give_refs, (keep_ref, gate_ref) = refs[:4], refs[4:]
    step = pl.program_id(0)

    @pl.when(step == 0)
    def _():
        high = marks_ref[...].astype(LOW)
        rest = (marks_ref[...] - high.astype(WIDE)).astype(LOW)
        gate_ref[...] = mm_tn(x_ref[...], high) + mm_tn(x_ref[...], rest)

    units = a_ref.shape[1] // 2

    def store(outs, kind):
        first = mm_tn(du_ref[...], x_ref[...])
        second = mm_tn(a_ref[...], dy_ref[...])
        for m, out in enumerate(outs):
            span = slice(m * units, (m + 1) * units)
            out[:units, :] = first[span].astype(kind)
            out[units:, :] = second[span].astype(kind)

    for n in range(2):

        @pl.when(step == n)
        def _(n=n):
            store(give_refs[2 * n : 2 * n + 2], LOW)

    @pl.when(step >= 2)
    def _():
        store((keep_ref.at[0, 0], keep_ref.at[0, 1]), WIDE)


def expert_grads(hidden, hidden_grads, x, dy, marks):
    rows, features = x.shape
    units = hidden.shape[1] // 4
    piece = pl.BlockSpec((rows, units), lambda p: (0, p ^ 2))
    all_rows = pl.BlockSpec((rows, features), lambda p: (0, 0))
    shape = (2, 2, units, features)
    return pl.pallas_call(
        expert_grads_kernel,
        grid=(4,),
        in_specs=[piece, piece, all_rows, all_rows, pl.BlockSpec(marks.shape, lambda p: (0, 0))],
        out_specs=[
            *([pl.BlockSpec(shape[2:], lambda p: (0, 0))] * 4),
            pl.BlockSpec((1,) + shape[1:], lambda p: (jnp.maximum(p - 2, 0), 0, 0, 0)),
            pl.BlockSpec((features, marks.shape[1]), lambda p: (0, 0)),
        ],
        out_shape=[
            *([jax.ShapeDtypeStruct(shape[2:], LOW)] * 4),
            jax.ShapeDtypeStruct(shape, WIDE),
            jax.ShapeDtypeStruct((features, marks.shape[1]), WIDE),
        ],
        compiler_params=pltpu.CompilerParams(vmem_limit_bytes=58 * 2**20),
        cost_estimate=LITTLE,
    )(hidden, hidden_grads, x, dy, marks)


def leave_kernel(keep_ref, give_0_ref, give_1_ref, out_ref):
    for n, give_ref in enumerate((give_0_ref, give_1_ref)):

        @pl.when(pl.program_id(0) == n)
        def _(give_ref=give_ref):
            out_ref[0] = (keep_ref[0, 0] + give_ref[...].astype(WIDE)).astype(LOW)


def far_sum(keep, give):
    _, halves, rows, features = keep.shape
    whole = pl.BlockSpec((rows, features), lambda m: (0, 0))
    return pl.pallas_call(
        leave_kernel,
        grid=(halves,),
        in_specs=[pl.BlockSpec((1, 1, rows, features), lambda m: (1, m, 0, 0)), whole, whole],
        out_specs=pl.BlockSpec((1, rows, features), lambda m: (m, 0, 0)),
        out_shape=jax.ShapeDtypeStruct((halves, rows, features), LOW),
        compiler_params=pltpu.CompilerParams(vmem_limit_bytes=40 * 2**20),
        cost_estimate=LITTLE,
    )(keep, *give)


def home_kernel(keep_ref, give_0_ref, give_1_ref, far_ref, kept_ref, other_ref):
    held = keep_ref[0, 0] + far_ref[0].astype(WIDE)

    @pl.when(pl.program_id(0) == 0)
    def _():
        other_ref[...] = (held + give_1_ref[...].astype(WIDE)).astype(LOW)

    @pl.when(pl.program_id(0) == 1)
    def _():
        kept_ref[...] = held + give_0_ref[...].astype(WIDE)


def home_sum(keep, give, far):
    _, halves, rows, features = keep.shape
    whole = pl.BlockSpec((rows, features), lambda m: (0, 0))
    return pl.pallas_call(
        home_kernel,
        grid=(halves,),
        in_specs=[
            pl.BlockSpec((1, 1, rows, features), lambda m: (0, 1 - m, 0, 0)),
            whole,
            whole,
            pl.BlockSpec((1, rows, features), lambda m: (1 - m, 0, 0)),
        ],
        out_specs=[whole, whole],
        out_shape=[
            jax.ShapeDtypeStruct((rows, features), WIDE),
            jax.ShapeDtypeStruct((rows, features), LOW),
        ],
        compiler_params=pltpu.CompilerParams(vmem_limit_bytes=40 * 2**20),
        cost_estimate=LITTLE,
    )(keep, *give, far)


def choose_kernel(odd_ref, kept_ref, other_ref, first_ref, second_ref):
    units = second_ref.shape[1]

    def store(value):
        first_ref[0] = value[:units].T
        second_ref[0] = value[units:]

    @pl.when(odd_ref[0] == 1)
    def _():
        store(kept_ref[...])

    @pl.when(odd_ref[0] == 0)
    def _():
        store(other_ref[...].astype(WIDE))


def choose(odd, kept, other):
    rows, features = kept.shape
    units = rows // 2
    whole = lambda *shape: pl.BlockSpec(shape, lambda i, o: (0,) * len(shape))
    grid_spec = pltpu.PrefetchScalarGridSpec(
        num_scalar_prefetch=1,
        grid=(1,),
        in_specs=[whole(rows, features), whole(rows, features)],
        out_specs=[whole(1, features, units), whole(1, units, features)],
    )
    return pl.pallas_call(
        choose_kernel,
        grid_spec=grid_spec,
        out_shape=[
            jax.ShapeDtypeStruct((1, features, units), WIDE),
            jax.ShapeDtypeStruct((1, units, features), WIDE),
        ],
        compiler_params=pltpu.CompilerParams(vmem_limit_bytes=40 * 2**20),
        cost_estimate=LITTLE,
    )(odd, kept, other)


def tokens_kernel(hot_ref, rows_ref, send_ref, keep_ref):
    total = mm_tn(hot_ref[...], rows_ref[...])

    @pl.when(pl.program_id(0) < 2)
    def _():
        send_ref[...] = total.astype(LOW)

    @pl.when(pl.program_id(0) >= 2)
    def _():
        keep_ref[...] = total


def to_tokens(hot, rows):
    count, features = rows.shape
    return pl.pallas_call(
        tokens_kernel,
        grid=(4,),
        in_specs=[
            pl.BlockSpec((count, BLOCK), lambda i: (0, i ^ 2)),
            pl.BlockSpec((count, features), lambda i: (0, 0)),
        ],
        out_specs=[
            pl.BlockSpec((BLOCK, features), lambda i: (jnp.minimum(i, 1), 0)),
            pl.BlockSpec((BLOCK, features), lambda i: (jnp.maximum(i - 2, 0), 0)),
        ],
        out_shape=[
            jax.ShapeDtypeStruct((2 * BLOCK, features), LOW),
            jax.ShapeDtypeStruct((2 * BLOCK, features), WIDE),
        ],
        compiler_params=pltpu.CompilerParams(vmem_limit_bytes=40 * 2**20),
        cost_estimate=LITTLE,
    )(hot, rows)


def finish_kernel(keep_ref, near_ref, far_ref, x_ref, gain_ref, dx_ref, out_ref):
    dh = keep_ref[...] + near_ref[...].astype(WIDE) + far_ref[...].astype(WIDE)
    normed, rstd = norm_parts(x_ref[...].astype(WIDE))
    scaled = dh * gain_ref[...]
    mean_plain = jnp.mean(scaled, axis=-1, keepdims=True)
    mean_normed = jnp.mean(scaled * normed, axis=-1, keepdims=True)
    out_ref[...] = dx_ref[...] + rstd * (scaled - mean_plain - normed * mean_normed)


def finish(keep, near, far, x, gain, dx):
    rows, features = x.shape
    size = 256
    by_row = pl.BlockSpec((size, features), lambda i: (i, 0))
    return pl.pallas_call(
        finish_kernel,
        grid=(rows // size,),
        in_specs=[by_row] * 4 + [pl.BlockSpec((1, features), lambda i: (0, 0)), by_row],
        out_specs=by_row,
        out_shape=jax.ShapeDtypeStruct((rows, features), WIDE),
        cost_estimate=LITTLE,
    )(keep, near, far, x, gain, dx)


def flip(array, axis, bits):
    size = lax.axis_size(axis)
    return lax.ppermute(array, axis, [(i, i ^ bits) for i in range(size)])


def flip_head_where(array, bits, odd):
    heads, rest = lax.axis_size("head"), lax.axis_size("dp")
    pairs = [
        (d * heads + h, d * heads + (h ^ bits)) for d in range(odd, rest, 2) for h in range(heads)
    ]
    return lax.ppermute(array, ("dp", "head"), pairs)


def after(value, *others):
    return lax.optimization_barrier((value, *others))[0]


def joined(pieces):
    return jnp.concatenate(pieces, axis=0)


def sum_over_dp_scattered(keep, give, other):
    bits, first = 1, None
    while True:
        come = flip(give, "dp", bits)
        if first is None:
            come = after(come, other)
        keep = keep + come.astype(WIDE)
        first = keep if first is None else first
        count = keep.shape[0]
        if count == 1:
            return keep[0], first
        keep, give = keep[: count // 2], keep[count // 2 :].astype(LOW)
        bits *= 2


def body(
    block_input,
    gain_one,
    gain_two,
    qkv_weight,
    out_weight,
    gate_weight,
    frozen_in,
    frozen_out,
    fresh_in,
    fresh_out,
    routes,
    doc_lengths,
    cotangent,
):
    own_rows, features = block_input.shape
    head_count, dp_count = lax.axis_size("head"), lax.axis_size("dp")
    head_index, dp_index = lax.axis_index("head"), lax.axis_index("dp")
    total = own_rows * head_count
    half = total // 2
    kinds = gate_weight.shape[1]
    share = 3 * total // kinds // head_count
    width = qkv_weight.shape[2]
    odd = dp_index % 2
    gain_one, gain_two = gain_one[None], gain_two[None]

    c_far = flip(cotangent, "head", 2)
    c_near, x_near = flip(cotangent, "head", 1), flip(block_input, "head", 1)
    x_far = flip(after(block_input, c_far), "head", 2)

    piece = jnp.concatenate(
        [qkv_weight[0], qkv_weight[1], qkv_weight[2], out_weight.T], axis=1
    ).astype(LOW)
    weights = lax.all_to_all(
        jnp.broadcast_to(piece[None], (dp_count,) + piece.shape), "dp", 0, 0, tiled=True
    ).reshape(features, 4 * width)

    tokens = jnp.arange(total, dtype=jnp.int32)
    hits = (routes[:, :, None] == jnp.arange(kinds, dtype=jnp.int32)).astype(LOW)
    earlier = (tokens[:, None] > tokens[None, :]).astype(LOW)
    counts = mm(earlier, hits.reshape(total, 2 * kinds)).reshape(total, 2, kinds)
    firsts = jnp.sum(hits[:, 0].astype(WIDE), axis=0)
    counts = counts + jnp.stack([jnp.zeros_like(firsts), firsts])[None]
    slots = jnp.sum(counts * hits.astype(WIDE), axis=2).astype(jnp.int32)
    hosts = routes % (kinds // 2) * 2 + routes // (kinds // 2)
    held_here = slots % head_count == head_index
    near_places = jnp.where(held_here, (hosts ^ dp_index) * share + slots // head_count, -1)
    places = jnp.where(held_here, hosts * share + slots // head_count, -1)
    placed = jnp.concatenate([near_places, places, jnp.sum(routes, axis=1, keepdims=True)], axis=1)
    placed = placed.reshape(head_count, own_rows, 5)
    placed = joined(
        [
            lax.dynamic_index_in_dim(placed, head_index ^ k, 0, keepdims=False)
            for k in (0, 2, 1, 3)
        ]
    ).T
    placed = jnp.pad(placed, ((0, 3), (0, 0)))
    here_dp = dp_index.astype(jnp.int32)[None]

    kept, given = expert_halves(
        after(odd.astype(jnp.int32)[None], c_far), frozen_in, frozen_out, fresh_in, fresh_out
    )

    come = flip(given, "dp", 1)

    c_pieces = [cotangent, c_far, c_near, flip(after(c_far, kept), "head", 1)]
    c_out, in_order, picks = send_rows(here_dp, placed, c_pieces, dp_count, share)
    x_far = after(x_far, c_out)
    x_pieces = [block_input, x_far, x_near, flip(x_far, "head", 1)]

    kept_far = flip(after(kept, x_far), "head", 2)

    near_kept = flip(kept, "head", 1)
    out = weights[:, 3 * width :]
    out_far, out_near = flip(out, "head", 2), flip(out, "head", 1)
    out_last = flip(out_far, "head", 1)

    ends = jnp.cumsum(doc_lengths[0])
    start = jnp.max(jnp.where(tokens[:, None] >= ends[None], ends[None], 0), axis=1)
    own_kind = dp_index // 2 + odd * (kinds // 2)
    meta = jnp.concatenate(
        [head_index[None], start[::BLOCK] // BLOCK, dp_index[None], own_kind[None]]
    ).astype(jnp.int32)
    start = start[None]
    h_one, qt, queries, keys, kt, values, context, context_t, log_totals = attend(
        meta, start, x_pieces, gain_one, weights, width
    )
    near_context = flip(context, "head", 1)
    far_context = flip(after(context, kept_far, near_kept, out_far), "head", 2)
    c_in = lax.all_to_all(c_out, "dp", 0, 0, tiled=True)
    last_context = flip(after(far_context, come), "head", 1)
    come_far = flip(after(come, far_context), "head", 2)
    last_kept = flip(kept_far, "head", 1)
    per = dp_count // 4
    x_one, *x_out = mix(
        placed, x_pieces, after(gain_two, last_kept),
        [context, far_context, near_context, last_context], [out, out_far, out_near, out_last],
        dp_count, share,
    )
    near_come, last_come = (flip(after(w, x_one), "head", 1) for w in (come, come_far))
    halves = [kept, come, kept_far, come_far, near_kept, near_come, last_kept, last_come]

    groups = [range(n * per, (n + 1) * per) for n in range(4)]
    x_parts = {k: flip(x_out[k], "dp", k) if k else x_out[0] for k in range(2 * per)}
    x_parts.update({k: flip(after(x_out[k], x_parts[1]), "dp", k) for k in groups[2]})
    held, dx_parts = None, {}
    for n, ks in enumerate(groups):
        xs = [x_parts[k] for k in ks]
        if n == 3:
            xs[0] = after(xs[0], *[dx_parts[k] for k in (*groups[0], *groups[1])])
        held, dx = run_experts(meta, xs, c_in, gate_weight.T, halves, n, 4, held)
        if n == 2:
            back = flip(joined(dx), "dp", n * per)
            for r, k in enumerate(ks):
                part = back[r * share : (r + 1) * share]
                dx_parts[k] = flip(part, "dp", r) if r else part
        else:
            dx_parts.update({k: part if k == 0 else flip(part, "dp", k) for k, part in zip(ks, dx)})
        if n == 0:
            x_parts.update({k: flip(after(x_out[k], dx[0]), "dp", k) for k in groups[3]})

    cut = 2 * per * share
    early = joined([dx_parts[k] for k in range(2 * per)])
    there = mm_tn(picks[:cut, half:], early)
    here = mm_tn(picks[:cut, :half], early)
    late = [dx_parts[k] for k in (*groups[2], *groups[3])]
    late = joined([after(late[0], there, here), *late[1:]])
    there = (there + mm_tn(picks[cut:, half:], late)).astype(LOW)
    sent = flip(there, "head", 1)
    here = (here + mm_tn(picks[cut:, :half], late) + sent.astype(WIDE)).astype(LOW)
    across = flip(here, "head", 2)

    hidden, hidden_grads, x_all, dy_all, marks, gated = held
    *give, keep, grad_gate = expert_grads(hidden, hidden_grads, after(x_all, here), dy_all, marks)
    give = [flip(part, "head", 1) for part in give]
    leave = far_sum(keep, give[2:])
    gated = after(gated, leave)
    dh_mine = (
        here.astype(WIDE) + joined([across[own_rows:], across[:own_rows]]).astype(WIDE)
    ).astype(LOW)
    dh_near = flip(dh_mine, "head", 1)
    crossed = flip_head_where(after(leave, dh_mine), 2, 1)
    keep_home, give_home = keep, give[:2]

    dx_one, grad_gain_two, send, mine, keep, give, dots = attend_back(
        meta, start, x_one, [dh_mine, dh_near], c_pieces, gain_two, weights,
        qt, queries, keys, kt, values, context_t, log_totals, h_one, context, dp_count,
    )
    send = flip(after(send, crossed), "head", 1)
    far_out = (mine[own_rows:] + send[own_rows:].astype(WIDE)).astype(LOW)
    far = flip(far_out, "head", 2)
    grad_input = finish(mine[:own_rows], send[:own_rows], far, block_input, gain_one, dx_one)
    grads, once_summed = sum_over_dp_scattered(keep, give, far_out)
    grad_qkv = jnp.stack([grads[:, n * width : (n + 1) * width] for n in range(3)])
    grad_out_weight = grads[:, 3 * width :].T

    gated = lax.all_to_all(
        gated.reshape(dp_count, share, features), "dp", 0, 0, tiled=True
    ).reshape(dp_count * share, features)
    small = joined([dots[:, 0][None] / gain_one, grad_gain_two, grad_gate.T])
    for bits in (1, 2):
        small = small + flip(small, "head", bits)
    small = after(small, once_summed)
    small = small + flip(small, "dp", 1)
    kept_home, other = home_sum(keep_home, give_home, after(crossed, far_out, once_summed))
    over = flip(after(other, small), "dp", 1)
    send, mine = to_tokens(in_order, after(gated, other))
    send = flip(send, "head", 1)
    y_out = (mine[own_rows:] + send[own_rows:].astype(WIDE)).astype(LOW)
    y_far = flip(y_out, "head", 2)
    mixture = mine[:own_rows] + send[:own_rows].astype(WIDE) + y_far.astype(WIDE)
    result = (x_one[:own_rows] + mixture).astype(LOW)
    small = after(small, y_out)
    bits = 2
    while bits < dp_count:
        small = small + flip(small, "dp", bits)
        bits *= 2
    grad_fresh_in, grad_fresh_out = choose(odd.astype(jnp.int32)[None], kept_home, over)
    return (
        result,
        grad_input,
        small[0],
        small[1],
        grad_qkv,
        grad_out_weight,
        small[2:].T,
        grad_fresh_in,
        grad_fresh_out,
    )


def solution(mesh):
    return jax.shard_map(
        body,
        mesh=mesh,
        in_specs=(
            P(("dp", "head"), None),
            P(),
            P(),
            P(None, "dp", "head"),
            P("head", "dp"),
            P(),
            P("dp", None, "head"),
            P("dp", "head", None),
            P("dp", None, "head"),
            P("dp", "head", None),
            P("dp", None),
            P("dp", None),
            P(("dp", "head"), None),
        ),
        out_specs=(
            P(("dp", "head"), None),
            P(("dp", "head"), None),
            P(),
            P(),
            P(None, "dp", "head"),
            P("head", "dp"),
            P(),
            P("dp", None, "head"),
            P("dp", "head", None),
        ),
        check_vma=False,
    )
```

```python
import functools

import jax
import jax.numpy as jnp
from jax import lax
from jax.experimental import pallas as pl
from jax.experimental.pallas import tpu as pltpu
from jax.sharding import PartitionSpec as P

HD = 64
EPS = 1e-05
MASKED = -1000000000.0
ROOT_HALF = 0.7071067811865476
INV_ROOT_TAU = 0.3989422804014327
BLOCK = 512
LOW = jnp.bfloat16
WIDE = jnp.float32
LITTLE = pl.CostEstimate(flops=10**6, bytes_accessed=10**5, transcendentals=0)
NT = (((1,), (1,)), ((), ()))
TN = (((0,), (0,)), ((), ()))
ERF_P = 0.4
ERF_C = (
    0.11596113048765463,
    0.08091125192311208,
    0.23413842084756234,
    -0.1854556415158047,
    0.35457470270248115,
    -0.10012987827403336,
)


def mm(a, b):
    return jnp.dot(a, b, preferred_element_type=WIDE)


def mm_nt(a, b):
    return lax.dot_general(a, b, NT, preferred_element_type=WIDE)


def mm_tn(a, b):
    return lax.dot_general(a, b, TN, preferred_element_type=WIDE)


def spot_of(k):
    return (k % 2) * 2 + k // 2


def select_piece(spot, refs, out):
    for n, ref in enumerate(refs):

        @pl.when(spot == n)
        def _(ref=ref):
            out[...] = ref[...]


def piece_specs(rows, features):
    return [pl.BlockSpec((rows, features), lambda *i: (0, 0))] * 4


def norm_parts(values):
    centred = values - jnp.mean(values, axis=-1, keepdims=True)
    rstd = lax.rsqrt(jnp.mean(centred * centred, axis=-1, keepdims=True) + EPS)
    return centred * rstd, rstd


def attend_kernel(
    meta_ref, start_ref, x_0_ref, x_1_ref, x_2_ref, x_3_ref, gain_ref, w_ref,
    h_ref, qt_ref, q_ref, k_ref, kt_ref, v_ref, ctx_ref, ctxt_ref, lse_ref, k_all, vt_all, x_ref,
):
    step = pl.program_id(0)
    heads = qt_ref.shape[0]
    width = heads * HD
    start = start_ref[...]
    key_iota = lax.broadcasted_iota(jnp.int32, (BLOCK, BLOCK), 0)
    query_iota = lax.broadcasted_iota(jnp.int32, (BLOCK, BLOCK), 1)

    select_piece(spot_of(step ^ meta_ref[0]), (x_0_ref, x_1_ref, x_2_ref, x_3_ref), x_ref)
    normed, _ = norm_parts(x_ref[...].astype(WIDE))
    h_one = (normed * gain_ref[...]).astype(LOW)
    h_ref[...] = h_one
    here = pl.ds(pl.multiple_of(step * BLOCK, BLOCK), BLOCK)
    q = mm(h_one, w_ref[:, :width]).astype(LOW) * (HD**-0.5)
    k = mm(h_one, w_ref[:, width : 2 * width]).astype(LOW)
    v = mm(h_one, w_ref[:, 2 * width : 3 * width]).astype(LOW)
    q = q.astype(LOW)
    q_t, k_t, v_t = q.T, k.T, v.T
    for h in range(heads):
        rows = slice(h * HD, (h + 1) * HD)
        qt_ref[h] = q_t[rows]
        q_ref[h] = q[:, rows]
        kt_ref[h] = k_t[rows]
        k_ref[h] = k[:, rows]
        k_all[h, here, :] = k[:, rows]
        v_ref[h] = v[:, rows]
        vt_all[h, :, here] = v_t[rows]

    def block(j, carry, last):
        base = pl.multiple_of(j * BLOCK, BLOCK)
        allowed = key_iota + base >= start
        if last:
            allowed = allowed & (key_iota <= query_iota)
        out = []
        for h in range(heads):
            top, total, acc = carry[h]
            scores = mm(k_all[h, pl.ds(base, BLOCK), :], qt_ref[h])
            scores = jnp.where(allowed, scores, MASKED)
            peak = jnp.maximum(top, jnp.max(scores, axis=0, keepdims=True))
            raised = jnp.exp(scores - peak)
            fade = jnp.exp(top - peak)
            total = total * fade + jnp.sum(raised, axis=0, keepdims=True)
            acc = acc * fade + mm(vt_all[h, :, pl.ds(base, BLOCK)], raised.astype(LOW))
            out.append((peak, total, acc))
        return tuple(out)

    carry = tuple(
        (
            jnp.full((1, BLOCK), MASKED, WIDE),
            jnp.zeros((1, BLOCK), WIDE),
            jnp.zeros((HD, BLOCK), WIDE),
        )
        for _ in range(heads)
    )
    carry = lax.fori_loop(meta_ref[1 + step], step, lambda j, c: block(j, c, False), carry)
    carry = block(step, carry, True)
    for h in range(heads):
        top, total, acc = carry[h]
        acc = acc / total
        ctxt_ref[h] = acc
        lse_ref[h] = top + jnp.log(total)
        ctx_ref[h * HD : (h + 1) * HD, :] = acc.astype(LOW)


def attend(meta, start, pieces, gain, weights, width):
    features = gain.shape[1]
    rows = 4 * BLOCK
    heads = width // HD
    spot = lambda i, m: spot_of(i ^ m[0])
    place = lambda i, m: (spot(i, m), 0)

    by_column = pl.BlockSpec((heads, HD, BLOCK), lambda i, m: (0, 0, i))
    by_row = pl.BlockSpec((heads, BLOCK, HD), lambda i, m: (0, i, 0))
    grid_spec = pltpu.PrefetchScalarGridSpec(
        num_scalar_prefetch=1,
        grid=(rows // BLOCK,),
        in_specs=[
            pl.BlockSpec((1, BLOCK), lambda i, m: (0, i)),
            *piece_specs(BLOCK, features),
            pl.BlockSpec((1, features), lambda i, m: (0, 0)),
            pl.BlockSpec(weights.shape, lambda i, m: (0, 0)),
        ],
        out_specs=[
            pl.BlockSpec((BLOCK, features), place),
            by_column,
            by_row,
            by_row,
            by_column,
            by_row,
            pl.BlockSpec((width, BLOCK), lambda i, m: (0, spot(i, m))),
            by_column,
            pl.BlockSpec((heads, 1, BLOCK), lambda i, m: (0, 0, i)),
        ],
        scratch_shapes=[
            pltpu.VMEM((heads, rows, HD), LOW),
            pltpu.VMEM((heads, HD, rows), LOW),
            pltpu.VMEM((BLOCK, features), LOW),
        ],
    )
    tall = jax.ShapeDtypeStruct((heads, rows, HD), LOW)
    flat = jax.ShapeDtypeStruct((heads, HD, rows), LOW)
    return pl.pallas_call(
        attend_kernel,
        grid_spec=grid_spec,
        out_shape=[
            jax.ShapeDtypeStruct((rows, features), LOW),
            flat,
            tall,
            tall,
            flat,
            tall,
            jax.ShapeDtypeStruct((width, rows), LOW),
            jax.ShapeDtypeStruct((heads, HD, rows), WIDE),
            jax.ShapeDtypeStruct((heads, 1, rows), WIDE),
        ],
        compiler_params=pltpu.CompilerParams(vmem_limit_bytes=50 * 2**20),
        cost_estimate=LITTLE,
    )(meta, start, *pieces, gain, weights)


def attend_back_kernel(
    meta_ref, start_ref, x_ref, dh_mine_ref, dh_near_ref, c_0_ref, c_1_ref, c_2_ref, c_3_ref,
    gain_ref, w_ref, qt_ref, q_ref, k_ref, kt_ref, v_ref, ctxt_ref, lse_ref, h_ref, ctx_ref,
    dx_ref, dgain_ref, send_own_ref, send_far_ref, own_ref, far_ref, keep_ref, give_ref, dots_ref,
    dk_acc, dv_acc, dh_ref, c_ref, dqkv, d_all, acc,
):
    step = pl.program_id(0)
    heads = qt_ref.shape[0]
    width = heads * HD

    @pl.when(step == 0)
    def _():
        dk_acc[...] = jnp.zeros_like(dk_acc)
        dv_acc[...] = jnp.zeros_like(dv_acc)
        acc[...] = jnp.zeros_like(acc)

    def place(piece):
        return pl.ds(pl.multiple_of(spot_of(piece ^ meta_ref[0]) * BLOCK, BLOCK), BLOCK)

    @pl.when(step < 4)
    def _():
        start = start_ref[...]
        key_iota = lax.broadcasted_iota(jnp.int32, (BLOCK, BLOCK), 0)
        query_iota = lax.broadcasted_iota(jnp.int32, (BLOCK, BLOCK), 1)
        spot = spot_of(step ^ meta_ref[0])
        select_piece(spot, (c_0_ref, c_1_ref, c_2_ref, c_3_ref), c_ref)

        @pl.when(spot < 2)
        def _():
            dh_ref[...] = dh_mine_ref[...]

        @pl.when(spot >= 2)
        def _():
            dh_ref[...] = dh_near_ref[...]

        normed, rstd = norm_parts(x_ref[...])
        dh = dh_ref[...].astype(WIDE)
        scaled = dh * gain_ref[...]
        mean_plain = jnp.mean(scaled, axis=-1, keepdims=True)
        mean_normed = jnp.mean(scaled * normed, axis=-1, keepdims=True)
        dx = c_ref[...].astype(WIDE) + rstd * (scaled - mean_plain - normed * mean_normed)
        dattn = dx.astype(LOW)
        d_all[place(step), :] = dattn

        @pl.when(step == meta_ref[0])
        def _():
            dx_ref[...] = dx
            dgain_ref[...] = jnp.sum(dh * normed, axis=0, keepdims=True)

        g_all = mm(dattn, w_ref[:, 3 * width :]).astype(LOW)
        gt_all = g_all.T
        g = [g_all[:, h * HD : (h + 1) * HD] for h in range(heads)]
        gt = [gt_all[h * HD : (h + 1) * HD] for h in range(heads)]
        delta = [
            jnp.sum(gt[h].astype(WIDE) * ctxt_ref[h], axis=0, keepdims=True)
            for h in range(heads)
        ]

        def block(j, carry, last):
            base = pl.multiple_of(j * BLOCK, BLOCK)
            rows = pl.ds(base, BLOCK)
            allowed = key_iota + base >= start
            if last:
                allowed = allowed & (key_iota <= query_iota)
            out = []
            for h in range(heads):
                scores = mm(k_ref[h, rows, :], qt_ref[h])
                probs = jnp.where(allowed, jnp.exp(scores - lse_ref[h]), 0.0)
                slopes = mm(v_ref[h, rows, :], gt[h])
                score_grads = (probs * (slopes - delta[h])).astype(LOW)
                dv_acc[h, rows, :] += mm(probs.astype(LOW), g[h])
                dk_acc[h, rows, :] += mm(score_grads, q_ref[h])
                out.append(carry[h] + mm(kt_ref[h, :, rows], score_grads))
            return tuple(out)

        carry = tuple(jnp.zeros((HD, BLOCK), WIDE) for _ in range(heads))
        carry = lax.fori_loop(meta_ref[1 + step], step, lambda j, c: block(j, c, False), carry)
        carry = block(step, carry, True)
        scale = HD**-0.5
        dqkv[place(step), :width] = jnp.concatenate(
            [(c * scale).T for c in carry], axis=1
        ).astype(LOW)

    @pl.when(step == 3)
    def _():
        for n in range(4):
            rows = slice(n * BLOCK, (n + 1) * BLOCK)
            dqkv[place(n), width:] = jnp.concatenate(
                [part[h, rows, :] for part in (dk_acc, dv_acc) for h in range(heads)], axis=1
            ).astype(LOW)

    def rest(out, kind):
        rows = pl.ds(pl.multiple_of(((step - 4) ^ 2) * BLOCK, BLOCK), BLOCK)
        grads = dqkv[rows, :]
        out[...] = mm_nt(grads, w_ref[:, : 3 * width]).astype(kind)
        acc[:, : 3 * width] += mm_tn(h_ref[...], grads)
        acc[:, 3 * width :] += mm_tn(d_all[rows, :], ctx_ref[...].T)

    for n, (out, kind) in enumerate(
        ((send_own_ref, LOW), (send_far_ref, LOW), (own_ref, WIDE), (far_ref, WIDE))
    ):

        @pl.when(step == 4 + n)
        def _(out=out, kind=kind):
            rest(out, kind)

    @pl.when(step == 7)
    def _():
        dots_ref[...] = jnp.sum(
            acc[:, : 3 * width] * w_ref[:, : 3 * width].astype(WIDE), axis=1, keepdims=True
        )
        count, size = 2 * keep_ref.shape[0], keep_ref.shape[1]
        for n in range(count):
            k = sum(((n >> b) & 1) * (count >> 1 >> b) for b in range(count.bit_length() - 1))
            part = acc[pl.ds(pl.multiple_of((meta_ref[5] ^ k) * size, 8), size), :]
            if n < count // 2:
                keep_ref[n] = part
            else:
                give_ref[n - count // 2] = part.astype(LOW)


def attend_back(
    meta, start, x_one, dh_pieces, c_pieces, gain, weights,
    qt, q, keys, kt, values, ctxt, lse, h_one, context, count,
):
    heads, _, rows = qt.shape
    features = x_one.shape[1]
    every = weights.shape[1]
    low = lambda i: jnp.minimum(i, 3)
    high = lambda i: jnp.maximum(i - 4, 0) ^ 2
    spot = lambda i, m: spot_of(low(i) ^ m[0])
    once = pl.Buffered(1)
    by_column = pl.BlockSpec((heads, HD, BLOCK), lambda i, m: (0, 0, low(i)))
    by_row = pl.BlockSpec((heads, BLOCK, HD), lambda i, m: (0, low(i), 0))

    def whole(*shape):
        return pl.BlockSpec(shape, lambda i, m: (0,) * len(shape), pipeline_mode=once)

    def out(*shape):
        return pl.BlockSpec(shape, lambda i, m: (0,) * len(shape))

    share = (count // 2, features // count, every)
    grid_spec = pltpu.PrefetchScalarGridSpec(
        num_scalar_prefetch=1,
        grid=(8,),
        in_specs=[
            pl.BlockSpec((1, BLOCK), lambda i, m: (0, low(i))),
            pl.BlockSpec((BLOCK, features), lambda i, m: (spot(i, m), 0)),
            pl.BlockSpec((BLOCK, features), lambda i, m: (jnp.minimum(spot(i, m), 1), 0)),
            pl.BlockSpec((BLOCK, features), lambda i, m: (jnp.maximum(spot(i, m) - 2, 0), 0)),
            *([whole(BLOCK, features)] * 4),
            whole(1, features),
            whole(*weights.shape),
            by_column,
            by_row,
            whole(heads, rows, HD),
            whole(heads, HD, rows),
            whole(heads, rows, HD),
            by_column,
            pl.BlockSpec((heads, 1, BLOCK), lambda i, m: (0, 0, low(i))),
            pl.BlockSpec((BLOCK, features), lambda i, m: (high(i), 0)),
            pl.BlockSpec((heads * HD, BLOCK), lambda i, m: (0, high(i))),
        ],
        out_specs=[
            out(BLOCK, features),
            out(1, features),
            *([out(BLOCK, features)] * 4),
            out(*share),
            out(*share),
            out(features, 1),
        ],
        scratch_shapes=[pltpu.VMEM((heads, rows, HD), WIDE)] * 2
        + [pltpu.VMEM((BLOCK, features), LOW)] * 2
        + [
            pltpu.VMEM((rows, 3 * heads * HD), LOW),
            pltpu.VMEM((rows, features), LOW),
            pltpu.VMEM((features, every), WIDE),
        ],
    )
    return pl.pallas_call(
        attend_back_kernel,
        grid_spec=grid_spec,
        out_shape=[
            jax.ShapeDtypeStruct((BLOCK, features), WIDE),
            jax.ShapeDtypeStruct((1, features), WIDE),
            *([jax.ShapeDtypeStruct((BLOCK, features), LOW)] * 2),
            *([jax.ShapeDtypeStruct((BLOCK, features), WIDE)] * 2),
            jax.ShapeDtypeStruct(share, WIDE),
            jax.ShapeDtypeStruct(share, LOW),
            jax.ShapeDtypeStruct((features, 1), WIDE),
        ],
        compiler_params=pltpu.CompilerParams(vmem_limit_bytes=61 * 2**20),
        cost_estimate=LITTLE,
    )(
        meta, start, x_one, *dh_pieces, *c_pieces, gain, weights,
        qt, q, keys, kt, values, ctxt, lse, h_one, context,
    )


def hot_rows(placed_ref, line, first, rows):
    spots = lax.broadcasted_iota(jnp.int32, (rows, placed_ref.shape[1]), 0) + first
    hot = (placed_ref[line : line + 1, :] == spots) | (placed_ref[line + 1 : line + 2, :] == spots)
    return jnp.where(hot, 1.0, 0.0).astype(LOW)


def send_kernel(
    index_ref, placed_ref, c_0_ref, c_1_ref, c_2_ref, c_3_ref, c_ref, in_order_ref, picks_ref, rows_all
):
    step = pl.program_id(0)
    share = in_order_ref.shape[0]
    size = c_0_ref.shape[0]

    @pl.when(step == 0)
    def _():
        for n, ref in enumerate((c_0_ref, c_1_ref, c_2_ref, c_3_ref)):
            rows_all[n * size : (n + 1) * size, :] = ref[...]

    hot = hot_rows(placed_ref, 2, step * share, share)
    in_order_ref[...] = hot
    picks_ref[...] = hot
    c_ref[0, :share, :] = mm(hot, rows_all[...]).astype(LOW)
    sums = mm_nt(placed_ref[...].astype(WIDE).astype(LOW), hot)[4:5]
    line = jnp.concatenate(
        [sums, jnp.zeros((1, c_ref.shape[2] - share), WIDE)], axis=1
    ) if c_ref.shape[2] > share else sums
    c_ref[0, share:, :] = jnp.broadcast_to(line, (16, c_ref.shape[2])).astype(LOW)


def send_rows(index, placed, pieces, count, share):
    size, features = pieces[0].shape
    total = 4 * size
    whole = lambda *shape: pl.BlockSpec(shape, lambda p, o: (0,) * len(shape))
    grid_spec = pltpu.PrefetchScalarGridSpec(
        num_scalar_prefetch=1,
        grid=(count,),
        in_specs=[
            whole(*placed.shape),
            *([whole(size, features)] * 4),
        ],
        out_specs=[
            pl.BlockSpec((1, share + 16, features), lambda p, o: (p, 0, 0)),
            pl.BlockSpec((share, total), lambda p, o: (p, 0)),
            pl.BlockSpec((share, total), lambda p, o: (p ^ o[0], 0)),
        ],
        scratch_shapes=[pltpu.VMEM((total, features), LOW)],
    )
    return pl.pallas_call(
        send_kernel,
        grid_spec=grid_spec,
        out_shape=[
            jax.ShapeDtypeStruct((count, share + 16, features), LOW),
            jax.ShapeDtypeStruct((count * share, total), LOW),
            jax.ShapeDtypeStruct((count * share, total), LOW),
        ],
        compiler_params=pltpu.CompilerParams(vmem_limit_bytes=40 * 2**20),
        cost_estimate=pl.CostEstimate(flops=4 * 10**10, bytes_accessed=10**7, transcendentals=0),
    )(index, placed, *pieces)


def halves_kernel(odd_ref, frozen_in_ref, frozen_out_ref, fresh_in_ref, fresh_out_ref, kept_ref, given_ref):
    units = frozen_out_ref.shape[1]

    def store(out, first, second):
        out[:units, :] = first[0].T.astype(LOW)
        out[units:, :] = second[0].astype(LOW)

    @pl.when(odd_ref[0] == 0)
    def _():
        store(kept_ref, frozen_in_ref, frozen_out_ref)
        store(given_ref, fresh_in_ref, fresh_out_ref)

    @pl.when(odd_ref[0] == 1)
    def _():
        store(kept_ref, fresh_in_ref, fresh_out_ref)
        store(given_ref, frozen_in_ref, frozen_out_ref)


def expert_halves(odd, frozen_in, frozen_out, fresh_in, fresh_out):
    _, features, units = frozen_in.shape
    grid_spec = pltpu.PrefetchScalarGridSpec(
        num_scalar_prefetch=1,
        grid=(1,),
        in_specs=[
            pl.BlockSpec(w.shape, lambda p, o: (0, 0, 0))
            for w in (frozen_in, frozen_out, fresh_in, fresh_out)
        ],
        out_specs=[pl.BlockSpec((2 * units, features), lambda p, o: (0, 0))] * 2,
    )
    return pl.pallas_call(
        halves_kernel,
        grid_spec=grid_spec,
        out_shape=[jax.ShapeDtypeStruct((2 * units, features), LOW)] * 2,
        compiler_params=pltpu.CompilerParams(vmem_limit_bytes=40 * 2**20),
        cost_estimate=LITTLE,
    )(odd, frozen_in, frozen_out, fresh_in, fresh_out)


def mix_kernel(count, gain_ref, placed_ref, *refs):
    context_refs, weight_refs, piece_refs = refs[:4], refs[4:8], refs[8:12]
    x_one_ref, taken_refs, x_ref, h_all = refs[12], refs[13 : 13 + count], refs[-2], refs[-1]
    step = pl.program_id(0)
    size = x_ref.shape[0]
    select_piece(step, piece_refs, x_ref)
    attn = mm_nt(context_refs[0][...].T, weight_refs[0][...])
    for n in range(1, 4):
        attn = attn + mm_nt(context_refs[n][...].T, weight_refs[n][...])
    x_one = x_ref[...].astype(WIDE) + attn
    x_one_ref[...] = x_one
    normed, _ = norm_parts(x_one)
    h_all[pl.ds(pl.multiple_of(step * size, size), size), :] = (normed * gain_ref[...]).astype(LOW)

    @pl.when(step == pl.num_programs(0) - 1)
    def _():
        share = taken_refs[0].shape[0]
        for k in range(count):
            hot = hot_rows(placed_ref, 0, k * share, share)
            taken_refs[k][...] = mm(hot, h_all[...]).astype(LOW)


def mix(placed, pieces, gain, contexts, weights, count, share):
    width, rows = contexts[0].shape
    features = gain.shape[1]
    size = rows // 4

    def context_spec(n):
        return pl.BlockSpec((width, size), lambda i: (0, i ^ n))

    return pl.pallas_call(
        functools.partial(mix_kernel, count),
        grid=(4,),
        in_specs=[
            pl.BlockSpec((1, features), lambda i: (0, 0)),
            pl.BlockSpec(placed.shape, lambda i: (0, 0)),
        ]
        + [context_spec(n) for n in range(4)]
        + [pl.BlockSpec((features, width), lambda i: (0, 0))] * 4
        + piece_specs(size, features),
        scratch_shapes=[pltpu.VMEM((size, features), LOW), pltpu.VMEM((rows, features), LOW)],
        out_specs=[pl.BlockSpec((size, features), lambda i: (i, 0))]
        + [pl.BlockSpec((share, features), lambda i: (0, 0))] * count,
        out_shape=[jax.ShapeDtypeStruct((rows, features), WIDE)]
        + [jax.ShapeDtypeStruct((share, features), LOW)] * count,
        compiler_params=pltpu.CompilerParams(vmem_limit_bytes=60 * 2**20),
        cost_estimate=LITTLE,
    )(gain, placed, *contexts, *weights, *pieces)


def expert_kernel(count, meta_ref, *refs):
    x_refs, refs = refs[:count], refs[count:]
    c_refs, refs = refs[:count], refs[count:]
    wg_ref, weight_refs = refs[0], refs[1:9]
    refs = refs[-(15 + count) :]
    a_ref, du_ref, xs_ref, dy_ref, mark_ref, y_ref = refs[:6]
    dx_refs, refs = refs[6 : 6 + count], refs[6 + count :]
    cs, w1_all, w2_all, sems, acc, acc_y, dots, others, gate = refs
    step, steps = pl.program_id(0), pl.num_programs(0)
    rows, kinds = xs_ref.shape[0], wg_ref.shape[0]
    share = rows // count
    units = w1_all.shape[1] // 2
    lanes = lax.broadcasted_iota(jnp.int32, (rows, kinds), 1)
    own = meta_ref[6]

    def fetches(n):
        slot = n % 2
        for m in range(2):
            span = slice(m * units, (m + 1) * units)
            for p, target in enumerate((w1_all, w2_all)):
                yield pltpu.make_async_copy(
                    weight_refs[2 * n + m].at[p * units : (p + 1) * units],
                    target.at[slot, span],
                    sems.at[slot, 2 * m + p],
                )

    def kinds_of():
        sums = [
            c_refs[n][0, share : share + 16, : -(-share // 128) * 128].astype(WIDE).T[:share, :1]
            for n in range(count)
        ]
        sums = jnp.concatenate(sums, axis=0).astype(jnp.int32)
        return lanes == own, lanes == sums - own

    @pl.when(step == 0)
    def _():
        for copy in fetches(0):
            copy.start()
        for n in range(count):
            xs_ref[n * share : (n + 1) * share, :] = x_refs[n][...]
            cs[n * share : (n + 1) * share, :] = c_refs[n][0, :share, :]
        logits = mm_nt(xs_ref[...], wg_ref[...].astype(LOW))
        here, there = kinds_of()
        mine = jnp.sum(jnp.where(here, logits, 0.0), axis=1, keepdims=True)
        theirs = jnp.sum(jnp.where(there, logits, 0.0), axis=1, keepdims=True)
        peak = jnp.maximum(mine, theirs)
        mine, theirs = jnp.exp(mine - peak), jnp.exp(theirs - peak)
        gate[...] = mine / (mine + theirs)
        others[...] = theirs / (mine + theirs)
        dy_ref[...] = (gate[...] * cs[...].astype(WIDE)).astype(LOW)
        acc[...] = jnp.zeros_like(acc)
        acc_y[...] = jnp.zeros_like(acc_y)
        dots[...] = jnp.zeros_like(dots)

    for n in range(4):

        @pl.when(step == n)
        def _(n=n):
            if n < 3:
                for copy in fetches(n + 1):
                    copy.start()
            for copy in fetches(n):
                copy.wait()

    w1, w2 = w1_all[step % 2], w2_all[step % 2]
    u = mm_nt(xs_ref[...], w1)
    da = mm_nt(cs[...], w2)
    bell = jnp.exp(u * u * -0.5)
    t = 1.0 / (1.0 + jnp.abs(u) * (ERF_P * ROOT_HALF))
    tail = ERF_C[-1] * t
    for coefficient in ERF_C[-2::-1]:
        tail = (tail + coefficient) * t
    tail = tail * bell
    part = jnp.where(u >= 0.0, 1.0 - tail, tail)
    a = (u * part).astype(LOW)
    slope = part + u * bell * INV_ROOT_TAU
    dots[...] += jnp.sum(a.astype(WIDE) * da, axis=1, keepdims=True)
    du = (gate[...] * da * slope).astype(LOW)
    a_ref[...] = a
    du_ref[...] = du
    acc_y[...] += mm(a, w2)
    acc[...] += mm(du, w1)

    @pl.when(step == steps - 1)
    def _():
        pull = gate[...] * others[...] * dots[...]
        here, there = kinds_of()
        marks = jnp.where(here, pull, 0.0) - jnp.where(there, pull, 0.0)
        mark_ref[...] = marks
        high = marks.astype(LOW)
        rest = (marks - high.astype(WIDE)).astype(LOW)
        gate_low = wg_ref[...].astype(LOW)
        dx = acc[...] + mm(high, gate_low) + mm(rest, gate_low)
        for n in range(count):
            dx_refs[n][...] = dx[n * share : (n + 1) * share].astype(LOW)
        y = (gate[...] * acc_y[...]).astype(LOW)
        for n in range(count):
            base = pl.multiple_of((meta_ref[5] % count ^ n) * share, 16)
            y_ref[pl.ds(base, share), :] = y[n * share : (n + 1) * share]


def run_experts(meta, xs, c, gate_weight, weights, chunk, chunks, held):
    count = len(xs)
    share, features = xs[0].shape
    rows = count * share
    units = weights[0].shape[0]
    kinds = gate_weight.shape[0]
    whole = lambda *shape: pl.BlockSpec(shape, lambda p, o: (0,) * len(shape))
    by_piece = pl.BlockSpec((rows, units), lambda p, o: (chunk, p))
    by_chunk = lambda width: pl.BlockSpec((rows, width), lambda p, o: (chunk, 0))
    anywhere = pl.BlockSpec(memory_space=pl.ANY)

    def c_spec(n):
        return pl.BlockSpec((1,) + c.shape[1:], lambda p, o: (o[5] ^ (chunk * count + n), 0, 0))

    operands = [meta, *xs, *([c] * count), gate_weight, *weights]
    in_specs = (
        [whole(share, features)] * count
        + [c_spec(n) for n in range(count)]
        + [whole(kinds, features)]
        + [anywhere] * 8
    )
    aliases = {}
    if held is not None:
        aliases = {len(operands) + n: n for n in range(6)}
        operands += held
        in_specs += [anywhere] * 6
    every = chunks * rows
    grid_spec = pltpu.PrefetchScalarGridSpec(
        num_scalar_prefetch=1,
        grid=(4,),
        in_specs=in_specs,
        out_specs=[
            by_piece,
            by_piece,
            by_chunk(features),
            by_chunk(features),
            by_chunk(kinds),
            pl.BlockSpec((rows, features), lambda p, o: (o[5] // count ^ chunk, 0)),
            *([whole(share, features)] * count),
        ],
        scratch_shapes=[
            pltpu.VMEM((rows, features), LOW),
            pltpu.VMEM((2, units, features), LOW),
            pltpu.VMEM((2, units, features), LOW),
            pltpu.SemaphoreType.DMA((2, 4)),
            pltpu.VMEM((rows, features), WIDE),
            pltpu.VMEM((rows, features), WIDE),
            pltpu.VMEM((rows, 1), WIDE),
            pltpu.VMEM((rows, 1), WIDE),
            pltpu.VMEM((rows, 1), WIDE),
        ],
    )
    out = pl.pallas_call(
        functools.partial(expert_kernel, count),
        grid_spec=grid_spec,
        out_shape=[
            jax.ShapeDtypeStruct((every, 4 * units), LOW),
            jax.ShapeDtypeStruct((every, 4 * units), LOW),
            jax.ShapeDtypeStruct((every, features), LOW),
            jax.ShapeDtypeStruct((every, features), LOW),
            jax.ShapeDtypeStruct((every, kinds), WIDE),
            jax.ShapeDtypeStruct((every, features), LOW),
            *([jax.ShapeDtypeStruct((share, features), LOW)] * count),
        ],
        input_output_aliases=aliases,
        compiler_params=pltpu.CompilerParams(vmem_limit_bytes=58 * 2**20),
        cost_estimate=LITTLE,
    )(*operands)
    return out[:6], out[6:]


def expert_grads_kernel(a_ref, du_ref, x_ref, dy_ref, marks_ref, *refs):
    give_refs, (keep_ref, gate_ref) = refs[:4], refs[4:]
    step = pl.program_id(0)

    @pl.when(step == 0)
    def _():
        high = marks_ref[...].astype(LOW)
        rest = (marks_ref[...] - high.astype(WIDE)).astype(LOW)
        gate_ref[...] = mm_tn(x_ref[...], high) + mm_tn(x_ref[...], rest)

    units = a_ref.shape[1] // 2

    def store(outs, kind):
        first = mm_tn(du_ref[...], x_ref[...])
        second = mm_tn(a_ref[...], dy_ref[...])
        for m, out in enumerate(outs):
            span = slice(m * units, (m + 1) * units)
            out[:units, :] = first[span].astype(kind)
            out[units:, :] = second[span].astype(kind)

    for n in range(2):

        @pl.when(step == n)
        def _(n=n):
            store(give_refs[2 * n : 2 * n + 2], LOW)

    @pl.when(step >= 2)
    def _():
        store((keep_ref.at[0, 0], keep_ref.at[0, 1]), WIDE)


def expert_grads(hidden, hidden_grads, x, dy, marks):
    rows, features = x.shape
    units = hidden.shape[1] // 4
    piece = pl.BlockSpec((rows, units), lambda p: (0, p ^ 2))
    all_rows = pl.BlockSpec((rows, features), lambda p: (0, 0))
    shape = (2, 2, units, features)
    return pl.pallas_call(
        expert_grads_kernel,
        grid=(4,),
        in_specs=[piece, piece, all_rows, all_rows, pl.BlockSpec(marks.shape, lambda p: (0, 0))],
        out_specs=[
            *([pl.BlockSpec(shape[2:], lambda p: (0, 0))] * 4),
            pl.BlockSpec((1,) + shape[1:], lambda p: (jnp.maximum(p - 2, 0), 0, 0, 0)),
            pl.BlockSpec((features, marks.shape[1]), lambda p: (0, 0)),
        ],
        out_shape=[
            *([jax.ShapeDtypeStruct(shape[2:], LOW)] * 4),
            jax.ShapeDtypeStruct(shape, WIDE),
            jax.ShapeDtypeStruct((features, marks.shape[1]), WIDE),
        ],
        compiler_params=pltpu.CompilerParams(vmem_limit_bytes=58 * 2**20),
        cost_estimate=LITTLE,
    )(hidden, hidden_grads, x, dy, marks)


def leave_kernel(keep_ref, give_0_ref, give_1_ref, out_ref):
    for n, give_ref in enumerate((give_0_ref, give_1_ref)):

        @pl.when(pl.program_id(0) == n)
        def _(give_ref=give_ref):
            out_ref[0] = (keep_ref[0, 0] + give_ref[...].astype(WIDE)).astype(LOW)


def far_sum(keep, give):
    _, halves, rows, features = keep.shape
    whole = pl.BlockSpec((rows, features), lambda m: (0, 0))
    return pl.pallas_call(
        leave_kernel,
        grid=(halves,),
        in_specs=[pl.BlockSpec((1, 1, rows, features), lambda m: (1, m, 0, 0)), whole, whole],
        out_specs=pl.BlockSpec((1, rows, features), lambda m: (m, 0, 0)),
        out_shape=jax.ShapeDtypeStruct((halves, rows, features), LOW),
        compiler_params=pltpu.CompilerParams(vmem_limit_bytes=40 * 2**20),
        cost_estimate=LITTLE,
    )(keep, *give)


def home_kernel(keep_ref, give_0_ref, give_1_ref, far_ref, kept_ref, *other_refs):
    held = keep_ref[0, 0] + far_ref[0].astype(WIDE)

    @pl.when(pl.program_id(0) == 0)
    def _():
        other = (held + give_1_ref[...].astype(WIDE)).astype(LOW)
        for n, out in enumerate(other_refs):
            out[...] = other[n * out.shape[0] : (n + 1) * out.shape[0]]

    @pl.when(pl.program_id(0) == 1)
    def _():
        kept_ref[...] = held + give_0_ref[...].astype(WIDE)


def home_sum(keep, give, far):
    _, halves, rows, features = keep.shape
    whole = pl.BlockSpec((rows, features), lambda m: (0, 0))
    return pl.pallas_call(
        home_kernel,
        grid=(halves,),
        in_specs=[
            pl.BlockSpec((1, 1, rows, features), lambda m: (0, 1 - m, 0, 0)),
            whole,
            whole,
            pl.BlockSpec((1, rows, features), lambda m: (1 - m, 0, 0)),
        ],
        out_specs=[whole] + [pl.BlockSpec((rows // 2, features), lambda m: (0, 0))] * 2,
        out_shape=[jax.ShapeDtypeStruct((rows, features), WIDE)]
        + [jax.ShapeDtypeStruct((rows // 2, features), LOW)] * 2,
        compiler_params=pltpu.CompilerParams(vmem_limit_bytes=40 * 2**20),
        cost_estimate=LITTLE,
    )(keep, *give, far)


def choose_kernel(odd_ref, kept_ref, other_0_ref, other_1_ref, first_ref, second_ref):
    units = second_ref.shape[1]

    @pl.when(odd_ref[0] == 1)
    def _():
        first_ref[0] = kept_ref[:units, :].T
        second_ref[0] = kept_ref[units:, :]

    @pl.when(odd_ref[0] == 0)
    def _():
        first_ref[0] = other_0_ref[...].astype(WIDE).T
        second_ref[0] = other_1_ref[...].astype(WIDE)


def choose(odd, kept, other):
    rows, features = kept.shape
    units = rows // 2
    whole = lambda *shape: pl.BlockSpec(shape, lambda i, o: (0,) * len(shape))
    grid_spec = pltpu.PrefetchScalarGridSpec(
        num_scalar_prefetch=1,
        grid=(1,),
        in_specs=[whole(rows, features)] + [whole(units, features)] * 2,
        out_specs=[whole(1, features, units), whole(1, units, features)],
    )
    return pl.pallas_call(
        choose_kernel,
        grid_spec=grid_spec,
        out_shape=[
            jax.ShapeDtypeStruct((1, features, units), WIDE),
            jax.ShapeDtypeStruct((1, units, features), WIDE),
        ],
        compiler_params=pltpu.CompilerParams(vmem_limit_bytes=40 * 2**20),
        cost_estimate=LITTLE,
    )(odd, kept, *other)


def tokens_kernel(hot_ref, rows_ref, *out_refs):
    total = mm_tn(hot_ref[...], rows_ref[...])
    for n, out in enumerate(out_refs):

        @pl.when(pl.program_id(0) == n)
        def _(out=out):
            out[...] = total.astype(out.dtype)


def to_tokens(hot, rows):
    count, features = rows.shape
    return pl.pallas_call(
        tokens_kernel,
        grid=(4,),
        in_specs=[
            pl.BlockSpec((count, BLOCK), lambda i: (0, i ^ 2)),
            pl.BlockSpec((count, features), lambda i: (0, 0)),
        ],
        out_specs=[pl.BlockSpec((BLOCK, features), lambda i: (0, 0))] * 4,
        out_shape=[jax.ShapeDtypeStruct((BLOCK, features), LOW)] * 2
        + [jax.ShapeDtypeStruct((BLOCK, features), WIDE)] * 2,
        compiler_params=pltpu.CompilerParams(vmem_limit_bytes=40 * 2**20),
        cost_estimate=LITTLE,
    )(hot, rows)


def finish_kernel(keep_ref, near_ref, far_ref, x_ref, gain_ref, dx_ref, out_ref):
    dh = keep_ref[...] + near_ref[...].astype(WIDE) + far_ref[...].astype(WIDE)
    normed, rstd = norm_parts(x_ref[...].astype(WIDE))
    scaled = dh * gain_ref[...]
    mean_plain = jnp.mean(scaled, axis=-1, keepdims=True)
    mean_normed = jnp.mean(scaled * normed, axis=-1, keepdims=True)
    out_ref[...] = dx_ref[...] + rstd * (scaled - mean_plain - normed * mean_normed)


def finish(keep, near, far, x, gain, dx):
    rows, features = x.shape
    size = 256
    by_row = pl.BlockSpec((size, features), lambda i: (i, 0))
    return pl.pallas_call(
        finish_kernel,
        grid=(rows // size,),
        in_specs=[by_row] * 4 + [pl.BlockSpec((1, features), lambda i: (0, 0)), by_row],
        out_specs=by_row,
        out_shape=jax.ShapeDtypeStruct((rows, features), WIDE),
        cost_estimate=LITTLE,
    )(keep, near, far, x, gain, dx)


def flip(array, axis, bits):
    size = lax.axis_size(axis)
    return lax.ppermute(array, axis, [(i, i ^ bits) for i in range(size)])


def flip_head_where(array, bits, odd):
    heads, rest = lax.axis_size("head"), lax.axis_size("dp")
    pairs = [
        (d * heads + h, d * heads + (h ^ bits)) for d in range(odd, rest, 2) for h in range(heads)
    ]
    return lax.ppermute(array, ("dp", "head"), pairs)


def after(value, *others):
    return lax.optimization_barrier((value, *others))[0]


def joined(pieces):
    return jnp.concatenate(pieces, axis=0)


def body(
    block_input,
    gain_one,
    gain_two,
    qkv_weight,
    out_weight,
    gate_weight,
    frozen_in,
    frozen_out,
    fresh_in,
    fresh_out,
    routes,
    doc_lengths,
    cotangent,
):
    own_rows, features = block_input.shape
    head_count, dp_count = lax.axis_size("head"), lax.axis_size("dp")
    head_index, dp_index = lax.axis_index("head"), lax.axis_index("dp")
    total = own_rows * head_count
    half = total // 2
    kinds = gate_weight.shape[1]
    share = 3 * total // kinds // head_count
    width = qkv_weight.shape[2]
    odd = dp_index % 2
    gain_one, gain_two = gain_one[None], gain_two[None]

    c_far = flip(cotangent, "head", 2)
    c_near, x_near = flip(cotangent, "head", 1), flip(block_input, "head", 1)
    x_far = flip(after(block_input, c_far), "head", 2)

    piece = jnp.concatenate(
        [qkv_weight[0], qkv_weight[1], qkv_weight[2], out_weight.T], axis=1
    ).astype(LOW)
    weights = lax.all_to_all(
        jnp.broadcast_to(piece[None], (dp_count,) + piece.shape), "dp", 0, 0, tiled=True
    ).reshape(features, 4 * width)

    tokens = jnp.arange(total, dtype=jnp.int32)
    hits = (routes[:, :, None] == jnp.arange(kinds, dtype=jnp.int32)).astype(LOW)
    earlier = (tokens[:, None] > tokens[None, :]).astype(LOW)
    counts = mm(earlier, hits.reshape(total, 2 * kinds)).reshape(total, 2, kinds)
    firsts = jnp.sum(hits[:, 0].astype(WIDE), axis=0)
    counts = counts + jnp.stack([jnp.zeros_like(firsts), firsts])[None]
    slots = jnp.sum(counts * hits.astype(WIDE), axis=2).astype(jnp.int32)
    hosts = routes % (kinds // 2) * 2 + routes // (kinds // 2)
    held_here = slots % head_count == head_index
    near_places = jnp.where(held_here, (hosts ^ dp_index) * share + slots // head_count, -1)
    places = jnp.where(held_here, hosts * share + slots // head_count, -1)
    placed = jnp.concatenate([near_places, places, jnp.sum(routes, axis=1, keepdims=True)], axis=1)
    placed = placed.reshape(head_count, own_rows, 5)
    placed = joined(
        [
            lax.dynamic_index_in_dim(placed, head_index ^ k, 0, keepdims=False)
            for k in (0, 2, 1, 3)
        ]
    ).T
    placed = jnp.pad(placed, ((0, 3), (0, 0)))
    here_dp = dp_index.astype(jnp.int32)[None]

    ends = jnp.cumsum(doc_lengths[0])
    start = jnp.max(jnp.where(tokens[:, None] >= ends[None], ends[None], 0), axis=1)
    own_kind = dp_index // 2 + odd * (kinds // 2)
    meta = jnp.concatenate(
        [head_index[None], start[::BLOCK] // BLOCK, dp_index[None], own_kind[None]]
    ).astype(jnp.int32)
    start = start[None]

    kept, given = expert_halves(
        after(odd.astype(jnp.int32)[None], c_far), frozen_in, frozen_out, fresh_in, fresh_out
    )

    come = flip(given, "dp", 1)

    c_pieces = [cotangent, c_far, c_near, flip(after(c_far, kept), "head", 1)]
    c_out, in_order, picks = send_rows(after(here_dp, meta, start), placed, c_pieces, dp_count, share)
    x_far = after(x_far, c_out)
    x_pieces = [block_input, x_far, x_near, flip(x_far, "head", 1)]

    kept_far = flip(after(kept, x_far), "head", 2)

    near_kept = flip(kept, "head", 1)
    out = weights[:, 3 * width :]
    out_far, out_near = flip(out, "head", 2), flip(out, "head", 1)
    out_last = flip(out_far, "head", 1)

    h_one, qt, queries, keys, kt, values, context, context_t, log_totals = attend(
        meta, start, x_pieces, gain_one, weights, width
    )
    near_context = flip(context, "head", 1)
    far_context = flip(after(context, kept_far, near_kept, out_far), "head", 2)
    c_in = lax.all_to_all(c_out, "dp", 0, 0, tiled=True)
    last_context = flip(after(far_context, come, out_near, out_last), "head", 1)
    come_far = flip(after(come, far_context), "head", 2)
    last_kept = flip(kept_far, "head", 1)
    per = dp_count // 4
    x_one, *x_out = mix(
        placed, x_pieces, after(gain_two, last_kept),
        [context, far_context, near_context, last_context], [out, out_far, out_near, out_last],
        dp_count, share,
    )
    near_come, last_come = (flip(after(w, x_one), "head", 1) for w in (come, come_far))
    halves = [kept, come, kept_far, come_far, near_kept, near_come, last_kept, last_come]

    groups = [range(n * per, (n + 1) * per) for n in range(4)]
    x_parts = {k: flip(x_out[k], "dp", k) if k else x_out[0] for k in range(2 * per)}
    x_parts.update({k: flip(after(x_out[k], x_parts[1]), "dp", k) for k in groups[2]})
    held, dx_parts = None, {}
    for n, ks in enumerate(groups):
        xs = [x_parts[k] for k in ks]
        if n == 3:
            xs[0] = after(xs[0], *[dx_parts[k] for k in (*groups[0], *groups[1])])
        held, dx = run_experts(meta, xs, c_in, gate_weight.T, halves, n, 4, held)
        if n == 2:
            back = flip(joined(dx), "dp", n * per)
            for r, k in enumerate(ks):
                part = back[r * share : (r + 1) * share]
                dx_parts[k] = flip(part, "dp", r) if r else part
        else:
            dx_parts.update({k: part if k == 0 else flip(part, "dp", k) for k, part in zip(ks, dx)})
        if n == 0:
            x_parts.update({k: flip(after(x_out[k], dx[0]), "dp", k) for k in groups[3]})

    cut = 2 * per * share
    early = joined([dx_parts[k] for k in range(2 * per)])
    there = mm_tn(picks[:cut, half:], early)
    here = mm_tn(picks[:cut, :half], early)
    late = [dx_parts[k] for k in (*groups[2], *groups[3])]
    late = joined([after(late[0], there, here), *late[1:]])
    there = (there + mm_tn(picks[cut:, half:], late)).astype(LOW)
    sent = flip(there, "head", 1)
    here = (here + mm_tn(picks[cut:, :half], late) + sent.astype(WIDE)).astype(LOW)
    across = flip(here, "head", 2)

    hidden, hidden_grads, x_all, dy_all, marks, gated = held
    *give, keep, grad_gate = expert_grads(hidden, hidden_grads, after(x_all, here), dy_all, marks)
    give = [flip(part, "head", 1) for part in give]
    leave = far_sum(keep, give[2:])
    gated = lax.all_to_all(
        after(gated, keep).reshape(dp_count, share, features), "dp", 0, 0, tiled=True
    ).reshape(dp_count * share, features)
    dh_mine = (
        here.astype(WIDE) + joined([across[own_rows:], across[:own_rows]]).astype(WIDE)
    ).astype(LOW)
    dh_near = flip(dh_mine, "head", 1)
    crossed = flip_head_where(after(leave, dh_mine), 2, 1)
    keep_home, give_home = keep, give[:2]

    dx_one, grad_gain_two, send_own, send_far, own, far, keep, give, dots = attend_back(
        meta, start, x_one, [dh_mine, dh_near], c_pieces, gain_two, weights,
        qt, queries, keys, kt, values, context_t, log_totals, h_one, context, dp_count,
    )
    send_far = flip(after(send_far, crossed), "head", 1)
    send_own = flip(send_own, "head", 1)
    far_out = (far + send_far.astype(WIDE)).astype(LOW)
    far = flip(far_out, "head", 2)
    grad_input = finish(own, send_own, far, block_input, gain_one, dx_one)

    y_send_own, y_send_far, y_own, y_far = to_tokens(in_order, after(gated, give))
    tokens_done = y_own
    y_send_far = flip(y_send_far, "head", 1)
    y_send_own = flip(y_send_own, "head", 1)
    y_out = (y_far + y_send_far.astype(WIDE)).astype(LOW)
    y_far = flip(y_out, "head", 2)
    mixture = y_own + y_send_own.astype(WIDE) + y_far.astype(WIDE)
    result = (x_one[:own_rows] + mixture).astype(LOW)

    dots = after(dots, send_far)
    small = joined([dots[:, 0][None] / gain_one, grad_gain_two, grad_gate.T])
    for bits in (1, 2):
        small = small + flip(small, "head", bits)
    keep = keep + after(flip(give, "dp", 1), far_out, small, tokens_done).astype(WIDE)
    kept_home, *other = home_sum(keep_home, give_home, after(crossed, keep))
    over = [flip(part, "dp", 1) for part in other]
    bits, small = 2, after(small, over[0])
    while bits < dp_count:
        count = keep.shape[0]
        come = flip(keep[count // 2 :].astype(LOW), "dp", bits)
        small = small + flip(small, "dp", bits)
        if bits == 2:
            come = after(come, *other)
        if count == 2:
            small = after(small, y_out)
            small = small + flip(small, "dp", 1)
            come = after(come, y_far, small, grad_input)
        keep = keep[: count // 2] + come.astype(WIDE)
        bits *= 2
    grads = keep[0]
    grad_qkv = jnp.stack([grads[:, n * width : (n + 1) * width] for n in range(3)])
    grad_out_weight = grads[:, 3 * width :].T
    grad_fresh_in, grad_fresh_out = choose(odd.astype(jnp.int32)[None], kept_home, over)
    return (
        result,
        grad_input,
        small[0],
        small[1],
        grad_qkv,
        grad_out_weight,
        small[2:].T,
        grad_fresh_in,
        grad_fresh_out,
    )


def solution(mesh):
    return jax.shard_map(
        body,
        mesh=mesh,
        in_specs=(
            P(("dp", "head"), None),
            P(),
            P(),
            P(None, "dp", "head"),
            P("head", "dp"),
            P(),
            P("dp", None, "head"),
            P("dp", "head", None),
            P("dp", None, "head"),
            P("dp", "head", None),
            P("dp", None),
            P("dp", None),
            P(("dp", "head"), None),
        ),
        out_specs=(
            P(("dp", "head"), None),
            P(("dp", "head"), None),
            P(),
            P(),
            P(None, "dp", "head"),
            P("head", "dp"),
            P(),
            P("dp", None, "head"),
            P("dp", "head", None),
        ),
        check_vma=False,
    )
```

```python
import functools

import jax
import jax.numpy as jnp
from jax import lax
from jax.experimental import pallas as pl
from jax.experimental.pallas import tpu as pltpu
from jax.sharding import PartitionSpec as P

HD = 64
EPS = 1e-05
MASKED = -1000000000.0
ROOT_HALF = 0.7071067811865476
INV_ROOT_TAU = 0.3989422804014327
BLOCK = 512
LOW = jnp.bfloat16
WIDE = jnp.float32
LITTLE = pl.CostEstimate(flops=10**6, bytes_accessed=10**5, transcendentals=0)
NT = (((1,), (1,)), ((), ()))
TN = (((0,), (0,)), ((), ()))
ERF_P = 0.4
ERF_C = (
    0.11596113048765463,
    0.08091125192311208,
    0.23413842084756234,
    -0.1854556415158047,
    0.35457470270248115,
    -0.10012987827403336,
)


def mm(a, b):
    return jnp.dot(a, b, preferred_element_type=WIDE)


def mm_nt(a, b):
    return lax.dot_general(a, b, NT, preferred_element_type=WIDE)


def mm_tn(a, b):
    return lax.dot_general(a, b, TN, preferred_element_type=WIDE)


def spot_of(k):
    return (k % 2) * 2 + k // 2


def select_piece(spot, refs, out):
    for n, ref in enumerate(refs):

        @pl.when(spot == n)
        def _(ref=ref):
            out[...] = ref[...]


def piece_specs(rows, features):
    return [pl.BlockSpec((rows, features), lambda *i: (0, 0))] * 4


def norm_parts(values):
    centred = values - jnp.mean(values, axis=-1, keepdims=True)
    rstd = lax.rsqrt(jnp.mean(centred * centred, axis=-1, keepdims=True) + EPS)
    return centred * rstd, rstd


def attend_kernel(
    meta_ref, start_ref, x_0_ref, x_1_ref, x_2_ref, x_3_ref, gain_ref, w_ref,
    h_ref, qt_ref, q_ref, k_ref, kt_ref, v_ref, ctx_ref, ctxt_ref, lse_ref, k_all, vt_all, x_ref,
):
    step = pl.program_id(0)
    heads = qt_ref.shape[0]
    width = heads * HD
    start = start_ref[...]
    key_iota = lax.broadcasted_iota(jnp.int32, (BLOCK, BLOCK), 0)
    query_iota = lax.broadcasted_iota(jnp.int32, (BLOCK, BLOCK), 1)

    select_piece(spot_of(step ^ meta_ref[0]), (x_0_ref, x_1_ref, x_2_ref, x_3_ref), x_ref)
    normed, _ = norm_parts(x_ref[...].astype(WIDE))
    h_one = (normed * gain_ref[...]).astype(LOW)
    h_ref[...] = h_one
    here = pl.ds(pl.multiple_of(step * BLOCK, BLOCK), BLOCK)
    q = mm(h_one, w_ref[:, :width]).astype(LOW) * (HD**-0.5)
    k = mm(h_one, w_ref[:, width : 2 * width]).astype(LOW)
    v = mm(h_one, w_ref[:, 2 * width : 3 * width]).astype(LOW)
    q = q.astype(LOW)
    q_t, k_t, v_t = q.T, k.T, v.T
    for h in range(heads):
        rows = slice(h * HD, (h + 1) * HD)
        qt_ref[h] = q_t[rows]
        q_ref[h] = q[:, rows]
        kt_ref[h] = k_t[rows]
        k_ref[h] = k[:, rows]
        k_all[h, here, :] = k[:, rows]
        v_ref[h] = v[:, rows]
        vt_all[h, :, here] = v_t[rows]

    def block(j, carry, last):
        base = pl.multiple_of(j * BLOCK, BLOCK)
        allowed = key_iota + base >= start
        if last:
            allowed = allowed & (key_iota <= query_iota)
        out = []
        for h in range(heads):
            top, total, acc = carry[h]
            scores = mm(k_all[h, pl.ds(base, BLOCK), :], qt_ref[h])
            scores = jnp.where(allowed, scores, MASKED)
            peak = jnp.maximum(top, jnp.max(scores, axis=0, keepdims=True))
            raised = jnp.exp(scores - peak)
            fade = jnp.exp(top - peak)
            total = total * fade + jnp.sum(raised, axis=0, keepdims=True)
            acc = acc * fade + mm(vt_all[h, :, pl.ds(base, BLOCK)], raised.astype(LOW))
            out.append((peak, total, acc))
        return tuple(out)

    carry = tuple(
        (
            jnp.full((1, BLOCK), MASKED, WIDE),
            jnp.zeros((1, BLOCK), WIDE),
            jnp.zeros((HD, BLOCK), WIDE),
        )
        for _ in range(heads)
    )
    carry = lax.fori_loop(meta_ref[1 + step], step, lambda j, c: block(j, c, False), carry)
    carry = block(step, carry, True)
    for h in range(heads):
        top, total, acc = carry[h]
        acc = acc / total
        ctxt_ref[h] = acc
        lse_ref[h] = top + jnp.log(total)
        ctx_ref[h * HD : (h + 1) * HD, :] = acc.astype(LOW)


def attend(meta, start, pieces, gain, weights, width):
    features = gain.shape[1]
    rows = 4 * BLOCK
    heads = width // HD
    spot = lambda i, m: spot_of(i ^ m[0])
    place = lambda i, m: (spot(i, m), 0)

    by_column = pl.BlockSpec((heads, HD, BLOCK), lambda i, m: (0, 0, i))
    by_row = pl.BlockSpec((heads, BLOCK, HD), lambda i, m: (0, i, 0))
    grid_spec = pltpu.PrefetchScalarGridSpec(
        num_scalar_prefetch=1,
        grid=(rows // BLOCK,),
        in_specs=[
            pl.BlockSpec((1, BLOCK), lambda i, m: (0, i)),
            *piece_specs(BLOCK, features),
            pl.BlockSpec((1, features), lambda i, m: (0, 0)),
            pl.BlockSpec(weights.shape, lambda i, m: (0, 0)),
        ],
        out_specs=[
            pl.BlockSpec((BLOCK, features), place),
            by_column,
            by_row,
            by_row,
            by_column,
            by_row,
            pl.BlockSpec((width, BLOCK), lambda i, m: (0, spot(i, m))),
            by_column,
            pl.BlockSpec((heads, 1, BLOCK), lambda i, m: (0, 0, i)),
        ],
        scratch_shapes=[
            pltpu.VMEM((heads, rows, HD), LOW),
            pltpu.VMEM((heads, HD, rows), LOW),
            pltpu.VMEM((BLOCK, features), LOW),
        ],
    )
    tall = jax.ShapeDtypeStruct((heads, rows, HD), LOW)
    flat = jax.ShapeDtypeStruct((heads, HD, rows), LOW)
    return pl.pallas_call(
        attend_kernel,
        grid_spec=grid_spec,
        out_shape=[
            jax.ShapeDtypeStruct((rows, features), LOW),
            flat,
            tall,
            tall,
            flat,
            tall,
            jax.ShapeDtypeStruct((width, rows), LOW),
            jax.ShapeDtypeStruct((heads, HD, rows), WIDE),
            jax.ShapeDtypeStruct((heads, 1, rows), WIDE),
        ],
        compiler_params=pltpu.CompilerParams(vmem_limit_bytes=50 * 2**20),
        cost_estimate=LITTLE,
    )(meta, start, *pieces, gain, weights)


def attend_back_kernel(
    meta_ref, start_ref, x_ref, dh_mine_ref, dh_near_ref, c_0_ref, c_1_ref, c_2_ref, c_3_ref,
    gain_ref, w_ref, qt_ref, q_ref, k_ref, kt_ref, v_ref, ctxt_ref, lse_ref, h_ref, ctx_ref,
    dx_ref, dgain_ref, send_own_ref, send_far_ref, own_ref, far_ref, keep_ref, give_ref, dots_ref,
    dk_acc, dv_acc, dh_ref, c_ref, dqkv, d_all, acc,
):
    step = pl.program_id(0)
    heads = qt_ref.shape[0]
    width = heads * HD

    @pl.when(step == 0)
    def _():
        dk_acc[...] = jnp.zeros_like(dk_acc)
        dv_acc[...] = jnp.zeros_like(dv_acc)
        acc[...] = jnp.zeros_like(acc)

    def place(piece):
        return pl.ds(pl.multiple_of(spot_of(piece ^ meta_ref[0]) * BLOCK, BLOCK), BLOCK)

    @pl.when(step < 4)
    def _():
        start = start_ref[...]
        key_iota = lax.broadcasted_iota(jnp.int32, (BLOCK, BLOCK), 0)
        query_iota = lax.broadcasted_iota(jnp.int32, (BLOCK, BLOCK), 1)
        spot = spot_of(step ^ meta_ref[0])
        select_piece(spot, (c_0_ref, c_1_ref, c_2_ref, c_3_ref), c_ref)

        @pl.when(spot < 2)
        def _():
            dh_ref[...] = dh_mine_ref[...]

        @pl.when(spot >= 2)
        def _():
            dh_ref[...] = dh_near_ref[...]

        normed, rstd = norm_parts(x_ref[...])
        dh = dh_ref[...].astype(WIDE)
        scaled = dh * gain_ref[...]
        mean_plain = jnp.mean(scaled, axis=-1, keepdims=True)
        mean_normed = jnp.mean(scaled * normed, axis=-1, keepdims=True)
        dx = c_ref[...].astype(WIDE) + rstd * (scaled - mean_plain - normed * mean_normed)
        dattn = dx.astype(LOW)
        d_all[place(step), :] = dattn

        @pl.when(step == meta_ref[0])
        def _():
            dx_ref[...] = dx
            dgain_ref[...] = jnp.sum(dh * normed, axis=0, keepdims=True)

        g_all = mm(dattn, w_ref[:, 3 * width :]).astype(LOW)
        gt_all = g_all.T
        g = [g_all[:, h * HD : (h + 1) * HD] for h in range(heads)]
        gt = [gt_all[h * HD : (h + 1) * HD] for h in range(heads)]
        delta = [
            jnp.sum(gt[h].astype(WIDE) * ctxt_ref[h], axis=0, keepdims=True)
            for h in range(heads)
        ]

        def block(j, carry, last):
            base = pl.multiple_of(j * BLOCK, BLOCK)
            rows = pl.ds(base, BLOCK)
            allowed = key_iota + base >= start
            if last:
                allowed = allowed & (key_iota <= query_iota)
            out = []
            for h in range(heads):
                scores = mm(k_ref[h, rows, :], qt_ref[h])
                probs = jnp.where(allowed, jnp.exp(scores - lse_ref[h]), 0.0)
                slopes = mm(v_ref[h, rows, :], gt[h])
                score_grads = (probs * (slopes - delta[h])).astype(LOW)
                dv_acc[h, rows, :] += mm(probs.astype(LOW), g[h])
                dk_acc[h, rows, :] += mm(score_grads, q_ref[h])
                out.append(carry[h] + mm(kt_ref[h, :, rows], score_grads))
            return tuple(out)

        carry = tuple(jnp.zeros((HD, BLOCK), WIDE) for _ in range(heads))
        carry = lax.fori_loop(meta_ref[1 + step], step, lambda j, c: block(j, c, False), carry)
        carry = block(step, carry, True)
        scale = HD**-0.5
        dqkv[place(step), :width] = jnp.concatenate(
            [(c * scale).T for c in carry], axis=1
        ).astype(LOW)

    @pl.when(step == 3)
    def _():
        for n in range(4):
            rows = slice(n * BLOCK, (n + 1) * BLOCK)
            dqkv[place(n), width:] = jnp.concatenate(
                [part[h, rows, :] for part in (dk_acc, dv_acc) for h in range(heads)], axis=1
            ).astype(LOW)

    def rest(out, kind):
        rows = pl.ds(pl.multiple_of(((step - 4) ^ 2) * BLOCK, BLOCK), BLOCK)
        grads = dqkv[rows, :]
        out[...] = mm_nt(grads, w_ref[:, : 3 * width]).astype(kind)
        acc[:, : 3 * width] += mm_tn(h_ref[...], grads)
        acc[:, 3 * width :] += mm_tn(d_all[rows, :], ctx_ref[...].T)

    for n, (out, kind) in enumerate(
        ((send_own_ref, LOW), (send_far_ref, LOW), (own_ref, WIDE), (far_ref, WIDE))
    ):

        @pl.when(step == 4 + n)
        def _(out=out, kind=kind):
            rest(out, kind)

    @pl.when(step == 7)
    def _():
        dots_ref[...] = jnp.sum(
            acc[:, : 3 * width] * w_ref[:, : 3 * width].astype(WIDE), axis=1, keepdims=True
        )
        count, size = 2 * keep_ref.shape[0], keep_ref.shape[1]
        for n in range(count):
            k = sum(((n >> b) & 1) * (count >> 1 >> b) for b in range(count.bit_length() - 1))
            part = acc[pl.ds(pl.multiple_of((meta_ref[5] ^ k) * size, 8), size), :]
            if n < count // 2:
                keep_ref[n] = part
            else:
                give_ref[n - count // 2] = part.astype(LOW)


def attend_back(
    meta, start, x_one, dh_pieces, c_pieces, gain, weights,
    qt, q, keys, kt, values, ctxt, lse, h_one, context, count,
):
    heads, _, rows = qt.shape
    features = x_one.shape[1]
    every = weights.shape[1]
    low = lambda i: jnp.minimum(i, 3)
    high = lambda i: jnp.maximum(i - 4, 0) ^ 2
    spot = lambda i, m: spot_of(low(i) ^ m[0])
    once = pl.Buffered(1)
    by_column = pl.BlockSpec((heads, HD, BLOCK), lambda i, m: (0, 0, low(i)))
    by_row = pl.BlockSpec((heads, BLOCK, HD), lambda i, m: (0, low(i), 0))

    def whole(*shape):
        return pl.BlockSpec(shape, lambda i, m: (0,) * len(shape), pipeline_mode=once)

    def out(*shape):
        return pl.BlockSpec(shape, lambda i, m: (0,) * len(shape))

    share = (count // 2, features // count, every)
    grid_spec = pltpu.PrefetchScalarGridSpec(
        num_scalar_prefetch=1,
        grid=(8,),
        in_specs=[
            pl.BlockSpec((1, BLOCK), lambda i, m: (0, low(i))),
            pl.BlockSpec((BLOCK, features), lambda i, m: (spot(i, m), 0)),
            pl.BlockSpec((BLOCK, features), lambda i, m: (jnp.minimum(spot(i, m), 1), 0)),
            pl.BlockSpec((BLOCK, features), lambda i, m: (jnp.maximum(spot(i, m) - 2, 0), 0)),
            *([whole(BLOCK, features)] * 4),
            whole(1, features),
            whole(*weights.shape),
            by_column,
            by_row,
            whole(heads, rows, HD),
            whole(heads, HD, rows),
            whole(heads, rows, HD),
            by_column,
            pl.BlockSpec((heads, 1, BLOCK), lambda i, m: (0, 0, low(i))),
            pl.BlockSpec((BLOCK, features), lambda i, m: (high(i), 0)),
            pl.BlockSpec((heads * HD, BLOCK), lambda i, m: (0, high(i))),
        ],
        out_specs=[
            out(BLOCK, features),
            out(1, features),
            *([out(BLOCK, features)] * 4),
            out(*share),
            out(*share),
            out(features, 1),
        ],
        scratch_shapes=[pltpu.VMEM((heads, rows, HD), WIDE)] * 2
        + [pltpu.VMEM((BLOCK, features), LOW)] * 2
        + [
            pltpu.VMEM((rows, 3 * heads * HD), LOW),
            pltpu.VMEM((rows, features), LOW),
            pltpu.VMEM((features, every), WIDE),
        ],
    )
    return pl.pallas_call(
        attend_back_kernel,
        grid_spec=grid_spec,
        out_shape=[
            jax.ShapeDtypeStruct((BLOCK, features), WIDE),
            jax.ShapeDtypeStruct((1, features), WIDE),
            *([jax.ShapeDtypeStruct((BLOCK, features), LOW)] * 2),
            *([jax.ShapeDtypeStruct((BLOCK, features), WIDE)] * 2),
            jax.ShapeDtypeStruct(share, WIDE),
            jax.ShapeDtypeStruct(share, LOW),
            jax.ShapeDtypeStruct((features, 1), WIDE),
        ],
        compiler_params=pltpu.CompilerParams(vmem_limit_bytes=61 * 2**20),
        cost_estimate=LITTLE,
    )(
        meta, start, x_one, *dh_pieces, *c_pieces, gain, weights,
        qt, q, keys, kt, values, ctxt, lse, h_one, context,
    )


def hot_rows(placed_ref, line, first, rows):
    spots = lax.broadcasted_iota(jnp.int32, (rows, placed_ref.shape[1]), 0) + first
    hot = (placed_ref[line : line + 1, :] == spots) | (placed_ref[line + 1 : line + 2, :] == spots)
    return jnp.where(hot, 1.0, 0.0).astype(LOW)


def send_kernel(
    index_ref, placed_ref, c_0_ref, c_1_ref, c_2_ref, c_3_ref, c_ref, in_order_ref, picks_ref, rows_all
):
    step = pl.program_id(0)
    share = in_order_ref.shape[0]
    size = c_0_ref.shape[0]

    @pl.when(step == 0)
    def _():
        for n, ref in enumerate((c_0_ref, c_1_ref, c_2_ref, c_3_ref)):
            rows_all[n * size : (n + 1) * size, :] = ref[...]

    hot = hot_rows(placed_ref, 2, step * share, share)
    in_order_ref[...] = hot
    picks_ref[...] = hot
    c_ref[0, :share, :] = mm(hot, rows_all[...]).astype(LOW)
    sums = mm_nt(placed_ref[...].astype(WIDE).astype(LOW), hot)[4:5]
    line = jnp.concatenate(
        [sums, jnp.zeros((1, c_ref.shape[2] - share), WIDE)], axis=1
    ) if c_ref.shape[2] > share else sums
    c_ref[0, share:, :] = jnp.broadcast_to(line, (16, c_ref.shape[2])).astype(LOW)


def send_rows(index, placed, pieces, count, share):
    size, features = pieces[0].shape
    total = 4 * size
    whole = lambda *shape: pl.BlockSpec(shape, lambda p, o: (0,) * len(shape))
    grid_spec = pltpu.PrefetchScalarGridSpec(
        num_scalar_prefetch=1,
        grid=(count,),
        in_specs=[
            whole(*placed.shape),
            *([whole(size, features)] * 4),
        ],
        out_specs=[
            pl.BlockSpec((1, share + 16, features), lambda p, o: (p, 0, 0)),
            pl.BlockSpec((share, total), lambda p, o: (p, 0)),
            pl.BlockSpec((share, total), lambda p, o: (p ^ o[0], 0)),
        ],
        scratch_shapes=[pltpu.VMEM((total, features), LOW)],
    )
    return pl.pallas_call(
        send_kernel,
        grid_spec=grid_spec,
        out_shape=[
            jax.ShapeDtypeStruct((count, share + 16, features), LOW),
            jax.ShapeDtypeStruct((count * share, total), LOW),
            jax.ShapeDtypeStruct((count * share, total), LOW),
        ],
        compiler_params=pltpu.CompilerParams(vmem_limit_bytes=40 * 2**20),
        cost_estimate=pl.CostEstimate(flops=4 * 10**10, bytes_accessed=10**7, transcendentals=0),
    )(index, placed, *pieces)


def halves_kernel(odd_ref, frozen_in_ref, frozen_out_ref, fresh_in_ref, fresh_out_ref, kept_ref, given_ref):
    units = frozen_out_ref.shape[1]

    def store(out, first, second):
        out[:units, :] = first[0].T.astype(LOW)
        out[units:, :] = second[0].astype(LOW)

    @pl.when(odd_ref[0] == 0)
    def _():
        store(kept_ref, frozen_in_ref, frozen_out_ref)
        store(given_ref, fresh_in_ref, fresh_out_ref)

    @pl.when(odd_ref[0] == 1)
    def _():
        store(kept_ref, fresh_in_ref, fresh_out_ref)
        store(given_ref, frozen_in_ref, frozen_out_ref)


def expert_halves(odd, frozen_in, frozen_out, fresh_in, fresh_out):
    _, features, units = frozen_in.shape
    grid_spec = pltpu.PrefetchScalarGridSpec(
        num_scalar_prefetch=1,
        grid=(1,),
        in_specs=[
            pl.BlockSpec(w.shape, lambda p, o: (0, 0, 0))
            for w in (frozen_in, frozen_out, fresh_in, fresh_out)
        ],
        out_specs=[pl.BlockSpec((2 * units, features), lambda p, o: (0, 0))] * 2,
    )
    return pl.pallas_call(
        halves_kernel,
        grid_spec=grid_spec,
        out_shape=[jax.ShapeDtypeStruct((2 * units, features), LOW)] * 2,
        compiler_params=pltpu.CompilerParams(vmem_limit_bytes=40 * 2**20),
        cost_estimate=LITTLE,
    )(odd, frozen_in, frozen_out, fresh_in, fresh_out)


def mix_kernel(count, gain_ref, placed_ref, *refs):
    context_refs, weight_refs, piece_refs = refs[:4], refs[4:8], refs[8:12]
    x_one_ref, taken_refs, x_ref, h_all = refs[12], refs[13 : 13 + count], refs[-2], refs[-1]
    step = pl.program_id(0)
    size = x_ref.shape[0]
    select_piece(step, piece_refs, x_ref)
    attn = mm_nt(context_refs[0][...].T, weight_refs[0][...])
    for n in range(1, 4):
        attn = attn + mm_nt(context_refs[n][...].T, weight_refs[n][...])
    x_one = x_ref[...].astype(WIDE) + attn
    x_one_ref[...] = x_one
    normed, _ = norm_parts(x_one)
    h_all[pl.ds(pl.multiple_of(step * size, size), size), :] = (normed * gain_ref[...]).astype(LOW)

    @pl.when(step == pl.num_programs(0) - 1)
    def _():
        share = taken_refs[0].shape[0]
        for k in range(count):
            hot = hot_rows(placed_ref, 0, k * share, share)
            taken_refs[k][...] = mm(hot, h_all[...]).astype(LOW)


def mix(placed, pieces, gain, contexts, weights, count, share):
    width, rows = contexts[0].shape
    features = gain.shape[1]
    size = rows // 4

    def context_spec(n):
        return pl.BlockSpec((width, size), lambda i: (0, i ^ n))

    return pl.pallas_call(
        functools.partial(mix_kernel, count),
        grid=(4,),
        in_specs=[
            pl.BlockSpec((1, features), lambda i: (0, 0)),
            pl.BlockSpec(placed.shape, lambda i: (0, 0)),
        ]
        + [context_spec(n) for n in range(4)]
        + [pl.BlockSpec((features, width), lambda i: (0, 0))] * 4
        + piece_specs(size, features),
        scratch_shapes=[pltpu.VMEM((size, features), LOW), pltpu.VMEM((rows, features), LOW)],
        out_specs=[pl.BlockSpec((size, features), lambda i: (i, 0))]
        + [pl.BlockSpec((share, features), lambda i: (0, 0))] * count,
        out_shape=[jax.ShapeDtypeStruct((rows, features), WIDE)]
        + [jax.ShapeDtypeStruct((share, features), LOW)] * count,
        compiler_params=pltpu.CompilerParams(vmem_limit_bytes=60 * 2**20),
        cost_estimate=LITTLE,
    )(gain, placed, *contexts, *weights, *pieces)


def expert_kernel(count, meta_ref, *refs):
    x_refs, refs = refs[:count], refs[count:]
    c_refs, refs = refs[:count], refs[count:]
    wg_ref, weight_refs = refs[0], refs[1:9]
    refs = refs[-(15 + count) :]
    a_ref, du_ref, xs_ref, dy_ref, mark_ref, y_ref = refs[:6]
    dx_refs, refs = refs[6 : 6 + count], refs[6 + count :]
    cs, w1_all, w2_all, sems, acc, acc_y, dots, others, gate = refs
    step, steps = pl.program_id(0), pl.num_programs(0)
    rows, kinds = xs_ref.shape[0], wg_ref.shape[0]
    share = rows // count
    units = w1_all.shape[1] // 2
    lanes = lax.broadcasted_iota(jnp.int32, (rows, kinds), 1)
    own = meta_ref[6]

    def fetches(n):
        slot = n % 2
        for m in range(2):
            span = slice(m * units, (m + 1) * units)
            for p, target in enumerate((w1_all, w2_all)):
                yield pltpu.make_async_copy(
                    weight_refs[2 * n + m].at[p * units : (p + 1) * units],
                    target.at[slot, span],
                    sems.at[slot, 2 * m + p],
                )

    def kinds_of():
        sums = [
            c_refs[n][0, share : share + 16, : -(-share // 128) * 128].astype(WIDE).T[:share, :1]
            for n in range(count)
        ]
        sums = jnp.concatenate(sums, axis=0).astype(jnp.int32)
        return lanes == own, lanes == sums - own

    @pl.when(step == 0)
    def _():
        for copy in fetches(0):
            copy.start()
        for n in range(count):
            xs_ref[n * share : (n + 1) * share, :] = x_refs[n][...]
            cs[n * share : (n + 1) * share, :] = c_refs[n][0, :share, :]
        logits = mm_nt(xs_ref[...], wg_ref[...].astype(LOW))
        here, there = kinds_of()
        mine = jnp.sum(jnp.where(here, logits, 0.0), axis=1, keepdims=True)
        theirs = jnp.sum(jnp.where(there, logits, 0.0), axis=1, keepdims=True)
        peak = jnp.maximum(mine, theirs)
        mine, theirs = jnp.exp(mine - peak), jnp.exp(theirs - peak)
        gate[...] = mine / (mine + theirs)
        others[...] = theirs / (mine + theirs)
        dy_ref[...] = (gate[...] * cs[...].astype(WIDE)).astype(LOW)
        acc[...] = jnp.zeros_like(acc)
        acc_y[...] = jnp.zeros_like(acc_y)
        dots[...] = jnp.zeros_like(dots)

    for n in range(4):

        @pl.when(step == n)
        def _(n=n):
            if n < 3:
                for copy in fetches(n + 1):
                    copy.start()
            for copy in fetches(n):
                copy.wait()

    w1, w2 = w1_all[step % 2], w2_all[step % 2]
    u = mm_nt(xs_ref[...], w1)
    da = mm_nt(cs[...], w2)
    bell = jnp.exp(u * u * -0.5)
    t = 1.0 / (1.0 + jnp.abs(u) * (ERF_P * ROOT_HALF))
    tail = ERF_C[-1] * t
    for coefficient in ERF_C[-2::-1]:
        tail = (tail + coefficient) * t
    tail = tail * bell
    part = jnp.where(u >= 0.0, 1.0 - tail, tail)
    a = (u * part).astype(LOW)
    slope = part + u * bell * INV_ROOT_TAU
    dots[...] += jnp.sum(a.astype(WIDE) * da, axis=1, keepdims=True)
    du = (gate[...] * da * slope).astype(LOW)
    a_ref[...] = a
    du_ref[...] = du
    acc_y[...] += mm(a, w2)
    acc[...] += mm(du, w1)

    @pl.when(step == steps - 1)
    def _():
        pull = gate[...] * others[...] * dots[...]
        here, there = kinds_of()
        marks = jnp.where(here, pull, 0.0) - jnp.where(there, pull, 0.0)
        mark_ref[...] = marks
        high = marks.astype(LOW)
        rest = (marks - high.astype(WIDE)).astype(LOW)
        gate_low = wg_ref[...].astype(LOW)
        dx = acc[...] + mm(high, gate_low) + mm(rest, gate_low)
        for n in range(count):
            dx_refs[n][...] = dx[n * share : (n + 1) * share].astype(LOW)
        y = (gate[...] * acc_y[...]).astype(LOW)
        for n in range(count):
            base = pl.multiple_of((meta_ref[5] % count ^ n) * share, 16)
            y_ref[pl.ds(base, share), :] = y[n * share : (n + 1) * share]


def run_experts(meta, xs, c, gate_weight, weights, chunk, chunks, held):
    count = len(xs)
    share, features = xs[0].shape
    rows = count * share
    units = weights[0].shape[0]
    kinds = gate_weight.shape[0]
    whole = lambda *shape: pl.BlockSpec(shape, lambda p, o: (0,) * len(shape))
    by_piece = pl.BlockSpec((rows, units), lambda p, o: (chunk, p))
    by_chunk = lambda width: pl.BlockSpec((rows, width), lambda p, o: (chunk, 0))
    anywhere = pl.BlockSpec(memory_space=pl.ANY)

    def c_spec(n):
        return pl.BlockSpec((1,) + c.shape[1:], lambda p, o: (o[5] ^ (chunk * count + n), 0, 0))

    operands = [meta, *xs, *([c] * count), gate_weight, *weights]
    in_specs = (
        [whole(share, features)] * count
        + [c_spec(n) for n in range(count)]
        + [whole(kinds, features)]
        + [anywhere] * 8
    )
    aliases = {}
    if held is not None:
        aliases = {len(operands) + n: n for n in range(6)}
        operands += held
        in_specs += [anywhere] * 6
    every = chunks * rows
    grid_spec = pltpu.PrefetchScalarGridSpec(
        num_scalar_prefetch=1,
        grid=(4,),
        in_specs=in_specs,
        out_specs=[
            by_piece,
            by_piece,
            by_chunk(features),
            by_chunk(features),
            by_chunk(kinds),
            pl.BlockSpec((rows, features), lambda p, o: (o[5] // count ^ chunk, 0)),
            *([whole(share, features)] * count),
        ],
        scratch_shapes=[
            pltpu.VMEM((rows, features), LOW),
            pltpu.VMEM((2, units, features), LOW),
            pltpu.VMEM((2, units, features), LOW),
            pltpu.SemaphoreType.DMA((2, 4)),
            pltpu.VMEM((rows, features), WIDE),
            pltpu.VMEM((rows, features), WIDE),
            pltpu.VMEM((rows, 1), WIDE),
            pltpu.VMEM((rows, 1), WIDE),
            pltpu.VMEM((rows, 1), WIDE),
        ],
    )
    out = pl.pallas_call(
        functools.partial(expert_kernel, count),
        grid_spec=grid_spec,
        out_shape=[
            jax.ShapeDtypeStruct((every, 4 * units), LOW),
            jax.ShapeDtypeStruct((every, 4 * units), LOW),
            jax.ShapeDtypeStruct((every, features), LOW),
            jax.ShapeDtypeStruct((every, features), LOW),
            jax.ShapeDtypeStruct((every, kinds), WIDE),
            jax.ShapeDtypeStruct((every, features), LOW),
            *([jax.ShapeDtypeStruct((share, features), LOW)] * count),
        ],
        input_output_aliases=aliases,
        compiler_params=pltpu.CompilerParams(vmem_limit_bytes=58 * 2**20),
        cost_estimate=LITTLE,
    )(*operands)
    return out[:6], out[6:]


def expert_grads_kernel(a_ref, du_ref, x_ref, dy_ref, marks_ref, *refs):
    give_refs, (keep_ref, gate_ref) = refs[:4], refs[4:]
    step = pl.program_id(0)

    @pl.when(step == 0)
    def _():
        high = marks_ref[...].astype(LOW)
        rest = (marks_ref[...] - high.astype(WIDE)).astype(LOW)
        gate_ref[...] = mm_tn(x_ref[...], high) + mm_tn(x_ref[...], rest)

    units = a_ref.shape[1] // 2

    def store(outs, kind):
        first = mm_tn(du_ref[...], x_ref[...])
        second = mm_tn(a_ref[...], dy_ref[...])
        for m, out in enumerate(outs):
            span = slice(m * units, (m + 1) * units)
            out[:units, :] = first[span].astype(kind)
            out[units:, :] = second[span].astype(kind)

    for n in range(2):

        @pl.when(step == n)
        def _(n=n):
            store(give_refs[2 * n : 2 * n + 2], LOW)

    @pl.when(step >= 2)
    def _():
        store((keep_ref.at[0, 0], keep_ref.at[0, 1]), WIDE)


def expert_grads(hidden, hidden_grads, x, dy, marks):
    rows, features = x.shape
    units = hidden.shape[1] // 4
    piece = pl.BlockSpec((rows, units), lambda p: (0, p ^ 2))
    all_rows = pl.BlockSpec((rows, features), lambda p: (0, 0))
    shape = (2, 2, units, features)
    return pl.pallas_call(
        expert_grads_kernel,
        grid=(4,),
        in_specs=[piece, piece, all_rows, all_rows, pl.BlockSpec(marks.shape, lambda p: (0, 0))],
        out_specs=[
            *([pl.BlockSpec(shape[2:], lambda p: (0, 0))] * 4),
            pl.BlockSpec((1,) + shape[1:], lambda p: (jnp.maximum(p - 2, 0), 0, 0, 0)),
            pl.BlockSpec((features, marks.shape[1]), lambda p: (0, 0)),
        ],
        out_shape=[
            *([jax.ShapeDtypeStruct(shape[2:], LOW)] * 4),
            jax.ShapeDtypeStruct(shape, WIDE),
            jax.ShapeDtypeStruct((features, marks.shape[1]), WIDE),
        ],
        compiler_params=pltpu.CompilerParams(vmem_limit_bytes=58 * 2**20),
        cost_estimate=LITTLE,
    )(hidden, hidden_grads, x, dy, marks)


def leave_kernel(keep_ref, give_0_ref, give_1_ref, out_ref):
    for n, give_ref in enumerate((give_0_ref, give_1_ref)):

        @pl.when(pl.program_id(0) == n)
        def _(give_ref=give_ref):
            out_ref[0] = (keep_ref[0, 0] + give_ref[...].astype(WIDE)).astype(LOW)


def far_sum(keep, give):
    _, halves, rows, features = keep.shape
    whole = pl.BlockSpec((rows, features), lambda m: (0, 0))
    return pl.pallas_call(
        leave_kernel,
        grid=(halves,),
        in_specs=[pl.BlockSpec((1, 1, rows, features), lambda m: (1, m, 0, 0)), whole, whole],
        out_specs=pl.BlockSpec((1, rows, features), lambda m: (m, 0, 0)),
        out_shape=jax.ShapeDtypeStruct((halves, rows, features), LOW),
        compiler_params=pltpu.CompilerParams(vmem_limit_bytes=60 * 2**20),
        cost_estimate=LITTLE,
    )(keep, *give)


def home_kernel(keep_ref, give_0_ref, give_1_ref, far_ref, kept_ref, *other_refs):
    held = keep_ref[0, 0] + far_ref[0].astype(WIDE)

    @pl.when(pl.program_id(0) == 0)
    def _():
        other = (held + give_1_ref[...].astype(WIDE)).astype(LOW)
        for n, out in enumerate(other_refs):
            out[...] = other[n * out.shape[0] : (n + 1) * out.shape[0]]

    @pl.when(pl.program_id(0) == 1)
    def _():
        kept_ref[...] = held + give_0_ref[...].astype(WIDE)


def home_sum(keep, give, far):
    _, halves, rows, features = keep.shape
    whole = pl.BlockSpec((rows, features), lambda m: (0, 0))
    return pl.pallas_call(
        home_kernel,
        grid=(halves,),
        in_specs=[
            pl.BlockSpec((1, 1, rows, features), lambda m: (0, 1 - m, 0, 0)),
            whole,
            whole,
            pl.BlockSpec((1, rows, features), lambda m: (1 - m, 0, 0)),
        ],
        out_specs=[whole] + [pl.BlockSpec((rows // 2, features), lambda m: (0, 0))] * 2,
        out_shape=[jax.ShapeDtypeStruct((rows, features), WIDE)]
        + [jax.ShapeDtypeStruct((rows // 2, features), LOW)] * 2,
        compiler_params=pltpu.CompilerParams(vmem_limit_bytes=40 * 2**20),
        cost_estimate=LITTLE,
    )(keep, *give, far)


def choose_kernel(odd_ref, kept_ref, other_0_ref, other_1_ref, first_ref, second_ref):
    units = second_ref.shape[1]

    @pl.when(odd_ref[0] == 1)
    def _():
        first_ref[0] = kept_ref[:units, :].T
        second_ref[0] = kept_ref[units:, :]

    @pl.when(odd_ref[0] == 0)
    def _():
        first_ref[0] = other_0_ref[...].astype(WIDE).T
        second_ref[0] = other_1_ref[...].astype(WIDE)


def choose(odd, kept, other):
    rows, features = kept.shape
    units = rows // 2
    whole = lambda *shape: pl.BlockSpec(shape, lambda i, o: (0,) * len(shape))
    grid_spec = pltpu.PrefetchScalarGridSpec(
        num_scalar_prefetch=1,
        grid=(1,),
        in_specs=[whole(rows, features)] + [whole(units, features)] * 2,
        out_specs=[whole(1, features, units), whole(1, units, features)],
    )
    return pl.pallas_call(
        choose_kernel,
        grid_spec=grid_spec,
        out_shape=[
            jax.ShapeDtypeStruct((1, features, units), WIDE),
            jax.ShapeDtypeStruct((1, units, features), WIDE),
        ],
        compiler_params=pltpu.CompilerParams(vmem_limit_bytes=40 * 2**20),
        cost_estimate=LITTLE,
    )(odd, kept, *other)


def tokens_kernel(hot_ref, rows_ref, *out_refs):
    total = mm_tn(hot_ref[...], rows_ref[...])
    for n, out in enumerate(out_refs):

        @pl.when(pl.program_id(0) == n)
        def _(out=out):
            out[...] = total.astype(out.dtype)


def to_tokens(hot, rows):
    count, features = rows.shape
    return pl.pallas_call(
        tokens_kernel,
        grid=(4,),
        in_specs=[
            pl.BlockSpec((count, BLOCK), lambda i: (0, i ^ 2)),
            pl.BlockSpec((count, features), lambda i: (0, 0)),
        ],
        out_specs=[pl.BlockSpec((BLOCK, features), lambda i: (0, 0))] * 4,
        out_shape=[jax.ShapeDtypeStruct((BLOCK, features), LOW)] * 2
        + [jax.ShapeDtypeStruct((BLOCK, features), WIDE)] * 2,
        compiler_params=pltpu.CompilerParams(vmem_limit_bytes=60 * 2**20),
        cost_estimate=LITTLE,
    )(hot, rows)


def finish_kernel(keep_ref, near_ref, far_ref, x_ref, gain_ref, dx_ref, out_ref):
    dh = keep_ref[...] + near_ref[...].astype(WIDE) + far_ref[...].astype(WIDE)
    normed, rstd = norm_parts(x_ref[...].astype(WIDE))
    scaled = dh * gain_ref[...]
    mean_plain = jnp.mean(scaled, axis=-1, keepdims=True)
    mean_normed = jnp.mean(scaled * normed, axis=-1, keepdims=True)
    out_ref[...] = dx_ref[...] + rstd * (scaled - mean_plain - normed * mean_normed)


def finish(keep, near, far, x, gain, dx):
    rows, features = x.shape
    size = 256
    by_row = pl.BlockSpec((size, features), lambda i: (i, 0))
    return pl.pallas_call(
        finish_kernel,
        grid=(rows // size,),
        in_specs=[by_row] * 4 + [pl.BlockSpec((1, features), lambda i: (0, 0)), by_row],
        out_specs=by_row,
        out_shape=jax.ShapeDtypeStruct((rows, features), WIDE),
        cost_estimate=LITTLE,
    )(keep, near, far, x, gain, dx)


def flip(array, axis, bits):
    size = lax.axis_size(axis)
    return lax.ppermute(array, axis, [(i, i ^ bits) for i in range(size)])


def flip_head_where(array, bits, odd):
    heads, rest = lax.axis_size("head"), lax.axis_size("dp")
    pairs = [
        (d * heads + h, d * heads + (h ^ bits)) for d in range(odd, rest, 2) for h in range(heads)
    ]
    return lax.ppermute(array, ("dp", "head"), pairs)


def after(value, *others):
    return lax.optimization_barrier((value, *others))[0]


def joined(pieces):
    return jnp.concatenate(pieces, axis=0)


def body(
    block_input,
    gain_one,
    gain_two,
    qkv_weight,
    out_weight,
    gate_weight,
    frozen_in,
    frozen_out,
    fresh_in,
    fresh_out,
    routes,
    doc_lengths,
    cotangent,
):
    own_rows, features = block_input.shape
    head_count, dp_count = lax.axis_size("head"), lax.axis_size("dp")
    head_index, dp_index = lax.axis_index("head"), lax.axis_index("dp")
    total = own_rows * head_count
    half = total // 2
    kinds = gate_weight.shape[1]
    share = 3 * total // kinds // head_count
    width = qkv_weight.shape[2]
    odd = dp_index % 2
    gain_one, gain_two = gain_one[None], gain_two[None]

    c_far = flip(cotangent, "head", 2)
    c_near, x_near = flip(cotangent, "head", 1), flip(block_input, "head", 1)
    x_far = flip(after(block_input, c_far), "head", 2)

    piece = jnp.concatenate(
        [qkv_weight[0], qkv_weight[1], qkv_weight[2], out_weight.T], axis=1
    ).astype(LOW)
    weights = lax.all_to_all(
        jnp.broadcast_to(piece[None], (dp_count,) + piece.shape), "dp", 0, 0, tiled=True
    ).reshape(features, 4 * width)

    tokens = jnp.arange(total, dtype=jnp.int32)
    hits = (routes[:, :, None] == jnp.arange(kinds, dtype=jnp.int32)).astype(LOW)
    earlier = (tokens[:, None] > tokens[None, :]).astype(LOW)
    counts = mm(earlier, hits.reshape(total, 2 * kinds)).reshape(total, 2, kinds)
    firsts = jnp.sum(hits[:, 0].astype(WIDE), axis=0)
    counts = counts + jnp.stack([jnp.zeros_like(firsts), firsts])[None]
    slots = jnp.sum(counts * hits.astype(WIDE), axis=2).astype(jnp.int32)
    hosts = routes % (kinds // 2) * 2 + routes // (kinds // 2)
    held_here = slots % head_count == head_index
    near_places = jnp.where(held_here, (hosts ^ dp_index) * share + slots // head_count, -1)
    places = jnp.where(held_here, hosts * share + slots // head_count, -1)
    placed = jnp.concatenate([near_places, places, jnp.sum(routes, axis=1, keepdims=True)], axis=1)
    placed = placed.reshape(head_count, own_rows, 5)
    placed = joined(
        [
            lax.dynamic_index_in_dim(placed, head_index ^ k, 0, keepdims=False)
            for k in (0, 2, 1, 3)
        ]
    ).T
    placed = jnp.pad(placed, ((0, 3), (0, 0)))
    here_dp = dp_index.astype(jnp.int32)[None]

    ends = jnp.cumsum(doc_lengths[0])
    start = jnp.max(jnp.where(tokens[:, None] >= ends[None], ends[None], 0), axis=1)
    own_kind = dp_index // 2 + odd * (kinds // 2)
    meta = jnp.concatenate(
        [head_index[None], start[::BLOCK] // BLOCK, dp_index[None], own_kind[None]]
    ).astype(jnp.int32)
    start = start[None]

    kept, given = expert_halves(
        after(odd.astype(jnp.int32)[None], c_far), frozen_in, frozen_out, fresh_in, fresh_out
    )

    come = flip(given, "dp", 1)

    c_pieces = [cotangent, c_far, c_near, flip(after(c_far, kept), "head", 1)]
    c_out, in_order, picks = send_rows(after(here_dp, meta, start), placed, c_pieces, dp_count, share)
    x_far = after(x_far, c_out)
    x_pieces = [block_input, x_far, x_near, flip(x_far, "head", 1)]

    kept_far = flip(after(kept, x_far), "head", 2)

    near_kept = flip(kept, "head", 1)
    out = weights[:, 3 * width :]
    out_far, out_near = flip(out, "head", 2), flip(out, "head", 1)
    out_last = flip(out_far, "head", 1)

    h_one, qt, queries, keys, kt, values, context, context_t, log_totals = attend(
        meta, start, x_pieces, gain_one, weights, width
    )
    near_context = flip(context, "head", 1)
    far_context = flip(after(context, kept_far, near_kept, out_far), "head", 2)
    c_in = lax.all_to_all(c_out, "dp", 0, 0, tiled=True)
    last_context = flip(after(far_context, come, out_near, out_last), "head", 1)
    come_far = flip(after(come, far_context), "head", 2)
    last_kept = flip(kept_far, "head", 1)
    per = dp_count // 4
    x_one, *x_out = mix(
        placed, x_pieces, after(gain_two, last_kept),
        [context, far_context, near_context, last_context], [out, out_far, out_near, out_last],
        dp_count, share,
    )
    near_come, last_come = (flip(after(w, x_one), "head", 1) for w in (come, come_far))
    halves = [kept, come, kept_far, come_far, near_kept, near_come, last_kept, last_come]

    groups = [range(n * per, (n + 1) * per) for n in range(4)]
    x_parts = {k: flip(x_out[k], "dp", k) if k else x_out[0] for k in range(2 * per)}
    x_parts.update({k: flip(after(x_out[k], x_parts[1]), "dp", k) for k in groups[2]})
    held, dx_parts = None, {}
    for n, ks in enumerate(groups):
        xs = [x_parts[k] for k in ks]
        if n == 3:
            xs[0] = after(xs[0], *[dx_parts[k] for k in (*groups[0], *groups[1])])
        held, dx = run_experts(meta, xs, c_in, gate_weight.T, halves, n, 4, held)
        if n == 2:
            back = flip(joined(dx), "dp", n * per)
            for r, k in enumerate(ks):
                part = back[r * share : (r + 1) * share]
                dx_parts[k] = flip(part, "dp", r) if r else part
        else:
            dx_parts.update({k: part if k == 0 else flip(part, "dp", k) for k, part in zip(ks, dx)})
        if n == 0:
            x_parts.update({k: flip(after(x_out[k], dx[0]), "dp", k) for k in groups[3]})

    cut = 2 * per * share
    early = joined([dx_parts[k] for k in range(2 * per)])
    there = mm_tn(picks[:cut, half:], early)
    here = mm_tn(picks[:cut, :half], early)
    late = [dx_parts[k] for k in (*groups[2], *groups[3])]
    late = joined([after(late[0], there, here), *late[1:]])
    there = (there + mm_tn(picks[cut:, half:], late)).astype(LOW)
    sent = flip(there, "head", 1)
    here = (here + mm_tn(picks[cut:, :half], late) + sent.astype(WIDE)).astype(LOW)
    across = flip(here, "head", 2)

    hidden, hidden_grads, x_all, dy_all, marks, gated = held
    *give, keep, grad_gate = expert_grads(hidden, hidden_grads, after(x_all, here), dy_all, marks)
    give = [flip(part, "head", 1) for part in give]
    leave = far_sum(keep, give[2:])
    gated = lax.all_to_all(
        after(gated, keep).reshape(dp_count, share, features), "dp", 0, 0, tiled=True
    ).reshape(dp_count * share, features)
    dh_mine = (
        here.astype(WIDE) + joined([across[own_rows:], across[:own_rows]]).astype(WIDE)
    ).astype(LOW)
    dh_near = flip(dh_mine, "head", 1)
    crossed = flip_head_where(after(leave, dh_mine), 2, 1)
    keep_home, give_home = keep, give[:2]

    dx_one, grad_gain_two, send_own, send_far, own, far, keep, give, dots = attend_back(
        meta, start, x_one, [dh_mine, dh_near], c_pieces, gain_two, weights,
        qt, queries, keys, kt, values, context_t, log_totals, h_one, context, dp_count,
    )
    send_far = flip(after(send_far, crossed), "head", 1)
    send_own = flip(send_own, "head", 1)
    far_out = (far + send_far.astype(WIDE)).astype(LOW)
    far = flip(far_out, "head", 2)
    grad_input = finish(own, send_own, far, block_input, gain_one, dx_one)

    y_send_own, y_send_far, y_own, y_far = to_tokens(in_order, after(gated, give))
    tokens_done = y_own
    y_send_far = flip(y_send_far, "head", 1)
    y_send_own = flip(y_send_own, "head", 1)
    y_out = (y_far + y_send_far.astype(WIDE)).astype(LOW)
    y_far = flip(y_out, "head", 2)
    mixture = y_own + y_send_own.astype(WIDE) + y_far.astype(WIDE)
    result = (x_one[:own_rows] + mixture).astype(LOW)

    dots = after(dots, send_far)
    small = joined([dots[:, 0][None] / gain_one, grad_gain_two, grad_gate.T])
    for bits in (1, 2):
        small = small + flip(small, "head", bits)
    keep = keep + after(flip(give, "dp", 1), far_out, small, tokens_done).astype(WIDE)
    kept_home, *other = home_sum(keep_home, give_home, after(crossed, keep))
    over = [flip(part, "dp", 1) for part in other]
    bits, small = 2, after(small, over[0])
    while bits < dp_count:
        count = keep.shape[0]
        come = flip(keep[count // 2 :].astype(LOW), "dp", bits)
        small = small + flip(small, "dp", bits)
        if bits == 2:
            come = after(come, *other)
        if count == 2:
            small = after(small, y_out)
            small = small + flip(small, "dp", 1)
            come = after(come, y_far, small, grad_input)
        keep = keep[: count // 2] + come.astype(WIDE)
        bits *= 2
    grads = keep[0]
    grad_qkv = jnp.stack([grads[:, n * width : (n + 1) * width] for n in range(3)])
    grad_out_weight = grads[:, 3 * width :].T
    grad_fresh_in, grad_fresh_out = choose(odd.astype(jnp.int32)[None], kept_home, over)
    return (
        result,
        grad_input,
        small[0],
        small[1],
        grad_qkv,
        grad_out_weight,
        small[2:].T,
        grad_fresh_in,
        grad_fresh_out,
    )


def solution(mesh):
    return jax.shard_map(
        body,
        mesh=mesh,
        in_specs=(
            P(("dp", "head"), None),
            P(),
            P(),
            P(None, "dp", "head"),
            P("head", "dp"),
            P(),
            P("dp", None, "head"),
            P("dp", "head", None),
            P("dp", None, "head"),
            P("dp", "head", None),
            P("dp", None),
            P("dp", None),
            P(("dp", "head"), None),
        ),
        out_specs=(
            P(("dp", "head"), None),
            P(("dp", "head"), None),
            P(),
            P(),
            P(None, "dp", "head"),
            P("head", "dp"),
            P(),
            P("dp", None, "head"),
            P("dp", "head", None),
        ),
        check_vma=False,
    )
```
